256 devices in a mesh: grp: 4 (over y), gy: 8 (over z), gx: 8 (over x, core).
Axes of the slice: x: 4, y: 4, z: 8, core: 2. Of those that a mesh axis runs over, the one named last changes fastest.
Arguments:
- soil_water: float32 [16, 6291456], P(None, ('grp', 'gy', 'gx'))
- conduct: bfloat16 [16, 6291456], P(None, ('grp', 'gy', 'gx')), may hold values from 0.099609375 to 3
- rainfall: float32 [6291456], P(('grp', 'gy', 'gx')), may hold values from 0.1 to 1
- infil_cap: float32 [6291456], P(('grp', 'gy', 'gx')), may hold values from 0.05 to 0.45
- live_counts: int32 [256], P(('grp', 'gy', 'gx')), may hold values from 6144 to 24576, as said below
- send_slot: int32 [256, 192], P(('grp', 'gy', 'gx')), may hold values from 0 to 511, as said below
- recv_row: int32 [256, 512], P(('grp', 'gy', 'gx')), may hold values from -1 to 1023, as said below
- bed_height: float32 [8192, 4096], P(('grp', 'gy'), 'gx'), may hold values from -3 to 3
- manning: float32 [8192, 4096], P(('grp', 'gy'), 'gx'), may hold values from 0.03 to 0.3
- depth_in: float32 [8192, 4096], P(('grp', 'gy'), 'gx'), may hold values from 0.5 to 3
- east_in: float32 [8192, 4096], P(('grp', 'gy'), 'gx'), may hold values from -3 to 3
- south_in: float32 [8192, 4096], P(('grp', 'gy'), 'gx'), may hold values from -3 to 3
- wet_mask: int32 [8192, 4096], P(('grp', 'gy'), 'gx'), may hold values 0 or 1
Outputs:
- soil_out: float32 [16, 6291456], P(None, ('grp', 'gy', 'gx'))
- depth_out: float32 [8192, 4096], P(('grp', 'gy'), 'gx')
- east_out: float32 [8192, 4096], P(('grp', 'gy'), 'gx')
- south_out: float32 [8192, 4096], P(('grp', 'gy'), 'gx')
- edge_we: float32 [16, 8192], P('gx', ('grp', 'gy'))
- edge_ns: float32 [64, 4096], P(('grp', 'gy'), 'gx')
The draws below stay inside these ranges and needn't reach their ends.
Inputs may be any that keep to these rules, and one draw needn't show every extreme that they name: `live_counts`: 24576 on at least one parcel. `send_slot`: on each parcel the 192 blocks name distinct slots; slot t * 2 + k is slot k towards tile t. Every parcel fills all 2 slots towards one common tile. `recv_row`: entry s * 2 + k of tile t is -1 exactly where parcel s fills no slot k towards t, else the tile row that this slot adds into.
All inputs are finite; a program needn't handle non-finite values. No bound on the sum of `wet_mask` on one device may be relied on, other than what follows from the above.
Results may differ from the reference program's by a relative error of at most 0.0003.
Values sent between devices are 32-bit elements; how exact they have to be, the bound alone decides.
No kernel may reach another device: no remote copies, remote signals or barrier semaphores. Data moves between devices by JAX's collectives and lax.ppermute only.
A program may use at most 128 MiB of HBM per device.

```python
import math
import jax
import jax.numpy as jnp

NL = 16
STEPS = 8
LAND_DEV = 24576
TILE_R = 256
TILE_C = 512
NB = 192
CAP = 2
LAND_CELLS = 6291456
NROWS = 8192
NCOLS = 4096
TROWS = 1024
N_GRP = 4
N_GY = 8
N_GX = 8
DEVICES = 256


def slot_tables(key):
    key = jax.random.fold_in(key, 101)
    key_hot, key_score, key_shuffle, key_rows = jax.random.split(key, 4)
    slot_count = DEVICES * CAP
    blocks = LAND_DEV // 128
    favored = jax.random.randint(key_hot, (), 0, DEVICES)
    index_row = jnp.arange(slot_count, dtype=jnp.int32)
    scores = jax.random.randint(key_score, (DEVICES, slot_count), 0, slot_count) * slot_count + index_row[None, :]
    scores = jnp.where((index_row // CAP == favored)[None, :], index_row[None, :] - slot_count, scores)
    chosen = jnp.argsort(scores, axis=1, stable=True)[:, :blocks].astype(jnp.int32)
    shuffle = jax.random.randint(key_shuffle, (DEVICES, blocks), 0, blocks) * blocks + jnp.arange(blocks, dtype=jnp.int32)[None, :]
    order_idx = jnp.argsort(shuffle, axis=1, stable=True)
    send_table = jnp.take_along_axis(chosen, order_idx, axis=1).astype(jnp.int32)
    source_idx = jnp.arange(DEVICES, dtype=jnp.int32)[:, None]
    filled = jnp.zeros((DEVICES, slot_count), jnp.int32).at[source_idx, chosen].set(1)
    filled = filled.reshape(DEVICES, DEVICES, CAP).transpose(1, 0, 2).reshape(DEVICES, slot_count)
    landing = jax.random.randint(key_rows, (DEVICES, slot_count), 0, TROWS)
    landing = landing.at[favored, 0].set(TROWS - 1)
    recv_table = jnp.where(filled > 0, landing, -1).astype(jnp.int32)
    return (send_table, recv_table)


def draw_send_slot(key, part):
    return slot_tables(key)[0]


def draw_recv_row(key, part):
    return slot_tables(key)[1]


def draw_live_counts(key, part):
    key = jax.random.fold_in(key, 23)
    key_count, key_full = jax.random.split(key)
    counts = jax.random.randint(key_count, (DEVICES,), LAND_DEV // 4, LAND_DEV + 1)
    fullest = jax.random.randint(key_full, (), 0, DEVICES)
    return counts.at[fullest].set(LAND_DEV).astype(jnp.int32)


def draw_soil_water(key, part):
    key = jax.random.fold_in(key, 37)
    key_cells, key_parcel = jax.random.split(key)
    spread = jax.random.uniform(key_cells, (NL, LAND_CELLS), jnp.float32)
    parcel_level = jax.random.uniform(key_parcel, (DEVICES,), jnp.float32)
    device_pos = jnp.arange(DEVICES, dtype=jnp.int32).astype(jnp.float32) / max(DEVICES - 1, 1)
    parcel_base = 0.1 + 0.2 * device_pos + 0.15 * parcel_level
    base_level = jnp.repeat(parcel_base, LAND_DEV)[None, :]
    return (base_level + 0.15 * spread).astype(jnp.float32)


def touch_ends(values, stream_key, least, largest):
    longest = values.shape.index(max(values.shape))
    spots = []
    for shift in (0, 1):
        where = [jax.random.randint(jax.random.fold_in(stream_key, axis), (), 0, length) for axis, length in enumerate(values.shape)]
        where[longest] = (where[longest] + shift) % values.shape[longest]
        spots.append(tuple(where))
    return values.at[spots[0]].set(least).at[spots[1]].set(largest)


def steps_of(own_key, shape, cuts, low, largest):
    gain = 1.0
    for dim, shards_of in cuts:
        heights = jax.random.uniform(jax.random.fold_in(jax.random.fold_in(own_key, 6), dim), (shards_of,), jnp.float32, low / len(cuts), largest / len(cuts))
        gain = gain * jnp.repeat(jnp.exp(heights), shape[dim] // shards_of).reshape((-1,) + (1,) * (len(shape) - 1 - dim))
    return gain


def scatter_about(stream_key, extent, scale, limit, cuts=(), held_as=jnp.bfloat16):
    entries = jax.random.normal(stream_key, extent, jnp.float32) * scale
    if len(cuts) > 0:
        entries = steps_of(stream_key, extent, cuts, -0.22, 0.18) * entries
    return jnp.clip(entries, min=-limit, max=limit).astype(held_as)


def setup_inputs(seed: int = 0) -> dict:
    key_list = jax.random.split(jax.random.key(seed), 14)
    return {
        "soil_water": draw_soil_water(jax.random.fold_in(key_list[13], 71), 0),
        "conduct": jnp.clip(jnp.exp(math.log(3.0) - 3.4051113 * jax.random.uniform(key_list[1], (NL, LAND_CELLS), jnp.float32) ** steps_of(key_list[1], (NL, LAND_CELLS), ((1, 256),), -0.2, 0.2)), 0.099609375, 3.0).astype(jnp.bfloat16),
        "rainfall": jnp.clip(jnp.exp(math.log(1.0) - 2.3025851 * jax.random.uniform(key_list[2], (LAND_CELLS,), jnp.float32) ** steps_of(key_list[2], (LAND_CELLS,), ((0, 256),), -0.2, 0.2)), 0.1, 1.0),
        "infil_cap": jnp.clip(jnp.exp(math.log(0.45) - 2.1972245 * jax.random.uniform(key_list[3], (LAND_CELLS,), jnp.float32) ** steps_of(key_list[3], (LAND_CELLS,), ((0, 256),), -0.2, 0.2)), 0.05, 0.45),
        "live_counts": draw_live_counts(jax.random.fold_in(key_list[13], 71), 0),
        "send_slot": draw_send_slot(jax.random.fold_in(key_list[13], 71), 0),
        "recv_row": draw_recv_row(jax.random.fold_in(key_list[13], 71), 0),
        "bed_height": scatter_about(key_list[7], (NROWS, NCOLS), 0.5, 3.0, ((0, 32), (1, 8)), jnp.float32),
        "manning": jnp.clip(jnp.exp(math.log(0.3) - 2.3025852 * jax.random.uniform(key_list[8], (NROWS, NCOLS), jnp.float32) ** steps_of(key_list[8], (NROWS, NCOLS), ((0, 32), (1, 8)), -0.2, 0.2)), 0.03, 0.3),
        "depth_in": jnp.clip(0.5 + 2.5 * jax.random.uniform(key_list[9], (NROWS, NCOLS), jnp.float32) ** steps_of(key_list[9], (NROWS, NCOLS), ((0, 32), (1, 8)), -0.2, 0.2), 0.5, 3.0),
        "east_in": scatter_about(key_list[10], (NROWS, NCOLS), 0.5, 3.0, ((0, 32), (1, 8)), jnp.float32),
        "south_in": scatter_about(key_list[11], (NROWS, NCOLS), 0.5, 3.0, ((0, 32), (1, 8)), jnp.float32),
        "wet_mask": touch_ends((jax.random.randint(key_list[12], (NROWS, NCOLS), 0, 4) < 3).astype(jnp.int32), jax.random.fold_in(key_list[12], 1), 0, 1),
    }


gravity = 9.81
cell_size = 30.0
time_step = 2.5
depth_floor = 0.25
half_rate = 0.5
lateral_rate = 0.2
drainage = 0.05
lower_start = 8


def solve_column(conduct_real, rhs_rows):
    layers = conduct_real.shape[0]
    zeros_row = jnp.zeros_like(conduct_real[0])
    face_coef = [0.5 * (conduct_real[layer_idx] + conduct_real[layer_idx + 1]) for layer_idx in range(layers - 1)]
    ratios = []
    values = []
    for layer_idx in range(layers):
        above_face = face_coef[layer_idx - 1] if layer_idx > 0 else zeros_row
        below_face = face_coef[layer_idx] if layer_idx < layers - 1 else zeros_row
        center = 1.0 + above_face + below_face
        if layer_idx == layers - 1:
            center = center + drainage
        if layer_idx == 0:
            divisor_now = center
            value_now = rhs_rows[0] / divisor_now
        else:
            divisor_now = center + above_face * ratios[-1]
            value_now = (rhs_rows[layer_idx] + above_face * values[-1]) / divisor_now
        ratios.append(-below_face / divisor_now)
        values.append(value_now)
    result = [values[-1]]
    for layer_idx in range(layers - 2, -1, -1):
        result.insert(0, values[layer_idx] - ratios[layer_idx] * result[0])
    return jnp.stack(result)


def land_update(soil_water, conduct_real, rainfall, infil_cap, ponded, live_mask, lateral):
    wetting = rainfall + jnp.maximum(ponded, 0.0)
    uptake = infil_cap * wetting / (wetting + half_rate)
    runoff = live_mask * rainfall * (1.0 - infil_cap / (wetting + half_rate))
    rhs_rows = soil_water.at[0].add(uptake)
    rhs_rows = rhs_rows.at[lower_start:].add(lateral)
    solved = solve_column(conduct_real, rhs_rows)
    return jnp.where(live_mask > 0, solved, soil_water), runoff


def face_flux(flux_in, level_a, level_b, bed_a, bed_b, rough_face):
    wet_depth = jnp.maximum(jnp.maximum(level_a, level_b) - jnp.maximum(bed_a, bed_b), depth_floor)
    slope_face = (level_b - level_a) / cell_size
    numer_part = flux_in - gravity * wet_depth * time_step * slope_face
    return numer_part / (1.0 + gravity * time_step * rough_face * rough_face * jnp.abs(flux_in) / wet_depth ** (7.0 / 3.0))


def advance(water_depth, east_flux, south_flux, bed_field, rough_field, east_open, south_open):
    surface = bed_field + water_depth
    east_new = face_flux(east_flux[:, :-1], surface[:, :-1], surface[:, 1:], bed_field[:, :-1], bed_field[:, 1:],
                         0.5 * (rough_field[:, :-1] + rough_field[:, 1:])) * east_open
    south_new = face_flux(south_flux[:-1], surface[:-1], surface[1:], bed_field[:-1], bed_field[1:],
                          0.5 * (rough_field[:-1] + rough_field[1:])) * south_open
    change = east_new[1:-1, 1:] - east_new[1:-1, :-1] + south_new[1:, 1:-1] - south_new[:-1, 1:-1]
    depth_new = water_depth[1:-1, 1:-1] - (time_step / cell_size) * change
    return depth_new, east_new[1:-1, 1:], south_new[1:, 1:-1]


def open_faces(anchor, margin, length, total_cells):
    position = anchor - margin + jnp.arange(length - 1, dtype=jnp.int32)
    return ((position >= 0) & (position + 1 <= total_cells - 1)).astype(jnp.float32)


def edge_lines(east_flux, south_flux, group_rows):
    east_edges = east_flux.reshape(NROWS, N_GX, TILE_C)[:, :, TILE_C - 1]
    west_edges = jnp.concatenate([jnp.zeros((NROWS, 1), jnp.float32), east_edges[:, :-1]], axis=1)
    across = jnp.stack([west_edges.T, east_edges.T], axis=1).reshape(2 * N_GX, NROWS)
    south_edges = south_flux.reshape(group_rows, TILE_R, NCOLS)[:, TILE_R - 1, :]
    north_edges = jnp.concatenate([jnp.zeros((1, NCOLS), jnp.float32), south_edges[:-1]], axis=0)
    down = jnp.stack([north_edges, south_edges], axis=1).reshape(2 * group_rows, NCOLS)
    return across, down


def reference(soil_water, conduct, rainfall, infil_cap, live_counts, send_slot, recv_row, bed_height, manning, depth_in, east_in, south_in, wet_mask):
    group_rows = N_GRP * N_GY
    depth_start = depth_in * wet_mask.astype(jnp.float32)
    tile_table = depth_start.reshape(group_rows, TILE_R, N_GX, TILE_C).transpose(0, 2, 1, 3).reshape(DEVICES, TROWS, 128)
    target = send_slot // CAP
    within = send_slot % CAP
    source = jnp.arange(DEVICES, dtype=jnp.int32)[:, None]
    row_pick = recv_row[target, source * CAP + within]
    ponded = tile_table[target, row_pick].reshape(LAND_CELLS)

    cell_index = jnp.arange(LAND_DEV, dtype=jnp.int32)
    live_grid = (cell_index[None, :] < live_counts[:, None]).astype(jnp.float32)
    live_mask = live_grid.reshape(LAND_CELLS)
    lower_part = soil_water[lower_start:].reshape(NL - lower_start, DEVICES, LAND_DEV)
    parcel_sums = jnp.sum(lower_part * live_grid[None], axis=(0, 2))
    parcel_mean = (parcel_sums / (live_counts.astype(jnp.float32) * (NL - lower_start))).reshape(group_rows, N_GX)
    padded = jnp.pad(parcel_mean, 1)
    row_place = jnp.arange(group_rows, dtype=jnp.int32)[:, None]
    col_place = jnp.arange(N_GX, dtype=jnp.int32)[None, :]
    lateral = jnp.where(row_place > 0, padded[:-2, 1:-1] - parcel_mean, 0.0)
    lateral = lateral + jnp.where(row_place < group_rows - 1, padded[2:, 1:-1] - parcel_mean, 0.0)
    lateral = lateral + jnp.where(col_place > 0, padded[1:-1, :-2] - parcel_mean, 0.0)
    lateral = lateral + jnp.where(col_place < N_GX - 1, padded[1:-1, 2:] - parcel_mean, 0.0)
    lateral_cells = jnp.repeat((lateral_rate * lateral).reshape(DEVICES), LAND_DEV)

    soil_out, runoff = land_update(soil_water, conduct.astype(jnp.float32), rainfall, infil_cap, ponded, live_mask, lateral_cells)

    blocks = runoff.reshape(DEVICES * NB, 128)
    segment_ids = (target * TROWS + row_pick).reshape(DEVICES * NB).astype(jnp.int32)
    inflow = jax.ops.segment_sum(blocks, segment_ids, num_segments=DEVICES * TROWS)
    inflow = inflow.reshape(group_rows, N_GX, TILE_R, TILE_C).transpose(0, 2, 1, 3).reshape(NROWS, NCOLS)

    bed_pad = jnp.pad(bed_height, 1)
    rough_pad = jnp.pad(manning, 1)
    east_open = open_faces(0, 1, NCOLS + 2, NCOLS)[None, :]
    south_open = open_faces(0, 1, NROWS + 2, NROWS)[:, None]
    water_depth, east_flux, south_flux = depth_start, east_in, south_in
    edge_we = jnp.zeros((2 * N_GX, NROWS), jnp.float32)
    edge_ns = jnp.zeros((2 * group_rows, NCOLS), jnp.float32)
    for step_index in range(STEPS):
        if step_index == STEPS // 2:
            water_depth = water_depth + inflow
        water_depth, east_flux, south_flux = advance(jnp.pad(water_depth, 1), jnp.pad(east_flux, 1), jnp.pad(south_flux, 1),
                                                     bed_pad, rough_pad, east_open, south_open)
        across, down = edge_lines(east_flux, south_flux, group_rows)
        edge_we = edge_we + across
        edge_ns = edge_ns + down
    return soil_out, water_depth, east_flux, south_flux, edge_we, edge_ns
```

```python
import jax
import jax.numpy as jnp
from jax import lax
from jax.experimental import pallas as pl
from jax.experimental.pallas import tpu as pltpu
from jax.sharding import PartitionSpec as P

F32 = jnp.float32
BF16 = jnp.bfloat16

NL = 16
STEPS = 8
TR = 256
TC = 512
NB = 192
LAND = NB * 128
DEV = 256
HALO = 8
ER = TR + 2 * HALO
EC = TC + 128
TILES = ER // 8
K = 7

gravity = 9.81
cell_size = 30.0
time_step = 2.5
depth_floor = 0.25
half_rate = 0.5
lateral_rate = 0.2
drainage = 0.05
slope_coef = gravity * time_step / cell_size
fric_coef = gravity * time_step

ROWS = ("grp", "gy")
ALL = ("grp", "gy", "gx")


def params(mib):
    return pltpu.CompilerParams(vmem_limit_bytes=mib * 1024 * 1024)


def iota(shape, dim):
    return lax.broadcasted_iota(jnp.int32, shape, dim)


def parts(x):
    high = x.astype(BF16)
    low = (x - high.astype(F32)).astype(BF16)
    return high, low


def hot_dot(hot, x):
    high, low = parts(x)
    both = jnp.dot(hot, jnp.concatenate([high, low], axis=1), preferred_element_type=F32)
    return both[:, :128] + both[:, 128:]


def lane_index(col):
    return jnp.concatenate([col, col], axis=1)


def turned(row):
    return jnp.broadcast_to(row, (128, row.shape[1])).T


def send_kernel(slot_ref, recv_ref, live_ref, rain_ref, cap_ref, depth_ref, wet_ref, out_ref, recv_out, tmp_ref):
    live = live_ref[0]
    cell = iota((NB, 128), 0) * 128 + iota((NB, 128), 1)
    rain_h, rain_l = parts(jnp.where(cell < live, rain_ref[...], 0.0))
    cap_h, cap_l = parts(cap_ref[...])
    rhs = jnp.concatenate([rain_h, rain_l, cap_h, cap_l], axis=1)
    slot = slot_ref[...]
    tile = iota((DEV, NB), 0)
    lane = iota((DEV, 128), 1)
    row = iota((DEV, 128), 0)
    for_west = jnp.zeros((DEV, 128), F32)
    for_east = jnp.zeros((DEV, 128), F32)
    for k in range(2):
        hot = (slot == 2 * tile + k).astype(F32).astype(BF16)
        res = jnp.dot(hot, rhs, preferred_element_type=F32)
        for a in range(2):
            got = res[:, 256 * a : 256 * a + 128] + res[:, 256 * a + 128 : 256 * a + 256]
            out_ref[pl.ds(2 * a + k, DEV, stride=K), :] = got
            g = 2 * a + k
            low, high = 124 - 8 * g, 8 * g
            moved_w = pltpu.roll(got, (128 - 8 * g) % 128, 1) if g else got
            moved_e = pltpu.roll(got, 8 * g, 1) if g else got
            for_west = jnp.where((lane >= low) & (lane < low + 4), moved_w, for_west)
            for_east = jnp.where((lane >= high) & (lane < high + 4), moved_e, for_east)
    edge = jnp.where(lane < 64, pltpu.roll(for_east, DEV - 1, 0), pltpu.roll(for_west, 1, 0))
    out_ref[pl.ds(6, DEV, stride=K), :] = edge
    tmp_ref[...] = turned(recv_ref[...].astype(F32))
    fields = []
    for c in range(4):
        d = depth_ref[:, 128 * c : 128 * c + 128] * wet_ref[:, 128 * c : 128 * c + 128].astype(F32)
        fields.append(jnp.concatenate(parts(d), axis=1))
    place4 = iota((DEV, 256), 1).astype(F32) * 4.0
    for k in range(2):
        col = tmp_ref[pl.ds(k, DEV, stride=2), :]
        recv_out[2 * k : 2 * k + 1, :] = col[:128].T[0:1]
        recv_out[2 * k + 1 : 2 * k + 2, :] = col[128:].T[0:1]
        wide = lane_index(col)
        acc = jnp.zeros((DEV, 256), F32)
        for c in range(4):
            hot = (wide == place4 + float(c)).astype(F32).astype(BF16)
            acc = acc + jnp.dot(hot, fields[c], preferred_element_type=F32)
        out_ref[pl.ds(4 + k, DEV, stride=K), :] = acc[:, :128] + acc[:, 128:]
    recv_out[4:8, :] = jnp.zeros((4, 128), F32)


def send_call(slot, recv, live, rain, cap, depth, wet):
    return pl.pallas_call(
        send_kernel,
        out_shape=(
            jax.ShapeDtypeStruct((DEV * K, 128), F32),
            jax.ShapeDtypeStruct((8, 128), F32),
        ),
        in_specs=[
            pl.BlockSpec(memory_space=pltpu.VMEM),
            pl.BlockSpec(memory_space=pltpu.VMEM),
            pl.BlockSpec(memory_space=pltpu.SMEM),
            pl.BlockSpec(memory_space=pltpu.VMEM),
            pl.BlockSpec(memory_space=pltpu.VMEM),
            pl.BlockSpec(memory_space=pltpu.VMEM),
            pl.BlockSpec(memory_space=pltpu.VMEM),
        ],
        scratch_shapes=[pltpu.VMEM((2 * DEV, 128), F32)],
        compiler_params=params(24),
        name="message",
    )(slot, recv, live, rain, cap, depth, wet)


def rows_kernel(live_ref, soil_ref, *refs):
    tops, bottoms = refs[:6], refs[6:12]
    up_ref, down_ref, mean_ref = refs[12:]
    live = live_ref[0]
    total = jnp.zeros((8, 128), F32)
    half = NB * 8
    which = iota((half, 128), 0) // 8 * 128 + iota((half, 128), 1)
    kept = jnp.where(which < live, soil_ref[...], 0.0)
    total = jnp.sum(kept.reshape(half // 8, 8, 128), axis=0)
    mean = jnp.sum(total) / (live.astype(F32) * 8.0)
    mean_row = jnp.full((8, TC), mean, F32)
    for src, out in ((tops, up_ref), (bottoms, down_ref)):
        depth, wet, bed, man, east, south = (r[...] for r in src)
        out[0:8, :] = depth * wet.astype(F32)
        out[8:16, :] = bed
        out[16:24, :] = man
        out[24:32, :] = east
        out[32:40, :] = south
        out[40:48, :] = mean_row
    mean_ref[...] = mean_row[:, :128]


def rows_call(live, soil, fields):
    top = [pl.BlockSpec((8, TC), lambda i: (0, 0)) for _ in range(6)]
    bottom = [pl.BlockSpec((8, TC), lambda i: (TR // 8 - 1, 0)) for _ in range(6)]
    strip = jax.ShapeDtypeStruct((48, TC), F32)
    return pl.pallas_call(
        rows_kernel,
        grid=(1,),
        out_shape=(strip, strip, jax.ShapeDtypeStruct((8, 128), F32)),
        in_specs=[pl.BlockSpec(memory_space=pltpu.SMEM), pl.BlockSpec((NB * 8, 128), lambda i: (1, 0))] + top + bottom,
        compiler_params=params(16),
        name="row_strips",
    )(live, soil, *fields, *fields)


def cols_kernel(north_ref, south_ref, recv_ref, mean_ref, *refs):
    west, east = refs[:6], refs[6:12]
    to_west, to_east = refs[12:]
    lane = iota((ER, 128), 1)
    for src, out, first, half in ((west, to_west, 0, 0), (east, to_east, 120, 3)):
        depth, wet, bed, man, qe, qs = (r[...] for r in src)
        acc = jnp.zeros((ER, 128), F32)
        for a, own in enumerate((depth * wet.astype(F32), bed, man, qe, qs)):
            cols = slice(128 * half, 128 * half + 128)
            whole = jnp.concatenate([north_ref[8 * a : 8 * a + 8, cols], own, south_ref[8 * a : 8 * a + 8, cols]], axis=0)
            shift = (8 * a - first) % 128
            moved = pltpu.roll(whole, shift, 1) if shift else whole
            acc = jnp.where((lane >= 8 * a) & (lane < 8 * a + 8), moved, acc)
        out[0:ER, :] = acc
        row = iota((8, 128), 0)
        out[ER : ER + 8, :] = jnp.where(row < 4, recv_ref[...], mean_ref[...])


def cols_call(north, south, recv, mean, fields):
    full = pl.BlockSpec((48, TC), lambda i: (0, 0))
    small = pl.BlockSpec((8, 128), lambda i: (0, 0))
    west = [pl.BlockSpec((TR, 128), lambda i: (0, 0)) for _ in range(6)]
    east = [pl.BlockSpec((TR, 128), lambda i: (0, 3)) for _ in range(6)]
    strip = jax.ShapeDtypeStruct((ER + 8, 128), F32)
    return pl.pallas_call(
        cols_kernel,
        grid=(1,),
        out_shape=(strip, strip),
        in_specs=[full, full, small, small] + west + east,
        compiler_params=params(16),
        name="column_strips",
    )(north, south, recv, mean, *fields, *fields)


def run_steps(count, s_ref, qe_ref, qs_ref, mbe_ref, cre_ref, mbs_ref, crs_ref, line_ref, edge_ref, row0, col0):
    lane = iota((8, EC), 1)
    gcol = jnp.where(lane < TC + 64, lane, lane - EC) + col0
    total_cols = TC * lax.axis_size("gx")
    total_rows = TR * lax.axis_size(ROWS)
    ge = jnp.where((gcol >= 0) & (gcol + 1 <= total_cols - 1), slope_coef, 0.0).astype(F32)
    sub = iota((8, EC), 0)
    last_row, first_row = sub == 7, sub == 0
    sub1 = iota((8, 128), 0)

    def flux(q, a, b, mb, cr, g):
        h = jnp.maximum(jnp.maximum(a, b) - mb, depth_floor)
        numer = q - g * (h * (b - a))
        power = jnp.exp2(jnp.log(h) * F32(-7.0 / 3.0 / 0.6931471805599453))
        den = 1.0 + cr * jnp.abs(q) * power
        r = pl.reciprocal(den, approx=True)
        r = r * (2.0 - den * r)
        return numer * r

    def one_step(_, c0):
        def body(i, carry):
            s, s_up, qn = carry
            r = pl.multiple_of(i * 8, 8)
            here = pl.ds(r, 8)
            s_nx = s_ref[pl.ds(r + 8, 8), :]
            s_nx_up = pltpu.roll(s_nx, 7, 0)
            s_south = jnp.where(last_row, s_nx_up, s_up)
            s_east = pltpu.roll(s, EC - 1, 1)
            grow = row0 - HALO + r + sub1
            gs1 = jnp.where((grow >= 0) & (grow + 1 <= total_rows - 1), slope_coef, 0.0).astype(F32)
            gs = jnp.concatenate([gs1] * (EC // 128), axis=1)
            qe = flux(qe_ref[here, :], s, s_east, mbe_ref[here, :], cre_ref[here, :], ge)
            qs = flux(qs_ref[here, :], s, s_south, mbs_ref[here, :], crs_ref[here, :], gs)
            qe_west = pltpu.roll(qe, 1, 1)
            qs_down = pltpu.roll(qs, 1, 0)
            qs_north = jnp.where(first_row, qn, qs_down)
            s_ref[here, :] = s - F32(time_step / cell_size) * ((qe - qe_west) + (qs - qs_north))
            qe_ref[here, :] = qe
            qs_ref[here, :] = qs
            edge_ref[here, :] = edge_ref[here, :] + qe[:, TC - 128 :]
            return s_nx, s_nx_up, qs_down

        s0 = s_ref[0:8, :]
        lax.fori_loop(0, TILES, body, (s0, pltpu.roll(s0, 7, 0), jnp.zeros((8, EC), F32)))
        line_ref[0:8, :] = line_ref[0:8, :] + qs_ref[0:8, :]
        line_ref[8:16, :] = line_ref[8:16, :] + qs_ref[TR : TR + 8, :]
        return c0

    lax.fori_loop(0, count, one_step, 0)


def first_kernel(
    north_ref, south_ref, west_ref, east_ref, mean_ref,
    depth_ref, wet_ref, bed_ref, man_ref, qe_in, qs_in,
    s_ref, qe_ref, qs_ref, mbe_ref, cre_ref, mbs_ref, crs_ref, line_ref, edge_ref, lat_ref, halo_ref,
    bed_x, man_x,
):
    rows = lax.axis_index(ROWS)
    cols = lax.axis_index("gx")
    n_rows, n_cols = lax.axis_size(ROWS), lax.axis_size("gx")
    row0, col0 = rows * TR, cols * TC
    lane = iota((ER, 128), 1)
    own = slice(HALO, HALO + TR)

    def side(a):
        e = east_ref[0:ER, :]
        w = west_ref[0:ER, :]
        shift = (128 - 8 * a) % 128
        e = pltpu.roll(e, shift, 1) if shift else e
        w = pltpu.roll(w, 120 - 8 * a, 1)
        return jnp.where(lane < 8, e, jnp.where(lane >= 120, w, 0.0))

    def assemble(out, a, inner):
        out[own, 0:TC] = inner
        out[0:HALO, 0:TC] = north_ref[8 * a : 8 * a + 8, :]
        out[ER - HALO : ER, 0:TC] = south_ref[8 * a : 8 * a + 8, :]
        out[0:ER, TC:EC] = side(a)

    assemble(s_ref, 0, depth_ref[...] * wet_ref[...].astype(F32))
    halo_ref[...] = s_ref[own, TC:EC]
    assemble(bed_x, 1, bed_ref[...])
    assemble(man_x, 2, man_ref[...])
    assemble(qe_ref, 3, qe_in[...])
    assemble(qs_ref, 4, qs_in[...])
    zero = jnp.zeros((8, EC), F32)
    s_ref[ER : ER + 8, :] = zero
    bed_x[ER : ER + 8, :] = zero
    man_x[ER : ER + 8, :] = zero
    line_ref[...] = jnp.zeros((16, EC), F32)

    lane8 = iota((8, EC), 1)
    gcol = jnp.where(lane8 < TC + 64, lane8, lane8 - EC) + col0
    east_open = (gcol >= 0) & (gcol + 1 <= n_cols * TC - 1)
    sub = iota((8, EC), 0)

    def setup(i, carry):
        r = pl.multiple_of(i * 8, 8)
        here = pl.ds(r, 8)
        nxt = pl.ds(r + 8, 8)
        bed, man = bed_x[here, :], man_x[here, :]
        bed_s = jnp.where(sub == 7, pltpu.roll(bed_x[nxt, :], 7, 0), pltpu.roll(bed, 7, 0))
        man_s = jnp.where(sub == 7, pltpu.roll(man_x[nxt, :], 7, 0), pltpu.roll(man, 7, 0))
        bed_e = pltpu.roll(bed, EC - 1, 1)
        man_e = pltpu.roll(man, EC - 1, 1)
        mbe_ref[here, :] = jnp.maximum(bed, bed_e)
        mbs_ref[here, :] = jnp.maximum(bed, bed_s)
        rough_e = 0.5 * (man + man_e)
        rough_s = 0.5 * (man + man_s)
        cre_ref[here, :] = fric_coef * rough_e * rough_e
        crs_ref[here, :] = fric_coef * rough_s * rough_s
        s_ref[here, :] = s_ref[here, :] + bed
        grow = row0 - HALO + r + sub
        south_open = (grow >= 0) & (grow + 1 <= n_rows * TR - 1)
        qe_ref[here, :] = jnp.where(east_open, qe_ref[here, :], 0.0)
        qs_ref[here, :] = jnp.where(south_open, qs_ref[here, :], 0.0)
        edge_ref[here, :] = jnp.zeros((8, 256), F32)
        return carry

    lax.fori_loop(0, TILES, setup, 0)

    mean = mean_ref[...]
    lat = jnp.where(rows > 0, north_ref[40:48, 0:128] - mean, 0.0)
    lat = lat + jnp.where(rows < n_rows - 1, south_ref[40:48, 0:128] - mean, 0.0)
    lat = lat + jnp.where(cols > 0, west_ref[ER + 7 : ER + 8, :] - mean, 0.0)
    lat = lat + jnp.where(cols < n_cols - 1, east_ref[ER + 7 : ER + 8, :] - mean, 0.0)
    lat_ref[...] = lateral_rate * lat

    run_steps(STEPS // 2, s_ref, qe_ref, qs_ref, mbe_ref, cre_ref, mbs_ref, crs_ref, line_ref, edge_ref, row0, col0)


def first_call(north, south, west, east, mean, fields):
    ext = jax.ShapeDtypeStruct((ER, EC), F32)
    ext1 = jax.ShapeDtypeStruct((ER + 8, EC), F32)
    return pl.pallas_call(
        first_kernel,
        out_shape=(
            ext1, ext, ext, ext, ext, ext, ext,
            jax.ShapeDtypeStruct((16, EC), F32),
            jax.ShapeDtypeStruct((ER, 256), F32),
            jax.ShapeDtypeStruct((8, 128), F32),
            jax.ShapeDtypeStruct((TR, 128), F32),
        ),
        scratch_shapes=[pltpu.VMEM((ER + 8, EC), F32), pltpu.VMEM((ER + 8, EC), F32)],
        compiler_params=params(32),
        name="first_steps",
    )(north, south, west, east, mean, *fields)


def inflow_kernel(sent_ref, got_ref, recv_ref, west_ref, east_ref, halo_ref, in_ref, side_ref, up_ref, down_ref):
    lane = iota((DEV, 128), 1)
    place4 = iota((TR, DEV), 0).astype(F32) * 4.0

    def runoff(rain, cap, pond):
        wetting = rain + jnp.maximum(pond, 0.0)
        return rain * (1.0 - cap / (wetting + half_rate))

    def recv_row(ref, k, base):
        return jnp.concatenate([ref[base + 2 * k : base + 2 * k + 1, :], ref[base + 2 * k + 1 : base + 2 * k + 2, :]], axis=1)

    flows = []
    for k in range(2):
        rain = got_ref[pl.ds(k, DEV, stride=K), :]
        cap = got_ref[pl.ds(2 + k, DEV, stride=K), :]
        pond = sent_ref[pl.ds(4 + k, DEV, stride=K), :]
        flows.append(jnp.concatenate(parts(runoff(rain, cap, pond)), axis=1))
    for c in range(4):
        acc = jnp.zeros((TR, 256), F32)
        for k in range(2):
            hot = (recv_row(recv_ref, k, 0) == place4 + float(c)).astype(F32).astype(BF16)
            acc = acc + jnp.dot(hot, flows[k], preferred_element_type=F32)
        in_ref[:, 128 * c : 128 * c + 128] = acc[:, :128] + acc[:, 128:]

    edge = got_ref[pl.ds(6, DEV, stride=K), :]
    depth = halo_ref[...]
    lane_place = iota((DEV, TR), 1).astype(F32) * 4.0
    is_east, is_west = lane < 4, lane >= 124
    acc = jnp.zeros((TR, 128), F32)
    for k in range(2):
        def pick(g):
            if g == 0:
                return edge
            return jnp.where(lane < 64, pltpu.roll(edge, 128 - 8 * g, 1), pltpu.roll(edge, 8 * g, 1))

        rain, cap = pick(k), pick(2 + k)
        pond = jnp.zeros((DEV, 128), F32)
        total = []
        for ref, c, mask in ((west_ref, 3, is_west), (east_ref, 0, is_east)):
            row = recv_row(ref, k, ER)
            col = lane_index(turned(row))
            hot = (col == lane_place + float(c)).astype(F32).astype(BF16)
            pond = jnp.where(mask, hot_dot(hot, depth), pond)
        flow = jnp.where(is_east | is_west, runoff(rain, cap, pond), 0.0)
        for ref, c, mask in ((west_ref, 3, is_west), (east_ref, 0, is_east)):
            hot = (recv_row(ref, k, ER) == place4 + float(c)).astype(F32).astype(BF16)
            acc = acc + hot_dot(hot, jnp.where(mask, flow, 0.0))
    rows = lax.axis_index("gx")
    acc = jnp.where(is_west & (rows > 0), acc, jnp.where(is_east & (rows < lax.axis_size("gx") - 1), acc, 0.0))
    side_ref[...] = acc
    up_ref[:, 0:TC] = in_ref[0:8, :]
    up_ref[:, TC:EC] = acc[0:8, :]
    down_ref[:, 0:TC] = in_ref[TR - 8 : TR, :]
    down_ref[:, TC:EC] = acc[TR - 8 : TR, :]


def inflow_call(sent, got, recv, west, east, halo):
    strip = jax.ShapeDtypeStruct((8, EC), F32)
    return pl.pallas_call(
        inflow_kernel,
        out_shape=(
            jax.ShapeDtypeStruct((TR, TC), F32),
            jax.ShapeDtypeStruct((TR, 128), F32),
            strip,
            strip,
        ),
        compiler_params=params(24),
        name="inflow",
    )(sent, got, recv, west, east, halo)


def last_kernel(
    in_ref, side_ref, north_ref, south_ref, bed_ref,
    s_in, qe_in, qs_in, mbe_ref, cre_ref, mbs_ref, crs_ref, line_in, edge_in,
    depth_out, east_out, south_out, we_ref, ns_ref,
    s_ref, qe_ref, qs_ref, line_ref, edge_ref,
):
    row0 = lax.axis_index(ROWS) * TR
    col0 = lax.axis_index("gx") * TC
    own = slice(HALO, HALO + TR)
    s_ref[0:8, :] = s_in[0:8, :] + north_ref[...]
    s_ref[ER - 8 : ER, :] = s_in[ER - 8 : ER, :] + south_ref[...]
    s_ref[own, 0:TC] = s_in[own, 0:TC] + in_ref[...]
    s_ref[own, TC:EC] = s_in[own, TC:EC] + side_ref[...]
    s_ref[ER : ER + 8, :] = s_in[ER : ER + 8, :]
    qe_ref[...] = qe_in[...]
    qs_ref[...] = qs_in[...]
    line_ref[...] = line_in[...]
    edge_ref[...] = edge_in[...]
    run_steps(STEPS - STEPS // 2, s_ref, qe_ref, qs_ref, mbe_ref, cre_ref, mbs_ref, crs_ref, line_ref, edge_ref, row0, col0)
    depth_out[...] = s_ref[own, 0:TC] - bed_ref[...]
    east_out[...] = qe_ref[own, 0:TC]
    south_out[...] = qs_ref[own, 0:TC]
    we_ref[0:1, :] = edge_ref[own, 128:256].T[127:128, :]
    we_ref[1:2, :] = edge_ref[own, 0:128].T[127:128, :]
    ns_ref[0:1, :] = line_ref[7:8, 0:TC]
    ns_ref[1:2, :] = line_ref[15:16, 0:TC]


def last_call(inflow, side, north, south, bed, state):
    tile = jax.ShapeDtypeStruct((TR, TC), F32)
    return pl.pallas_call(
        last_kernel,
        out_shape=(tile, tile, tile, jax.ShapeDtypeStruct((2, TR), F32), jax.ShapeDtypeStruct((2, TC), F32)),
        scratch_shapes=[
            pltpu.VMEM((ER + 8, EC), F32),
            pltpu.VMEM((ER, EC), F32),
            pltpu.VMEM((ER, EC), F32),
            pltpu.VMEM((16, EC), F32),
            pltpu.VMEM((ER, 256), F32),
        ],
        compiler_params=params(32),
        name="last_steps",
    )(inflow, side, north, south, bed, *state)


def land_kernel(live_ref, slot_ref, got_ref, lat_ref, rain_ref, cap_ref, soil_ref, cond_ref, out_ref, cond_x, pond_ref):
    live = live_ref[0]
    slot = jnp.broadcast_to(slot_ref[...].astype(F32), (128, NB))
    slot = jnp.concatenate([slot, jnp.full((128, 256 - NB), -1.0, F32)], axis=1).T
    slot = lane_index(slot[0:NB])
    tile2 = iota((NB, DEV), 1).astype(F32) * 2.0
    pond = jnp.zeros((NB, 128), F32)
    for k in range(2):
        hot = (slot == tile2 + float(k)).astype(F32).astype(BF16)
        pond = pond + hot_dot(hot, got_ref[pl.ds(4 + k, DEV, stride=K), :])
    pond_ref[...] = pond
    for b in range(NB):
        cond_x[16 * b : 16 * b + 16, :] = cond_ref[:, 128 * b : 128 * b + 128].astype(F32)
    lat = lat_ref[...]
    sub, lane = iota((8, 128), 0), iota((8, 128), 1)

    def body(c, carry):
        base = pl.multiple_of(c * 8, 8)
        blocks = pl.ds(base, 8)
        rain, cap = rain_ref[blocks, :], cap_ref[blocks, :]
        wetting = rain + jnp.maximum(pond_ref[blocks, :], 0.0)
        uptake = cap * wetting / (wetting + half_rate)
        kept = ((base + sub) * 128 + lane) < live

        def soil_at(layer):
            return pl.ds((layer // 8) * (NB * 8) + c * 64 + layer % 8, 8, stride=8)

        cond = [cond_x[pl.ds(c * 128 + layer, 8, stride=16), :] for layer in range(NL)]
        face = [0.5 * (cond[j] + cond[j + 1]) for j in range(NL - 1)]
        ratios, values = [], []
        for j in range(NL):
            rhs = soil_ref[soil_at(j), :]
            if j == 0:
                rhs = rhs + uptake
            if j >= 8:
                rhs = rhs + lat
            center = 1.0
            if j > 0:
                center = center + face[j - 1]
            if j < NL - 1:
                center = center + face[j]
            else:
                center = center + drainage
            if j > 0:
                center = center + face[j - 1] * ratios[-1]
                rhs = rhs + face[j - 1] * values[-1]
            r = pl.reciprocal(center, approx=True)
            r = r * (2.0 - center * r)
            if j < NL - 1:
                ratios.append(-face[j] * r)
            values.append(rhs * r)
        x = values[-1]
        for j in range(NL - 1, -1, -1):
            if j < NL - 1:
                x = values[j] - ratios[j] * x
            out_ref[soil_at(j), :] = jnp.where(kept, x, soil_ref[soil_at(j), :])
        return carry

    lax.fori_loop(0, NB // 8, body, 0)


def land_call(live, slot, got, lat, rain, cap, soil, cond):
    return pl.pallas_call(
        land_kernel,
        out_shape=jax.ShapeDtypeStruct((NB * NL, 128), F32),
        in_specs=[pl.BlockSpec(memory_space=pltpu.SMEM)] + [pl.BlockSpec(memory_space=pltpu.VMEM)] * 7,
        scratch_shapes=[pltpu.VMEM((NB * NL, 128), F32), pltpu.VMEM((NB, 128), F32)],
        compiler_params=params(24),
        name="soil_columns",
    )(live, slot, got, lat, rain, cap, soil, cond)


def shift(first, second, axis):
    count = lax.axis_size(axis)
    ahead = [(i, i + 1) for i in range(count - 1)]
    back = [(j, i) for i, j in ahead]
    return lax.ppermute(first, axis, ahead), lax.ppermute(second, axis, back)


def local(
    soil_water, conduct, rainfall, infil_cap, live_counts, send_slot, recv_row,
    bed_height, manning, depth_in, east_in, south_in, wet_mask,
):
    rain = rainfall.reshape(NB, 128)
    cap = infil_cap.reshape(NB, 128)
    soil = soil_water.reshape(2, 8, NB, 128).transpose(0, 2, 1, 3).reshape(NB * NL, 128)
    fields = (depth_in, wet_mask, bed_height, manning, east_in, south_in)

    sent, recv = send_call(send_slot, recv_row, live_counts, rain, cap, depth_in, wet_mask)
    got = lax.all_to_all(sent.reshape(DEV, 1, K * 128), ALL, split_axis=0, concat_axis=0, tiled=True)
    got = got.reshape(DEV * K, 128)

    up, down, mean = rows_call(live_counts, soil, fields)
    north, south = shift(down, up, ROWS)
    to_west, to_east = cols_call(north, south, recv, mean, fields)
    west, east = shift(to_east, to_west, "gx")
    *state, lat, halo = first_call(north, south, west, east, mean, fields)

    inflow, side, in_up, in_down = inflow_call(sent, got, recv, west, east, halo)
    in_north, in_south = shift(in_down, in_up, ROWS)
    soil_out = land_call(live_counts, send_slot, got, lat, rain, cap, soil, conduct)
    depth, east_q, south_q, edge_we, edge_ns = last_call(inflow, side, in_north, in_south, bed_height, state)
    soil_out = soil_out.reshape(2, NB, 8, 128).transpose(0, 2, 1, 3).reshape(NL, LAND)
    return soil_out, depth, east_q, south_q, edge_we, edge_ns


def solution(mesh):
    placed = (
        P(None, ALL),
        P(None, ALL),
        P(ALL),
        P(ALL),
        P(ALL),
        P(ALL, None),
        P(ALL, None),
    ) + (P(ROWS, "gx"),) * 6
    return jax.shard_map(
        local,
        mesh=mesh,
        in_specs=placed,
        out_specs=(
            P(None, ALL),
            P(ROWS, "gx"),
            P(ROWS, "gx"),
            P(ROWS, "gx"),
            P("gx", ROWS),
            P(ROWS, "gx"),
        ),
        check_vma=False,
    )
```

```python
import jax
import jax.numpy as jnp
from jax import lax
from jax.experimental import pallas as pl
from jax.experimental.pallas import tpu as pltpu
from jax.sharding import PartitionSpec as P

F32 = jnp.float32
BF16 = jnp.bfloat16

NL = 16
STEPS = 8
TR = 256
TC = 512
NB = 192
LAND = NB * 128
DEV = 256
HALO = 8
ER = TR + 2 * HALO
TILES = ER // 8
K = 7
PANELS = 5
SPAN = ER + 16
EXT = PANELS * SPAN
STRIP = 5 * PANELS * 8 + 8

gravity = 9.81
cell_size = 30.0
time_step = 2.5
depth_floor = 0.25
half_rate = 0.5
lateral_rate = 0.2
drainage = 0.05
slope_coef = gravity * time_step / cell_size
fric_coef = gravity * time_step

ROWS = ("grp", "gy")
ALL = ("grp", "gy", "gx")
VMEM = pl.BlockSpec(memory_space=pltpu.VMEM)
SMEM = pl.BlockSpec(memory_space=pltpu.SMEM)
HBM = pl.BlockSpec(memory_space=pltpu.HBM)
ANY = pl.BlockSpec(memory_space=pl.ANY)


def params(mib):
    return pltpu.CompilerParams(vmem_limit_bytes=mib * 1024 * 1024)


def array(*shape):
    return jax.ShapeDtypeStruct(shape, F32)


def iota(shape, dim):
    return lax.broadcasted_iota(jnp.int32, shape, dim)


def copies(sem, pairs):
    made = [pltpu.make_async_copy(src, dst, sem.at[n]) for n, (src, dst) in enumerate(pairs)]
    for c in made:
        c.start()
    return made


def wait(made):
    for c in made:
        c.wait()


def parts(x):
    high = x.astype(BF16)
    low = (x - high.astype(F32)).astype(BF16)
    return high, low


def hot_dot(hot, x):
    both = jnp.dot(hot, jnp.concatenate(parts(x), axis=1), preferred_element_type=F32)
    return both[:, :128] + both[:, 128:]


def as_hot(mask):
    return mask.astype(F32).astype(BF16)


def twice(col):
    return jnp.concatenate([col, col], axis=1)


def turned(row):
    return jnp.broadcast_to(row, (128, row.shape[1])).T


def send_kernel(
    live_ref, slot_hbm, recv_hbm, rain_hbm, cap_hbm, depth_hbm, wet_hbm,
    out_hbm, pond_hbm, recv_out,
    slot_ref, recv_ref, rain_ref, cap_ref, depth_ref, wet_ref, out_ref, pond_ref, tmp_ref, sem, sem_out,
):
    got = copies(
        sem,
        (
            (slot_hbm, slot_ref), (rain_hbm, rain_ref), (cap_hbm, cap_ref),
            (recv_hbm, recv_ref), (depth_hbm, depth_ref), (wet_hbm, wet_ref),
        ),
    )
    live = live_ref[0]
    wait(got[:3])
    cell = iota((NB, 128), 0) * 128 + iota((NB, 128), 1)
    rain = jnp.where(cell < live, rain_ref[...], 0.0)
    rhs = jnp.concatenate(parts(rain) + parts(cap_ref[...]), axis=1)
    slot = slot_ref[...]
    tile = iota((DEV, NB), 0)
    lane = iota((DEV, 128), 1)
    for_west = jnp.zeros((DEV, 128), F32)
    for_east = jnp.zeros((DEV, 128), F32)
    for k in range(2):
        res = jnp.dot(as_hot(slot == 2 * tile + k), rhs, preferred_element_type=F32)
        for a in range(2):
            block = res[:, 256 * a : 256 * a + 128] + res[:, 256 * a + 128 : 256 * a + 256]
            out_ref[pl.ds(2 * a + k, DEV, stride=K), :] = block
            g = 2 * a + k
            low, high = 124 - 8 * g, 8 * g
            moved_w = pltpu.roll(block, (128 - 8 * g) % 128, 1) if g else block
            moved_e = pltpu.roll(block, 8 * g, 1) if g else block
            for_west = jnp.where((lane >= low) & (lane < low + 4), moved_w, for_west)
            for_east = jnp.where((lane >= high) & (lane < high + 4), moved_e, for_east)
    edge = jnp.where(lane < 64, pltpu.roll(for_east, DEV - 1, 0), pltpu.roll(for_west, 1, 0))
    out_ref[pl.ds(6, DEV, stride=K), :] = edge
    wait(got[3:])
    tmp_ref[...] = turned(recv_ref[...].astype(F32))
    fields = []
    for c in range(4):
        cols = slice(128 * c, 128 * c + 128)
        fields.append(jnp.concatenate(parts(depth_ref[:, cols] * wet_ref[:, cols].astype(F32)), axis=1))
    place4 = iota((DEV, 256), 1).astype(F32) * 4.0
    recv_out[4:8, :] = jnp.zeros((4, 128), F32)
    for k in range(2):
        col = tmp_ref[pl.ds(k, DEV, stride=2), :]
        recv_out[2 * k : 2 * k + 1, :] = col[:128].T[0:1]
        recv_out[2 * k + 1 : 2 * k + 2, :] = col[128:].T[0:1]
        wide = twice(col)
        acc = jnp.zeros((DEV, 256), F32)
        for c in range(4):
            acc = acc + jnp.dot(as_hot(wide == place4 + float(c)), fields[c], preferred_element_type=F32)
        pond = acc[:, :128] + acc[:, 128:]
        out_ref[pl.ds(4 + k, DEV, stride=K), :] = pond
        pond_ref[DEV * k : DEV * k + DEV, :] = pond
    wait(copies(sem_out, ((out_ref, out_hbm), (pond_ref, pond_hbm))))


def send_call(live, slot, recv, rain, cap, depth, wet):
    return pl.pallas_call(
        send_kernel,
        out_shape=(array(DEV * K, 128), array(2 * DEV, 128), array(8, 128)),
        in_specs=[SMEM] + [HBM] * 6,
        out_specs=(HBM, HBM, VMEM),
        scratch_shapes=[
            pltpu.VMEM((1, NB), jnp.int32),
            pltpu.VMEM((1, 2 * DEV), jnp.int32),
            pltpu.VMEM((NB, 128), F32),
            pltpu.VMEM((NB, 128), F32),
            pltpu.VMEM((TR, TC), F32),
            pltpu.VMEM((TR, TC), jnp.int32),
            pltpu.VMEM((DEV * K, 128), F32),
            pltpu.VMEM((2 * DEV, 128), F32),
            pltpu.VMEM((2 * DEV, 128), F32),
            pltpu.SemaphoreType.DMA((6,)),
            pltpu.SemaphoreType.DMA((2,)),
        ],
        compiler_params=params(24),
        name="message",
    )(live, slot, recv, rain, cap, depth, wet)


def cols_kernel(
    live_ref, recv_ref, soil_hbm, depth, wet, bed, man, qe, qs,
    to_west, to_east, mean_ref,
    soil_ref, west_ref, east_ref, wet_w, wet_e, sem,
):
    left, right = slice(0, 128), slice(TC - 128, TC)
    pairs = [(wet.at[:, left], wet_w), (wet.at[:, right], wet_e)]
    for n, f in enumerate((depth, bed, man, qe, qs)):
        rows = slice(TR * n, TR * n + TR)
        pairs.append((f.at[:, left], west_ref.at[rows, :]))
        pairs.append((f.at[:, right], east_ref.at[rows, :]))
    pairs.append((soil_hbm.at[NB * 8 : NB * 16, :], soil_ref))
    got = copies(sem, pairs)
    wait(got[:-1])
    lane = iota((TR, 128), 1)
    for src, mask, out, first in ((west_ref, wet_w, to_west, 0), (east_ref, wet_e, to_east, 120)):
        acc = jnp.zeros((TR, 128), F32)
        for n in range(5):
            own = src[TR * n : TR * n + TR, :]
            if n == 0:
                own = own * mask[...].astype(F32)
            shift = (8 * n - first) % 128
            moved = pltpu.roll(own, shift, 1) if shift else own
            acc = jnp.where((lane >= 8 * n) & (lane < 8 * n + 8), moved, acc)
        out[0:TR, :] = acc
    live = live_ref[0]
    half = NB * 8
    wait(got[-1:])
    which = iota((half, 128), 0) // 8 * 128 + iota((half, 128), 1)
    kept = jnp.where(which < live, soil_ref[...], 0.0)
    total = jnp.sum(kept.reshape(half // 8, 8, 128), axis=0)
    mean = jnp.sum(total) / (live.astype(F32) * 8.0)
    row = jnp.full((8, 128), mean, F32)
    mean_ref[...] = row
    tail = jnp.where(iota((8, 128), 0) < 4, recv_ref[...], row)
    to_west[TR : TR + 8, :] = tail
    to_east[TR : TR + 8, :] = tail


def cols_call(live, recv, soil, fields):
    return pl.pallas_call(
        cols_kernel,
        out_shape=(array(TR + 8, 128), array(TR + 8, 128), array(8, 128)),
        in_specs=[SMEM, VMEM] + [HBM] * 7,
        scratch_shapes=[
            pltpu.VMEM((NB * 8, 128), F32),
            pltpu.VMEM((5 * TR, 128), F32),
            pltpu.VMEM((5 * TR, 128), F32),
            pltpu.VMEM((TR, 128), jnp.int32),
            pltpu.VMEM((TR, 128), jnp.int32),
            pltpu.SemaphoreType.DMA((13,)),
        ],
        compiler_params=params(16),
        name="column_strips",
    )(live, recv, soil, *fields)


def rows_kernel(
    west_ref, east_ref, mean_ref, depth, wet, bed, man, qe, qs,
    up_ref, down_ref, side_hbm, note_hbm,
    top_ref, bottom_ref, wet_t, wet_b, side_ref, note_ref, sem, sem_out,
):
    first, last = slice(0, 8), slice(TR - 8, TR)
    pairs = [(wet.at[first, :], wet_t), (wet.at[last, :], wet_b)]
    for n, f in enumerate((depth, bed, man, qe, qs)):
        rows = slice(8 * n, 8 * n + 8)
        pairs.append((f.at[first, :], top_ref.at[rows, :]))
        pairs.append((f.at[last, :], bottom_ref.at[rows, :]))
    got = copies(sem, pairs)
    lane = iota((TR, 128), 1)
    for n in range(5):
        shift = (128 - 8 * n) % 128
        e, w = east_ref[0:TR, :], west_ref[0:TR, :]
        e = pltpu.roll(e, shift, 1) if shift else e
        w = pltpu.roll(w, 120 - 8 * n, 1)
        side_ref[TR * n : TR * n + TR, :] = jnp.where(lane < 8, e, jnp.where(lane >= 120, w, 0.0))
    note_ref[0:8, :] = west_ref[TR : TR + 8, :]
    note_ref[8:16, :] = east_ref[TR : TR + 8, :]
    stored = copies(sem_out, ((side_ref, side_hbm), (note_ref, note_hbm)))
    wait(got)
    for src, mask, out, at in ((top_ref, wet_t, up_ref, 0), (bottom_ref, wet_b, down_ref, TR - 8)):
        for n in range(5):
            for j in range(PANELS):
                to = slice(8 * (PANELS * n + j), 8 * (PANELS * n + j) + 8)
                if j < 4:
                    cols = slice(128 * j, 128 * j + 128)
                    own = src[8 * n : 8 * n + 8, cols]
                    if n == 0:
                        own = own * mask[:, cols].astype(F32)
                    out[to, :] = own
                else:
                    out[to, :] = side_ref[TR * n + at : TR * n + at + 8, :]
        out[STRIP - 8 : STRIP, :] = mean_ref[...]
    wait(stored)


def rows_call(west, east, mean, fields):
    return pl.pallas_call(
        rows_kernel,
        out_shape=(array(STRIP, 128), array(STRIP, 128), array(5 * TR, 128), array(16, 128)),
        in_specs=[VMEM] * 3 + [HBM] * 6,
        out_specs=(VMEM, VMEM, HBM, HBM),
        scratch_shapes=[
            pltpu.VMEM((40, TC), F32),
            pltpu.VMEM((40, TC), F32),
            pltpu.VMEM((8, TC), jnp.int32),
            pltpu.VMEM((8, TC), jnp.int32),
            pltpu.VMEM((5 * TR, 128), F32),
            pltpu.VMEM((16, 128), F32),
            pltpu.SemaphoreType.DMA((12,)),
            pltpu.SemaphoreType.DMA((2,)),
        ],
        compiler_params=params(16),
        name="row_strips",
    )(west, east, mean, *fields)


def inflow_kernel(
    got_ref, pond_hbm, recv_hbm, side_hbm, note_hbm,
    in_ref, up_ref, down_ref,
    pond_ref, recv_ref, depth_ref, note_ref, sem,
):
    moved = copies(
        sem,
        (
            (pond_hbm, pond_ref), (recv_hbm, recv_ref),
            (side_hbm.at[0:TR, :], depth_ref), (note_hbm, note_ref),
        ),
    )
    lane = iota((DEV, 128), 1)
    place4 = iota((TR, DEV), 0).astype(F32) * 4.0

    def runoff(rain, cap, pond):
        wetting = rain + jnp.maximum(pond, 0.0)
        return rain * (1.0 - cap / (wetting + half_rate))

    def line(ref, k, base):
        at = base + 2 * k
        return jnp.concatenate([ref[at : at + 1, :], ref[at + 1 : at + 2, :]], axis=1)

    wait(moved)
    flows = []
    for k in range(2):
        rain = got_ref[pl.ds(k, DEV, stride=K), :]
        cap = got_ref[pl.ds(2 + k, DEV, stride=K), :]
        flow = runoff(rain, cap, pond_ref[DEV * k : DEV * k + DEV, :])
        flows.append(jnp.concatenate(parts(flow), axis=1))
    for c in range(4):
        acc = jnp.zeros((TR, 256), F32)
        for k in range(2):
            hot = as_hot(line(recv_ref, k, 0) == place4 + float(c))
            acc = acc + jnp.dot(hot, flows[k], preferred_element_type=F32)
        in_ref[TR * c : TR * c + TR, :] = acc[:, :128] + acc[:, 128:]

    edge = got_ref[pl.ds(6, DEV, stride=K), :]
    depth = depth_ref[...]
    lane_place = iota((DEV, TR), 1).astype(F32) * 4.0
    is_east, is_west = lane < 4, lane >= 124
    acc = jnp.zeros((TR, 128), F32)

    def pick(g):
        if g == 0:
            return edge
        return jnp.where(lane < 64, pltpu.roll(edge, 128 - 8 * g, 1), pltpu.roll(edge, 8 * g, 1))

    sides = ((0, 3, is_west), (8, 0, is_east))
    for k in range(2):
        rain, cap = pick(k), pick(2 + k)
        pond = jnp.zeros((DEV, 128), F32)
        for base, c, mask in sides:
            col = twice(turned(line(note_ref, k, base)))
            pond = jnp.where(mask, hot_dot(as_hot(col == lane_place + float(c)), depth), pond)
        flow = jnp.where(is_east | is_west, runoff(rain, cap, pond), 0.0)
        for base, c, mask in sides:
            hot = as_hot(line(note_ref, k, base) == place4 + float(c))
            acc = acc + hot_dot(hot, jnp.where(mask, flow, 0.0))
    here = lax.axis_index("gx")
    acc = jnp.where(is_west & (here > 0), acc, jnp.where(is_east & (here < lax.axis_size("gx") - 1), acc, 0.0))
    in_ref[4 * TR : 5 * TR, :] = acc
    for j in range(PANELS):
        up_ref[8 * j : 8 * j + 8, :] = in_ref[TR * j : TR * j + 8, :]
        down_ref[8 * j : 8 * j + 8, :] = in_ref[TR * j + TR - 8 : TR * j + TR, :]


def inflow_call(got, pond, recv, side, note):
    return pl.pallas_call(
        inflow_kernel,
        out_shape=(array(PANELS * TR, 128), array(PANELS * 8, 128), array(PANELS * 8, 128)),
        in_specs=[VMEM, HBM, ANY, HBM, HBM],
        scratch_shapes=[
            pltpu.VMEM((2 * DEV, 128), F32),
            pltpu.VMEM((8, 128), F32),
            pltpu.VMEM((TR, 128), F32),
            pltpu.VMEM((16, 128), F32),
            pltpu.SemaphoreType.DMA((4,)),
        ],
        compiler_params=params(24),
        name="inflow",
    )(got, pond, recv, side, note)


def at(i, j, shift=0):
    start = j * SPAN + 8 + 8 * i + shift
    return slice(start, start + 8)


def column_of(j, col0):
    lane = iota((8, 128), 1)
    if j < 4:
        return col0 + 128 * j + lane
    return col0 + jnp.where(lane < 64, TC + lane, lane - 128)


def east_open(j, col0):
    col = column_of(j, col0)
    return (col >= 0) & (col + 1 <= TC * lax.axis_size("gx") - 1)


def south_open(i, row0):
    row = row0 - HALO + 8 * i + iota((8, 128), 0)
    return (row >= 0) & (row + 1 <= TR * lax.axis_size(ROWS) - 1)


def shifted(values, shift, lane, offset):
    moved = [pltpu.roll(v, shift, 1) for v in values]
    edge = iota((8, 128), 1) == lane
    return [jnp.where(edge, moved[(j + offset) % PANELS], moved[j]) for j in range(PANELS)]


def run_steps(count, s_ref, qe_ref, qs_ref, mbe_ref, cre_ref, mbs_ref, crs_ref, line_ref, edge_ref, east_ref, row0, col0):
    ge = [jnp.where(east_open(j, col0), slope_coef, 0.0).astype(F32) for j in range(PANELS)]

    def flux(q, a, b, mb, cr, g):
        h = jnp.maximum(jnp.maximum(a, b) - mb, depth_floor)
        numer = q - g * (h * (b - a))
        power = jnp.exp2(jnp.log(h) * F32(-7.0 / 3.0 / 0.6931471805599453))
        return numer * pltpu.reciprocal(1.0 + cr * jnp.abs(q) * power, approx=True)

    def one_step(_, c0):
        for i in range(TILES):
            moved = shifted([s_ref[at(i, j), :] for j in range(PANELS)], 127, 127, 1)
            for j in range(PANELS):
                east_ref[at(i, j), :] = moved[j]
        for i in range(TILES):
            gs = jnp.where(south_open(i, row0), slope_coef, 0.0).astype(F32)
            for j in range(PANELS):
                p = at(i, j)
                s = s_ref[p, :]
                qe_ref[p, :] = flux(qe_ref[p, :], s, east_ref[p, :], mbe_ref[p, :], cre_ref[p, :], ge[j])
                qs_ref[p, :] = flux(qs_ref[p, :], s, s_ref[at(i, j, 1), :], mbs_ref[p, :], crs_ref[p, :], gs)
        for i in range(TILES):
            qe = [qe_ref[at(i, j), :] for j in range(PANELS)]
            west = shifted(qe, 1, 0, PANELS - 1)
            for j in range(PANELS):
                p = at(i, j)
                change = (qe[j] - west[j]) + (qs_ref[p, :] - qs_ref[at(i, j, -1), :])
                s_ref[p, :] = s_ref[p, :] - F32(time_step / cell_size) * change
            if 0 < i < TILES - 1:
                for n in range(2):
                    rows = slice(TR * n + 8 * i - 8, TR * n + 8 * i)
                    edge_ref[rows, :] = edge_ref[rows, :] + qe[3 + n]
        for j in range(4):
            for n, i in enumerate((0, TR // 8)):
                rows = slice(16 * j + 8 * n, 16 * j + 8 * n + 8)
                line_ref[rows, :] = line_ref[rows, :] + qs_ref[at(i, j), :]
        return c0

    lax.fori_loop(0, count, one_step, 0)


def first_kernel(
    after_ref, north_ref, south_ref, note_ref, mean_ref, side_any, depth_any, wet_any, bed_any, man_any, qe_any, qs_any,
    s_ref, qe_ref, qs_ref, mbe_ref, cre_ref, mbs_ref, crs_ref, line_ref, edge_ref, lat_ref,
    bed_x, man_x, depth_ref, wet_ref, east_ref, sem,
):
    own = slice(16, 16 + TR)
    pairs = [(depth_any, depth_ref), (wet_any, wet_ref)]
    targets = (s_ref, bed_x, man_x, qe_ref, qs_ref)
    for n, src in ((1, bed_any), (2, man_any), (3, qe_any), (4, qs_any)):
        for j in range(4):
            rows = slice(j * SPAN + own.start, j * SPAN + own.stop)
            pairs.append((src.at[:, 128 * j : 128 * j + 128], targets[n].at[rows, :]))
    for n in range(5):
        rows = slice(4 * SPAN + own.start, 4 * SPAN + own.stop)
        pairs.append((side_any.at[TR * n : TR * n + TR, :], targets[n].at[rows, :]))
    got = copies(sem, pairs)

    rows, cols = lax.axis_index(ROWS), lax.axis_index("gx")
    row0, col0 = rows * TR, cols * TC
    mean = mean_ref[...]
    lat = jnp.where(rows > 0, north_ref[STRIP - 8 : STRIP, :] - mean, 0.0)
    lat = lat + jnp.where(rows < lax.axis_size(ROWS) - 1, south_ref[STRIP - 8 : STRIP, :] - mean, 0.0)
    lat = lat + jnp.where(cols > 0, note_ref[7:8, :] - mean, 0.0)
    lat = lat + jnp.where(cols < lax.axis_size("gx") - 1, note_ref[15:16, :] - mean, 0.0)
    lat_ref[...] = lateral_rate * lat

    zero = jnp.zeros((8, 128), F32)
    for n, out in enumerate(targets):
        for j in range(PANELS):
            strip = slice(8 * (PANELS * n + j), 8 * (PANELS * n + j) + 8)
            out[at(0, j), :] = north_ref[strip, :]
            out[at(TILES - 1, j), :] = south_ref[strip, :]
            out[at(-1, j), :] = zero
            out[at(TILES, j), :] = zero
    line_ref[...] = jnp.zeros((64, 128), F32)
    edge_ref[...] = jnp.zeros((2 * TR, 128), F32)
    wait(got)

    open_e = east_open(3, col0)
    for i in range(TILES):
        bed = [bed_x[at(i, j), :] for j in range(PANELS)]
        man = [man_x[at(i, j), :] for j in range(PANELS)]
        bed_e, man_e = shifted(bed, 127, 127, 1), shifted(man, 127, 127, 1)
        for j in range(PANELS):
            p = at(i, j)
            mbe_ref[p, :] = jnp.maximum(bed[j], bed_e[j])
            mbs_ref[p, :] = jnp.maximum(bed[j], bed_x[at(i, j, 1), :])
            rough_e = 0.5 * (man[j] + man_e[j])
            rough_s = 0.5 * (man[j] + man_x[at(i, j, 1), :])
            cre_ref[p, :] = fric_coef * rough_e * rough_e
            crs_ref[p, :] = fric_coef * rough_s * rough_s
            if j < 4 and 0 < i < TILES - 1:
                place = (slice(8 * i - 8, 8 * i), slice(128 * j, 128 * j + 128))
                s_ref[p, :] = depth_ref[place] * wet_ref[place].astype(F32) + bed[j]
            else:
                s_ref[p, :] = s_ref[p, :] + bed[j]
        qe_ref[at(i, 3), :] = jnp.where(open_e, qe_ref[at(i, 3), :], 0.0)
    for j in range(PANELS):
        p = at(TR // 8, j)
        qs_ref[p, :] = jnp.where(south_open(TR // 8, row0), qs_ref[p, :], 0.0)

    run_steps(
        STEPS // 2, s_ref, qe_ref, qs_ref, mbe_ref, cre_ref, mbs_ref, crs_ref, line_ref, edge_ref, east_ref, row0, col0
    )


def first_call(after, north, south, note, mean, side, fields):
    ext = array(EXT, 128)
    return pl.pallas_call(
        first_kernel,
        out_shape=(ext,) * 7 + (array(64, 128), array(2 * TR, 128), array(8, 128)),
        in_specs=[ANY] + [VMEM] * 4 + [ANY] * 7,
        scratch_shapes=[
            pltpu.VMEM((EXT, 128), F32),
            pltpu.VMEM((EXT, 128), F32),
            pltpu.VMEM((TR, TC), F32),
            pltpu.VMEM((TR, TC), jnp.int32),
            pltpu.VMEM((EXT, 128), F32),
            pltpu.SemaphoreType.DMA((23,)),
        ],
        compiler_params=params(32),
        name="first_steps",
    )(after, north, south, note, mean, side, *fields)


def last_kernel(
    in_ref, north_ref, south_ref, bed_any,
    s_in, qe_in, qs_in, mbe_ref, cre_ref, mbs_ref, crs_ref, line_in, edge_in,
    depth_hbm, qe_hbm, qs_hbm, we_ref, ns_ref,
    s_ref, qe_ref, qs_ref, line_ref, edge_ref, east_ref, bed_ref, sem_in, sem,
):
    loaded = copies(sem_in, ((bed_any, bed_ref),))
    row0 = lax.axis_index(ROWS) * TR
    col0 = lax.axis_index("gx") * TC
    for j in range(PANELS):
        first, last = at(0, j), at(TILES - 1, j)
        s_ref[first, :] = s_in[first, :] + north_ref[8 * j : 8 * j + 8, :]
        s_ref[last, :] = s_in[last, :] + south_ref[8 * j : 8 * j + 8, :]
        own = slice(j * SPAN + 16, j * SPAN + 16 + TR)
        s_ref[own, :] = s_in[own, :] + in_ref[TR * j : TR * j + TR, :]
        s_ref[at(TILES, j), :] = s_in[at(TILES, j), :]
    qe_ref[...] = qe_in[...]
    qs_ref[...] = qs_in[...]
    line_ref[...] = line_in[...]
    edge_ref[...] = edge_in[...]
    run_steps(
        STEPS - STEPS // 2, s_ref, qe_ref, qs_ref, mbe_ref, cre_ref, mbs_ref, crs_ref, line_ref, edge_ref, east_ref,
        row0, col0,
    )
    pairs = []
    for src, dst in ((qe_ref, qe_hbm), (qs_ref, qs_hbm)):
        for j in range(4):
            rows = slice(j * SPAN + 16, j * SPAN + 16 + TR)
            pairs.append((src.at[rows, :], dst.at[:, 128 * j : 128 * j + 128]))
    stored = copies(sem, pairs)
    wait(loaded)
    for j in range(4):
        cols = slice(128 * j, 128 * j + 128)
        bed_ref[:, cols] = s_ref[j * SPAN + 16 : j * SPAN + 16 + TR, :] - bed_ref[:, cols]
    depth = pltpu.make_async_copy(bed_ref, depth_hbm, sem.at[8])
    depth.start()
    we_ref[0:1, :] = edge_ref[TR : 2 * TR, :].T[127:128, :]
    we_ref[1:2, :] = edge_ref[0:TR, :].T[127:128, :]
    for j in range(4):
        for n in range(2):
            row = 16 * j + 8 * n + 7
            ns_ref[n : n + 1, 128 * j : 128 * j + 128] = line_ref[row : row + 1, :]
    wait(stored)
    depth.wait()


def last_call(inflow, north, south, bed, state):
    return pl.pallas_call(
        last_kernel,
        out_shape=(array(TR, TC), array(TR, TC), array(TR, TC), array(2, TR), array(2, TC)),
        in_specs=[VMEM] * 3 + [ANY] + [VMEM] * 9,
        out_specs=(HBM, HBM, HBM, VMEM, VMEM),
        scratch_shapes=[
            pltpu.VMEM((EXT, 128), F32),
            pltpu.VMEM((EXT, 128), F32),
            pltpu.VMEM((EXT, 128), F32),
            pltpu.VMEM((64, 128), F32),
            pltpu.VMEM((2 * TR, 128), F32),
            pltpu.VMEM((EXT, 128), F32),
            pltpu.VMEM((TR, TC), F32),
            pltpu.SemaphoreType.DMA((1,)),
            pltpu.SemaphoreType.DMA((9,)),
        ],
        compiler_params=params(32),
        name="last_steps",
    )(inflow, north, south, bed, *state)


CHUNK = 32
CHUNKS = NB // CHUNK


def land_kernel(
    live_ref, got_ref, lat_ref, slot_hbm, rain_hbm, cap_hbm, soil_hbm, cond_hbm,
    out_hbm,
    slot_ref, rain_ref, cap_ref, soil_ref, cond_ref, cond_x, pond_ref, sem, sem_out,
):
    pairs = [(slot_hbm, slot_ref), (rain_hbm, rain_ref), (cap_hbm, cap_ref)]
    half = NB * 8
    for c in range(CHUNKS):
        cols = slice(c * CHUNK * 128, (c + 1) * CHUNK * 128)
        pairs.append((cond_hbm.at[:, cols], cond_ref.at[:, cols]))
        for h in range(2):
            rows = slice(h * half + c * CHUNK * 8, h * half + (c + 1) * CHUNK * 8)
            pairs.append((soil_hbm.at[rows, :], soil_ref.at[rows, :]))
    moved = copies(sem, pairs)
    live = live_ref[0]
    wait(moved[:3])
    slot = jnp.broadcast_to(slot_ref[...].astype(F32), (128, NB))
    slot = jnp.concatenate([slot, jnp.full((128, 256 - NB), -1.0, F32)], axis=1).T
    slot = twice(slot[0:NB])
    tile2 = iota((NB, DEV), 1).astype(F32) * 2.0
    pond = jnp.zeros((NB, 128), F32)
    for k in range(2):
        pond = pond + hot_dot(as_hot(slot == tile2 + float(k)), got_ref[pl.ds(4 + k, DEV, stride=K), :])
    pond_ref[...] = pond
    lat = lat_ref[...]
    sub, lane = iota((8, 128), 0), iota((8, 128), 1)
    group = range(CHUNK // 8)
    stored = []
    for c in range(CHUNKS):
        wait(moved[3 + 3 * c : 6 + 3 * c])
        for b in range(c * CHUNK, (c + 1) * CHUNK):
            cond_x[16 * b : 16 * b + 16, :] = cond_ref[:, 128 * b : 128 * b + 128].astype(F32)

        def soil_at(g, layer):
            return pl.ds((layer // 8) * half + (c * CHUNK + 8 * g) * 8 + layer % 8, 8, stride=8)

        def cond_at(g, layer):
            return cond_x[pl.ds((c * CHUNK + 8 * g) * 16 + layer, 8, stride=16), :]

        uptake, kept = [], []
        for g in group:
            blocks = slice(c * CHUNK + 8 * g, c * CHUNK + 8 * g + 8)
            rain, cap = rain_ref[blocks, :], cap_ref[blocks, :]
            wetting = rain + jnp.maximum(pond_ref[blocks, :], 0.0)
            uptake.append(cap * wetting * pltpu.reciprocal(wetting + half_rate, approx=True))
            kept.append((blocks.start + sub) * 128 + lane < live)
        ratios = [[] for _ in group]
        values = [[] for _ in group]
        above = [None for _ in group]
        cond = [cond_at(g, 0) for g in group]
        for j in range(NL):
            for g in group:
                rhs = soil_ref[soil_at(g, j), :]
                if j == 0:
                    rhs = rhs + uptake[g]
                if j >= 8:
                    rhs = rhs + lat
                center = 1.0 if j < NL - 1 else 1.0 + drainage
                if j > 0:
                    rhs = rhs + above[g] * values[g][-1]
                    center = center + (above[g] + above[g] * ratios[g][-1])
                if j < NL - 1:
                    below = cond_at(g, j + 1)
                    face = 0.5 * (cond[g] + below)
                    cond[g] = below
                    center = center + face
                r = pltpu.reciprocal(center, approx=True)
                if j < NL - 1:
                    ratios[g].append(-face * r)
                    above[g] = face
                values[g].append(rhs * r)
        x = [values[g][-1] for g in group]
        for j in range(NL - 1, -1, -1):
            for g in group:
                if j < NL - 1:
                    x[g] = values[g][j] - ratios[g][j] * x[g]
                soil_ref[soil_at(g, j), :] = jnp.where(kept[g], x[g], soil_ref[soil_at(g, j), :])
        for h in range(2):
            rows = slice(h * half + c * CHUNK * 8, h * half + (c + 1) * CHUNK * 8)
            stored.append(pltpu.make_async_copy(soil_ref.at[rows, :], out_hbm.at[rows, :], sem_out.at[2 * c + h]))
            stored[-1].start()
    wait(stored)


def land_call(live, got, lat, slot, rain, cap, soil, cond):
    return pl.pallas_call(
        land_kernel,
        out_shape=array(NB * NL, 128),
        in_specs=[SMEM, VMEM, VMEM] + [HBM] * 5,
        out_specs=HBM,
        scratch_shapes=[
            pltpu.VMEM((1, NB), jnp.int32),
            pltpu.VMEM((NB, 128), F32),
            pltpu.VMEM((NB, 128), F32),
            pltpu.VMEM((NB * NL, 128), F32),
            pltpu.VMEM((NL, LAND), BF16),
            pltpu.VMEM((NB * NL, 128), F32),
            pltpu.VMEM((NB, 128), F32),
            pltpu.SemaphoreType.DMA((3 + 3 * CHUNKS,)),
            pltpu.SemaphoreType.DMA((2 * CHUNKS,)),
        ],
        compiler_params=params(24),
        name="soil_columns",
    )(live, got, lat, slot, rain, cap, soil, cond)


def shift(first, second, axis):
    count = lax.axis_size(axis)
    ahead = [(i, i + 1) for i in range(count - 1)]
    back = [(j, i) for i, j in ahead]
    return lax.ppermute(first, axis, ahead), lax.ppermute(second, axis, back)


def local(
    soil_water, conduct, rainfall, infil_cap, live_counts, send_slot, recv_row,
    bed_height, manning, depth_in, east_in, south_in, wet_mask,
):
    rain = rainfall.reshape(NB, 128)
    cap = infil_cap.reshape(NB, 128)
    soil = soil_water.reshape(2, 8, NB, 128).transpose(0, 2, 1, 3).reshape(NB * NL, 128)
    fields = (depth_in, wet_mask, bed_height, manning, east_in, south_in)

    sent, pond, recv = send_call(live_counts, send_slot, recv_row, rain, cap, depth_in, wet_mask)
    got = lax.all_to_all(sent.reshape(DEV, 1, K * 128), ALL, split_axis=0, concat_axis=0, tiled=True)
    got = got.reshape(DEV * K, 128)

    to_west, to_east, mean = cols_call(live_counts, recv, soil, fields)
    west, east = shift(to_east, to_west, "gx")
    up, down, side, note = rows_call(west, east, mean, fields)
    north, south = shift(down, up, ROWS)

    inflow, in_up, in_down = inflow_call(got, pond, recv, side, note)
    in_north, in_south = shift(in_down, in_up, ROWS)
    *state, lat = first_call(in_up, north, south, note, mean, side, fields)
    soil_out = land_call(live_counts, got, lat, send_slot, rain, cap, soil, conduct)
    depth, east_q, south_q, edge_we, edge_ns = last_call(inflow, in_north, in_south, bed_height, state)
    soil_out = soil_out.reshape(2, NB, 8, 128).transpose(0, 2, 1, 3).reshape(NL, LAND)
    return soil_out, depth, east_q, south_q, edge_we, edge_ns


def solution(mesh):
    placed = (
        P(None, ALL),
        P(None, ALL),
        P(ALL),
        P(ALL),
        P(ALL),
        P(ALL, None),
        P(ALL, None),
    ) + (P(ROWS, "gx"),) * 6
    return jax.shard_map(
        local,
        mesh=mesh,
        in_specs=placed,
        out_specs=(
            P(None, ALL),
            P(ROWS, "gx"),
            P(ROWS, "gx"),
            P(ROWS, "gx"),
            P("gx", ROWS),
            P(ROWS, "gx"),
        ),
        check_vma=False,
    )
```

```python
import jax
import jax.numpy as jnp
from jax import lax
from jax.experimental import pallas as pl
from jax.experimental.pallas import tpu as pltpu
from jax.sharding import PartitionSpec as P

F32 = jnp.float32
BF16 = jnp.bfloat16

NL = 16
STEPS = 8
TR = 256
TC = 512
NB = 192
LAND = NB * 128
DEV = 256
HALO = 8
K = 7
PANELS = 5
SPAN = TR + 16
EXT = PANELS * SPAN
BAND = 32
BANDS = 2 * PANELS * BAND
STRIP = 5 * PANELS * 8 + 8
PREP = 2 * DEV + TR + 16 + 8
FULL = 63

gravity = 9.81
cell_size = 30.0
time_step = 2.5
depth_floor = 0.25
half_rate = 0.5
lateral_rate = 0.2
drainage = 0.05
slope_coef = gravity * time_step / cell_size
fric_coef = gravity * time_step

ROWS = ("grp", "gy")
ALL = ("grp", "gy", "gx")
VMEM = pl.BlockSpec(memory_space=pltpu.VMEM)
SMEM = pl.BlockSpec(memory_space=pltpu.SMEM)
HBM = pl.BlockSpec(memory_space=pltpu.HBM)
ANY = pl.BlockSpec(memory_space=pl.ANY)


def params(mib):
    return pltpu.CompilerParams(vmem_limit_bytes=mib * 1024 * 1024)


def array(*shape):
    return jax.ShapeDtypeStruct(shape, F32)


def iota(shape, dim):
    return lax.broadcasted_iota(jnp.int32, shape, dim)


def copies(sem, pairs):
    made = [pltpu.make_async_copy(src, dst, sem.at[n]) for n, (src, dst) in enumerate(pairs)]
    for c in made:
        c.start()
    return made


def wait(made):
    for c in made:
        c.wait()


def parts(x):
    high = x.astype(BF16)
    low = (x - high.astype(F32)).astype(BF16)
    return high, low


def hot_dot(hot, x):
    both = jnp.dot(hot, jnp.concatenate(parts(x), axis=1), preferred_element_type=F32)
    return both[:, :128] + both[:, 128:]


def as_hot(mask):
    return mask.astype(F32).astype(BF16)


def twice(col):
    return jnp.concatenate([col, col], axis=1)


def turned(row):
    return jnp.broadcast_to(row, (128, row.shape[1])).T


def send_kernel(
    live_ref, slot_hbm, recv_hbm, rain_hbm, cap_hbm, depth_hbm, wet_hbm,
    out_hbm, pond_hbm, recv_out,
    slot_ref, recv_ref, rain_ref, cap_ref, depth_ref, wet_ref, out_ref, pond_ref, tmp_ref, sem, sem_out,
):
    got = copies(
        sem,
        (
            (slot_hbm, slot_ref), (rain_hbm, rain_ref), (cap_hbm, cap_ref),
            (recv_hbm, recv_ref), (depth_hbm, depth_ref), (wet_hbm, wet_ref),
        ),
    )
    live = live_ref[0]
    wait(got[:3])
    cell = iota((NB, 128), 0) * 128 + iota((NB, 128), 1)
    rain = jnp.where(cell < live, rain_ref[...], 0.0)
    rhs = jnp.concatenate(parts(rain) + parts(cap_ref[...]), axis=1)
    slot = slot_ref[...]
    tile = iota((DEV, NB), 0)
    lane = iota((DEV, 128), 1)
    for_west = jnp.zeros((DEV, 128), F32)
    for_east = jnp.zeros((DEV, 128), F32)
    for k in range(2):
        res = jnp.dot(as_hot(slot == 2 * tile + k), rhs, preferred_element_type=F32)
        for a in range(2):
            block = res[:, 256 * a : 256 * a + 128] + res[:, 256 * a + 128 : 256 * a + 256]
            out_ref[pl.ds(2 * a + k, DEV, stride=K), :] = block
            g = 2 * a + k
            low, high = 124 - 8 * g, 8 * g
            moved_w = pltpu.roll(block, (128 - 8 * g) % 128, 1) if g else block
            moved_e = pltpu.roll(block, 8 * g, 1) if g else block
            for_west = jnp.where((lane >= low) & (lane < low + 4), moved_w, for_west)
            for_east = jnp.where((lane >= high) & (lane < high + 4), moved_e, for_east)
    edge = jnp.where(lane < 64, pltpu.roll(for_east, DEV - 1, 0), pltpu.roll(for_west, 1, 0))
    out_ref[pl.ds(6, DEV, stride=K), :] = edge
    wait(got[3:])
    tmp_ref[...] = turned(recv_ref[...].astype(F32))
    fields = []
    for c in range(4):
        cols = slice(128 * c, 128 * c + 128)
        fields.append(jnp.concatenate(parts(depth_ref[:, cols] * wet_ref[:, cols].astype(F32)), axis=1))
    place4 = iota((DEV, 256), 1).astype(F32) * 4.0
    recv_out[4:8, :] = jnp.zeros((4, 128), F32)
    for k in range(2):
        col = tmp_ref[pl.ds(k, DEV, stride=2), :]
        recv_out[2 * k : 2 * k + 1, :] = col[:128].T[0:1]
        recv_out[2 * k + 1 : 2 * k + 2, :] = col[128:].T[0:1]
        wide = twice(col)
        acc = jnp.zeros((DEV, 256), F32)
        for c in range(4):
            acc = acc + jnp.dot(as_hot(wide == place4 + float(c)), fields[c], preferred_element_type=F32)
        pond = acc[:, :128] + acc[:, 128:]
        out_ref[pl.ds(4 + k, DEV, stride=K), :] = pond
        pond_ref[DEV * k : DEV * k + DEV, :] = pond
    wait(copies(sem_out, ((out_ref, out_hbm), (pond_ref, pond_hbm))))


def send_call(live, slot, recv, rain, cap, depth, wet):
    return pl.pallas_call(
        send_kernel,
        out_shape=(array(DEV * K, 128), array(2 * DEV, 128), array(8, 128)),
        in_specs=[SMEM] + [HBM] * 6,
        out_specs=(HBM, HBM, VMEM),
        scratch_shapes=[
            pltpu.VMEM((1, NB), jnp.int32),
            pltpu.VMEM((1, 2 * DEV), jnp.int32),
            pltpu.VMEM((NB, 128), F32),
            pltpu.VMEM((NB, 128), F32),
            pltpu.VMEM((TR, TC), F32),
            pltpu.VMEM((TR, TC), jnp.int32),
            pltpu.VMEM((DEV * K, 128), F32),
            pltpu.VMEM((2 * DEV, 128), F32),
            pltpu.VMEM((2 * DEV, 128), F32),
            pltpu.SemaphoreType.DMA((6,)),
            pltpu.SemaphoreType.DMA((2,)),
        ],
        compiler_params=params(FULL),
        name="message",
    )(live, slot, recv, rain, cap, depth, wet)


def cols_kernel(
    live_ref, recv_ref, soil_hbm, depth, wet, bed, man, qe, qs,
    to_west, to_east, mean_ref,
    soil_ref, west_ref, east_ref, wet_w, wet_e, sem,
):
    left, right = slice(0, 128), slice(TC - 128, TC)
    pairs = [(wet.at[:, left], wet_w), (wet.at[:, right], wet_e)]
    for n, f in enumerate((depth, bed, man, qe, qs)):
        rows = slice(TR * n, TR * n + TR)
        pairs.append((f.at[:, left], west_ref.at[rows, :]))
        pairs.append((f.at[:, right], east_ref.at[rows, :]))
    pairs.append((soil_hbm.at[NB * 8 : NB * 16, :], soil_ref))
    got = copies(sem, pairs)
    wait(got[:-1])
    lane = iota((TR, 128), 1)
    for src, mask, out, first in ((west_ref, wet_w, to_west, 0), (east_ref, wet_e, to_east, 120)):
        acc = jnp.zeros((TR, 128), F32)
        for n in range(5):
            own = src[TR * n : TR * n + TR, :]
            if n == 0:
                own = own * mask[...].astype(F32)
            shift = (8 * n - first) % 128
            moved = pltpu.roll(own, shift, 1) if shift else own
            acc = jnp.where((lane >= 8 * n) & (lane < 8 * n + 8), moved, acc)
        out[0:TR, :] = acc
    live = live_ref[0]
    half = NB * 8
    wait(got[-1:])
    which = iota((half, 128), 0) // 8 * 128 + iota((half, 128), 1)
    kept = jnp.where(which < live, soil_ref[...], 0.0)
    total = jnp.sum(kept.reshape(half // 8, 8, 128), axis=0)
    mean = jnp.sum(total) / (live.astype(F32) * 8.0)
    row = jnp.full((8, 128), mean, F32)
    mean_ref[...] = row
    tail = jnp.where(iota((8, 128), 0) < 4, recv_ref[...], row)
    to_west[TR : TR + 8, :] = tail
    to_east[TR : TR + 8, :] = tail


def cols_call(live, recv, soil, fields):
    return pl.pallas_call(
        cols_kernel,
        out_shape=(array(TR + 8, 128), array(TR + 8, 128), array(8, 128)),
        in_specs=[SMEM, VMEM] + [HBM] * 7,
        scratch_shapes=[
            pltpu.VMEM((NB * 8, 128), F32),
            pltpu.VMEM((5 * TR, 128), F32),
            pltpu.VMEM((5 * TR, 128), F32),
            pltpu.VMEM((TR, 128), jnp.int32),
            pltpu.VMEM((TR, 128), jnp.int32),
            pltpu.SemaphoreType.DMA((13,)),
        ],
        compiler_params=params(FULL),
        name="column_strips",
    )(live, recv, soil, *fields)


def rows_kernel(
    west_hbm, east_hbm, mean_hbm, recv_hbm, pond_hbm, depth, wet, bed, man, qe, qs,
    up_hbm, down_hbm, side_hbm, prep_hbm,
    west_ref, east_ref, mean_ref, top_ref, bottom_ref, wet_t, wet_b, side_ref, prep_ref, up_ref, down_ref, sem, sem_out,
):
    first, last = slice(0, 8), slice(TR - 8, TR)
    pairs = [
        (west_hbm, west_ref), (east_hbm, east_ref), (mean_hbm, mean_ref),
        (wet.at[first, :], wet_t), (wet.at[last, :], wet_b),
    ]
    for n, f in enumerate((depth, bed, man, qe, qs)):
        rows = slice(8 * n, 8 * n + 8)
        pairs.append((f.at[first, :], top_ref.at[rows, :]))
        pairs.append((f.at[last, :], bottom_ref.at[rows, :]))
    pairs.append((pond_hbm, prep_ref.at[0 : 2 * DEV, :]))
    pairs.append((recv_hbm, prep_ref.at[PREP - 8 : PREP, :]))
    got = copies(sem, pairs)
    wait(got[:2])
    lane = iota((TR, 128), 1)
    for n in range(5):
        shift = (128 - 8 * n) % 128
        e, w = east_ref[0:TR, :], west_ref[0:TR, :]
        e = pltpu.roll(e, shift, 1) if shift else e
        w = pltpu.roll(w, 120 - 8 * n, 1)
        side_ref[TR * n : TR * n + TR, :] = jnp.where(lane < 8, e, jnp.where(lane >= 120, w, 0.0))
    stored = copies(sem_out, ((side_ref, side_hbm),))
    at = 2 * DEV
    prep_ref[at : at + TR, :] = side_ref[0:TR, :]
    prep_ref[at + TR : at + TR + 8, :] = west_ref[TR : TR + 8, :]
    prep_ref[at + TR + 8 : at + TR + 16, :] = east_ref[TR : TR + 8, :]
    wait(got[2:])
    for src, mask, out, at in ((top_ref, wet_t, up_ref, 0), (bottom_ref, wet_b, down_ref, TR - 8)):
        for n in range(5):
            for j in range(PANELS):
                to = slice(8 * (PANELS * n + j), 8 * (PANELS * n + j) + 8)
                if j < 4:
                    cols = slice(128 * j, 128 * j + 128)
                    own = src[8 * n : 8 * n + 8, cols]
                    if n == 0:
                        own = own * mask[:, cols].astype(F32)
                    out[to, :] = own
                else:
                    out[to, :] = side_ref[TR * n + at : TR * n + at + 8, :]
        out[STRIP - 8 : STRIP, :] = mean_ref[...]
    outs = ((up_ref, up_hbm, 1), (down_ref, down_hbm, 2), (prep_ref, prep_hbm, 3))
    for src, dst, n in outs:
        stored.append(pltpu.make_async_copy(src, dst, sem_out.at[n]))
        stored[-1].start()
    wait(stored)


def rows_call(west, east, mean, recv, pond, fields):
    return pl.pallas_call(
        rows_kernel,
        out_shape=(array(STRIP, 128), array(STRIP, 128), array(5 * TR, 128), array(PREP, 128)),
        in_specs=[HBM] * 11,
        out_specs=(HBM,) * 4,
        scratch_shapes=[
            pltpu.VMEM((TR + 8, 128), F32),
            pltpu.VMEM((TR + 8, 128), F32),
            pltpu.VMEM((8, 128), F32),
            pltpu.VMEM((40, TC), F32),
            pltpu.VMEM((40, TC), F32),
            pltpu.VMEM((8, TC), jnp.int32),
            pltpu.VMEM((8, TC), jnp.int32),
            pltpu.VMEM((5 * TR, 128), F32),
            pltpu.VMEM((PREP, 128), F32),
            pltpu.VMEM((STRIP, 128), F32),
            pltpu.VMEM((STRIP, 128), F32),
            pltpu.SemaphoreType.DMA((17,)),
            pltpu.SemaphoreType.DMA((4,)),
        ],
        compiler_params=params(FULL),
        name="row_strips",
    )(west, east, mean, recv, pond, *fields)


def inflow_kernel(
    after_any, got_ref, prep_hbm,
    in_hbm, up_ref, down_ref,
    prep_ref, in_ref, sem, sem_out,
):
    moved = copies(sem, ((prep_hbm, prep_ref),))
    lane = iota((DEV, 128), 1)
    place4 = iota((TR, DEV), 0).astype(F32) * 4.0

    def runoff(rain, cap, pond):
        wetting = rain + jnp.maximum(pond, 0.0)
        return rain * (1.0 - cap / (wetting + half_rate))

    def line(k, base):
        at = base + 2 * k
        return jnp.concatenate([prep_ref[at : at + 1, :], prep_ref[at + 1 : at + 2, :]], axis=1)

    note, own = 2 * DEV + TR, PREP - 8
    wait(moved)
    flows = []
    for k in range(2):
        rain = got_ref[pl.ds(k, DEV, stride=K), :]
        cap = got_ref[pl.ds(2 + k, DEV, stride=K), :]
        flow = runoff(rain, cap, prep_ref[DEV * k : DEV * k + DEV, :])
        flows.append(jnp.concatenate(parts(flow), axis=1))
    for c in range(4):
        acc = jnp.zeros((TR, 256), F32)
        for k in range(2):
            hot = as_hot(line(k, own) == place4 + float(c))
            acc = acc + jnp.dot(hot, flows[k], preferred_element_type=F32)
        in_ref[TR * c : TR * c + TR, :] = acc[:, :128] + acc[:, 128:]
    own_rows = slice(0, 4 * TR)
    stored = copies(sem_out, ((in_ref.at[own_rows, :], in_hbm.at[own_rows, :]),))

    edge = got_ref[pl.ds(6, DEV, stride=K), :]
    depth = prep_ref[2 * DEV : 2 * DEV + TR, :]
    lane_place = iota((DEV, TR), 1).astype(F32) * 4.0
    is_east, is_west = lane < 4, lane >= 124
    acc = jnp.zeros((TR, 128), F32)

    def pick(g):
        if g == 0:
            return edge
        return jnp.where(lane < 64, pltpu.roll(edge, 128 - 8 * g, 1), pltpu.roll(edge, 8 * g, 1))

    sides = ((note, 3, is_west), (note + 8, 0, is_east))
    for k in range(2):
        rain, cap = pick(k), pick(2 + k)
        pond = jnp.zeros((DEV, 128), F32)
        for base, c, mask in sides:
            col = twice(turned(line(k, base)))
            pond = jnp.where(mask, hot_dot(as_hot(col == lane_place + float(c)), depth), pond)
        flow = jnp.where(is_east | is_west, runoff(rain, cap, pond), 0.0)
        for base, c, mask in sides:
            hot = as_hot(line(k, base) == place4 + float(c))
            acc = acc + hot_dot(hot, jnp.where(mask, flow, 0.0))
    here = lax.axis_index("gx")
    acc = jnp.where(is_west & (here > 0), acc, jnp.where(is_east & (here < lax.axis_size("gx") - 1), acc, 0.0))
    side_rows = slice(4 * TR, 5 * TR)
    in_ref[side_rows, :] = acc
    stored.append(pltpu.make_async_copy(in_ref.at[side_rows, :], in_hbm.at[side_rows, :], sem_out.at[1]))
    stored[-1].start()
    for j in range(PANELS):
        up_ref[8 * j : 8 * j + 8, :] = in_ref[TR * j : TR * j + 8, :]
        down_ref[8 * j : 8 * j + 8, :] = in_ref[TR * j + TR - 8 : TR * j + TR, :]
    wait(stored)


def inflow_call(after, got, prep):
    return pl.pallas_call(
        inflow_kernel,
        out_shape=(array(PANELS * TR, 128), array(PANELS * 8, 128), array(PANELS * 8, 128)),
        in_specs=[ANY, VMEM, HBM],
        out_specs=(HBM, VMEM, VMEM),
        scratch_shapes=[
            pltpu.VMEM((PREP, 128), F32),
            pltpu.VMEM((PANELS * TR, 128), F32),
            pltpu.SemaphoreType.DMA((1,)),
            pltpu.SemaphoreType.DMA((2,)),
        ],
        compiler_params=pltpu.CompilerParams(vmem_limit_bytes=60 * 1024 * 1024),
        name="inflow",
    )(after, got, prep)


class Grid:
    def __init__(self, bases, tiles, rows):
        self.bases, self.tiles, self.rows = bases, tiles, rows
        self.all = [(g, i) for g in range(len(bases)) for i in range(tiles)]

    def at(self, g, i, j, shift=0):
        start = self.bases[g][j] + 8 + 8 * i + shift
        return slice(start, start + 8)

    def south_open(self, g, i, row0):
        row = row0 + self.rows[g] + 8 * i + iota((8, 128), 0)
        return (row >= 0) & (row + 1 <= TR * lax.axis_size(ROWS) - 1)


BULK = Grid([[j * SPAN for j in range(PANELS)]], TR // 8, [0])
EDGES = Grid([[(PANELS * g + j) * BAND for j in range(PANELS)] for g in range(2)], 2, [-8, TR - 8])


def east_open(j, col0):
    lane = iota((8, 128), 1)
    if j < 4:
        col = col0 + 128 * j + lane
    else:
        col = col0 + jnp.where(lane < 64, TC + lane, lane - 128)
    return (col >= 0) & (col + 1 <= TC * lax.axis_size("gx") - 1)


def shifted(values, shift, lane, offset):
    moved = [pltpu.roll(v, shift, 1) for v in values]
    edge = iota((8, 128), 1) == lane
    return [jnp.where(edge, moved[(j + offset) % PANELS], moved[j]) for j in range(PANELS)]


def run_steps(count, grid, state, consts, east_ref, row0, col0, after):
    s_ref, qe_ref, qs_ref = state
    mbe_ref, cre_ref, mbs_ref, crs_ref = consts
    ge = [jnp.where(east_open(j, col0), slope_coef, 0.0).astype(F32) for j in range(PANELS)]

    def flux(q, a, b, mb, cr, g):
        h = jnp.maximum(jnp.maximum(a, b) - mb, depth_floor)
        numer = q - g * (h * (b - a))
        power = jnp.exp2(jnp.log(h) * F32(-7.0 / 3.0 / 0.6931471805599453))
        return numer * pltpu.reciprocal(1.0 + cr * jnp.abs(q) * power, approx=True)

    def one_step(_, c0):
        for g, i in grid.all:
            moved = shifted([s_ref[grid.at(g, i, j), :] for j in range(PANELS)], 127, 127, 1)
            for j in range(PANELS):
                east_ref[grid.at(g, i, j), :] = moved[j]
        for g, i in grid.all:
            gs = jnp.where(grid.south_open(g, i, row0), slope_coef, 0.0).astype(F32)
            for j in range(PANELS):
                p = grid.at(g, i, j)
                s = s_ref[p, :]
                qe_ref[p, :] = flux(qe_ref[p, :], s, east_ref[p, :], mbe_ref[p, :], cre_ref[p, :], ge[j])
                qs_ref[p, :] = flux(qs_ref[p, :], s, s_ref[grid.at(g, i, j, 1), :], mbs_ref[p, :], crs_ref[p, :], gs)
        for g, i in grid.all:
            qe = [qe_ref[grid.at(g, i, j), :] for j in range(PANELS)]
            west = shifted(qe, 1, 0, PANELS - 1)
            for j in range(PANELS):
                p = grid.at(g, i, j)
                change = (qe[j] - west[j]) + (qs_ref[p, :] - qs_ref[grid.at(g, i, j, -1), :])
                s_ref[p, :] = s_ref[p, :] - F32(time_step / cell_size) * change
            after(g, i, qe)
        return c0

    lax.fori_loop(0, count, one_step, 0)


def set_up(grid, state, consts, bed_ref, man_ref, row0, col0):
    s_ref, qe_ref, qs_ref = state
    mbe_ref, cre_ref, mbs_ref, crs_ref = consts
    open_e = east_open(3, col0)
    for g, i in grid.all:
        bed = [bed_ref[grid.at(g, i, j), :] for j in range(PANELS)]
        man = [man_ref[grid.at(g, i, j), :] for j in range(PANELS)]
        bed_e, man_e = shifted(bed, 127, 127, 1), shifted(man, 127, 127, 1)
        for j in range(PANELS):
            p = grid.at(g, i, j)
            mbe_ref[p, :] = jnp.maximum(bed[j], bed_e[j])
            mbs_ref[p, :] = jnp.maximum(bed[j], bed_ref[grid.at(g, i, j, 1), :])
            rough_e = 0.5 * (man[j] + man_e[j])
            rough_s = 0.5 * (man[j] + man_ref[grid.at(g, i, j, 1), :])
            cre_ref[p, :] = fric_coef * rough_e * rough_e
            crs_ref[p, :] = fric_coef * rough_s * rough_s
            s_ref[p, :] = s_ref[p, :] + bed[j]
        qe_ref[grid.at(g, i, 3), :] = jnp.where(open_e, qe_ref[grid.at(g, i, 3), :], 0.0)
        if grid.rows[g] + 8 * i == TR - 8:
            for j in range(PANELS):
                p = grid.at(g, i, j)
                qs_ref[p, :] = jnp.where(grid.south_open(g, i, row0), qs_ref[p, :], 0.0)


def clear_guards(grid, refs):
    zero = jnp.zeros((8, 128), F32)
    for ref in refs:
        for g in range(len(grid.bases)):
            for j in range(PANELS):
                ref[grid.at(g, -1, j), :] = zero
                ref[grid.at(g, grid.tiles, j), :] = zero


def place():
    return lax.axis_index(ROWS) * TR, lax.axis_index("gx") * TC


def add_bulk_edges(edge_ref):
    def after(g, i, qe):
        for n in range(2):
            rows = slice(TR * n + 8 * i, TR * n + 8 * i + 8)
            edge_ref[rows, :] = edge_ref[rows, :] + qe[3 + n]

    return after


def add_band_edges(sum_ref, qs_ref):
    def after(g, i, qe):
        if EDGES.rows[g] + 8 * i in (0, TR - 8):
            for n in range(2):
                rows = slice(16 * g + 8 * n, 16 * g + 8 * n + 8)
                sum_ref[rows, :] = sum_ref[rows, :] + qe[3 + n]
        if i == 0:
            for j in range(4):
                rows = slice(32 + 8 * (4 * g + j), 40 + 8 * (4 * g + j))
                sum_ref[rows, :] = sum_ref[rows, :] + qs_ref[EDGES.at(g, 0, j), :]

    return after


SUMS = 32 + 64


def first_kernel(
    side_hbm, depth_hbm, wet_hbm, bed_hbm, man_hbm, qe_hbm, qs_hbm,
    s_out, qe_out, qs_out, mbe_out, cre_out, mbs_out, crs_out, edge_out,
    s_ref, qe_ref, qs_ref, mbe_ref, cre_ref, mbs_ref, crs_ref, edge_ref, bed_x, man_x, wet_ref, east_ref, sem, sem_out,
):
    pairs = [(wet_hbm, wet_ref)]
    targets = (s_ref, bed_x, man_x, qe_ref, qs_ref)
    for n, src in enumerate((depth_hbm, bed_hbm, man_hbm, qe_hbm, qs_hbm)):
        for j in range(PANELS):
            to = targets[n].at[j * SPAN + 8 : j * SPAN + 8 + TR, :]
            if j < 4:
                pairs.append((src.at[:, 128 * j : 128 * j + 128], to))
            else:
                pairs.append((side_hbm.at[TR * n : TR * n + TR, :], to))
    got = copies(sem, pairs)
    row0, col0 = place()
    state, consts = (s_ref, qe_ref, qs_ref), (mbe_ref, cre_ref, mbs_ref, crs_ref)
    clear_guards(BULK, targets + consts)
    edge_ref[...] = jnp.zeros((2 * TR, 128), F32)
    wait(got)
    for j in range(4):
        own = slice(j * SPAN + 8, j * SPAN + 8 + TR)
        s_ref[own, :] = s_ref[own, :] * wet_ref[:, 128 * j : 128 * j + 128].astype(F32)
    set_up(BULK, state, consts, bed_x, man_x, row0, col0)
    stored = copies(sem_out, list(zip(consts, (mbe_out, cre_out, mbs_out, crs_out))))
    run_steps(STEPS // 2, BULK, state, consts, east_ref, row0, col0, add_bulk_edges(edge_ref))
    for n, (src, dst) in enumerate(zip(state + (edge_ref,), (s_out, qe_out, qs_out, edge_out))):
        stored.append(pltpu.make_async_copy(src, dst, sem_out.at[4 + n]))
        stored[-1].start()
    wait(stored)


def first_call(side, fields):
    ext = array(EXT, 128)
    buffer = pltpu.VMEM((EXT, 128), F32)
    return pl.pallas_call(
        first_kernel,
        out_shape=(ext,) * 7 + (array(2 * TR, 128),),
        in_specs=[HBM] * 7,
        out_specs=(HBM,) * 8,
        scratch_shapes=[buffer] * 7
        + [pltpu.VMEM((2 * TR, 128), F32), buffer, buffer, pltpu.VMEM((TR, TC), jnp.int32), buffer]
        + [pltpu.SemaphoreType.DMA((26,)), pltpu.SemaphoreType.DMA((8,))],
        compiler_params=params(FULL),
        name="first_steps",
    )(side, *fields)


CHUNK = 32
CHUNKS = NB // CHUNK


def land_copies(soil_hbm, cond_hbm, soil_ref, cond_ref):
    pairs = []
    half = NB * 8
    for c in range(CHUNKS):
        cols = slice(c * CHUNK * 128, (c + 1) * CHUNK * 128)
        pairs.append((cond_hbm.at[:, cols], cond_ref.at[:, cols]))
        for h in range(2):
            rows = slice(h * half + c * CHUNK * 8, h * half + (c + 1) * CHUNK * 8)
            pairs.append((soil_hbm.at[rows, :], soil_ref.at[rows, :]))
    return pairs


def land_part(
    live, moved, got_ref, north_ref, south_ref, mean_ref, note_ref, slot_ref, rain_ref, cap_ref, soil_ref, cond_ref,
    out_hbm, cond_x, pond_ref, sem_out,
):
    half = NB * 8
    slot = jnp.broadcast_to(slot_ref[...].astype(F32), (128, NB))
    slot = jnp.concatenate([slot, jnp.full((128, 256 - NB), -1.0, F32)], axis=1).T
    slot = twice(slot[0:NB])
    tile2 = iota((NB, DEV), 1).astype(F32) * 2.0
    pond = jnp.zeros((NB, 128), F32)
    for k in range(2):
        pond = pond + hot_dot(as_hot(slot == tile2 + float(k)), got_ref[pl.ds(4 + k, DEV, stride=K), :])
    pond_ref[...] = pond
    rows, cols = lax.axis_index(ROWS), lax.axis_index("gx")
    mean = mean_ref[...]
    lat = jnp.where(rows > 0, north_ref[STRIP - 8 : STRIP, :] - mean, 0.0)
    lat = lat + jnp.where(rows < lax.axis_size(ROWS) - 1, south_ref[STRIP - 8 : STRIP, :] - mean, 0.0)
    lat = lat + jnp.where(cols > 0, note_ref[7:8, :] - mean, 0.0)
    lat = lat + jnp.where(cols < lax.axis_size("gx") - 1, note_ref[15:16, :] - mean, 0.0)
    lat = lateral_rate * lat
    sub, lane = iota((8, 128), 0), iota((8, 128), 1)
    group = range(CHUNK // 8)
    stored = []
    for c in range(CHUNKS):
        wait(moved[3 * c : 3 * c + 3])
        for b in range(c * CHUNK, (c + 1) * CHUNK):
            cond_x[16 * b : 16 * b + 16, :] = cond_ref[:, 128 * b : 128 * b + 128].astype(F32)

        def soil_at(g, layer):
            return pl.ds((layer // 8) * half + (c * CHUNK + 8 * g) * 8 + layer % 8, 8, stride=8)

        def cond_at(g, layer):
            return cond_x[pl.ds((c * CHUNK + 8 * g) * 16 + layer, 8, stride=16), :]

        uptake, kept = [], []
        for g in group:
            blocks = slice(c * CHUNK + 8 * g, c * CHUNK + 8 * g + 8)
            rain, cap = rain_ref[blocks, :], cap_ref[blocks, :]
            wetting = rain + jnp.maximum(pond_ref[blocks, :], 0.0)
            uptake.append(cap * wetting * pltpu.reciprocal(wetting + half_rate, approx=True))
            kept.append((blocks.start + sub) * 128 + lane < live)
        ratios = [[] for _ in group]
        values = [[] for _ in group]
        above = [None for _ in group]
        cond = [cond_at(g, 0) for g in group]
        for j in range(NL):
            for g in group:
                rhs = soil_ref[soil_at(g, j), :]
                if j == 0:
                    rhs = rhs + uptake[g]
                if j >= 8:
                    rhs = rhs + lat
                center = 1.0 if j < NL - 1 else 1.0 + drainage
                if j > 0:
                    rhs = rhs + above[g] * values[g][-1]
                    center = center + (above[g] + above[g] * ratios[g][-1])
                if j < NL - 1:
                    below = cond_at(g, j + 1)
                    face = 0.5 * (cond[g] + below)
                    cond[g] = below
                    center = center + face
                r = pltpu.reciprocal(center, approx=True)
                if j < NL - 1:
                    ratios[g].append(-face * r)
                    above[g] = face
                values[g].append(rhs * r)
        x = [values[g][-1] for g in group]
        for j in range(NL - 1, -1, -1):
            for g in group:
                if j < NL - 1:
                    x[g] = values[g][j] - ratios[g][j] * x[g]
                soil_ref[soil_at(g, j), :] = jnp.where(kept[g], x[g], soil_ref[soil_at(g, j), :])
        for h in range(2):
            rows = slice(h * half + c * CHUNK * 8, h * half + (c + 1) * CHUNK * 8)
            stored.append(pltpu.make_async_copy(soil_ref.at[rows, :], out_hbm.at[rows, :], sem_out.at[2 * c + h]))
            stored[-1].start()
    return stored


LEFT = 8 * BANDS + SUMS + 2 * TR + 192


def middle_kernel(
    live_ref, north_hbm, south_hbm, up_hbm, down_hbm, in_hbm,
    s_in, qe_in, qs_in, mbe_in, cre_in, mbs_in, crs_in, edge_in, bed_hbm,
    got_hbm, mean_hbm, prep_hbm, slot_hbm, rain_hbm, cap_hbm, soil_hbm, cond_hbm,
    depth_hbm, qe_hbm, qs_hbm, left_hbm, soil_out,
    north_ref, south_ref, up_ref, down_ref, in_ref,
    s_ref, qe_ref, qs_ref, mbe_ref, cre_ref, mbs_ref, crs_ref, bed_ref,
    got_ref, mean_ref, note_ref, slot_ref, rain_ref, cap_ref, soil_ref, cond_ref, cond_x, pond_ref,
    left_ref, bman, beast, east_ref, sem, sem_state, sem_land, sem_soil, sem_tiles, sem_left, sem_out,
):
    strips = copies(sem, ((north_hbm, north_ref), (south_hbm, south_ref), (up_hbm, up_ref), (down_hbm, down_ref)))
    state, consts = (s_ref, qe_ref, qs_ref), (mbe_ref, cre_ref, mbs_ref, crs_ref)
    top = 8 * BANDS + SUMS
    edge_ref = left_ref.at[top : top + 2 * TR, :]
    own_ref = left_ref.at[top + 2 * TR : LEFT, :]
    sources = (s_in, qe_in, qs_in, mbe_in, cre_in, mbs_in, crs_in, in_hbm, edge_in, bed_hbm)
    loaded = copies(sem_state, list(zip(sources, state + consts + (in_ref, edge_ref, bed_ref))))
    note = 2 * DEV + TR
    land = copies(
        sem_land,
        (
            (slot_hbm, slot_ref), (rain_hbm, rain_ref), (cap_hbm, cap_ref), (mean_hbm, mean_ref),
            (prep_hbm.at[note : note + 16, :], note_ref), (got_hbm, got_ref),
        ),
    )
    soil = copies(sem_soil, land_copies(soil_hbm, cond_hbm, soil_ref, cond_ref))

    row0, col0 = place()
    bs_ref, bqe_ref, bqs_ref, bmbe, bcre, bmbs, bcrs, bbed = (
        left_ref.at[BANDS * n : BANDS * n + BANDS, :] for n in range(8)
    )
    sum_ref = left_ref.at[8 * BANDS : 8 * BANDS + SUMS, :]
    band, band_consts = (bs_ref, bqe_ref, bqs_ref), (bmbe, bcre, bmbs, bcrs)
    targets = (bs_ref, bbed, bman, bqe_ref, bqs_ref)
    clear_guards(EDGES, targets + band_consts)
    sum_ref[...] = jnp.zeros((SUMS, 128), F32)
    wait(strips)
    for n, out in enumerate(targets):
        for j in range(PANELS):
            strip = slice(8 * (PANELS * n + j), 8 * (PANELS * n + j) + 8)
            out[EDGES.at(0, 0, j), :] = north_ref[strip, :]
            out[EDGES.at(0, 1, j), :] = up_ref[strip, :]
            out[EDGES.at(1, 0, j), :] = down_ref[strip, :]
            out[EDGES.at(1, 1, j), :] = south_ref[strip, :]
    set_up(EDGES, band, band_consts, bbed, bman, row0, col0)
    run_steps(STEPS // 2, EDGES, band, band_consts, beast, row0, col0, add_band_edges(sum_ref, bqs_ref))

    wait(loaded)
    half = iota((8, 128), 0) < 4
    for j in range(PANELS):
        for big, small in zip(state, band):
            p, b = BULK.at(0, 0, j), EDGES.at(0, 1, j)
            both = jnp.where(half, small[b, :], big[p, :])
            big[p, :] = both
            small[b, :] = both
            p, b = BULK.at(0, TR // 8 - 1, j), EDGES.at(1, 0, j)
            both = jnp.where(half, big[p, :], small[b, :])
            big[p, :] = both
            small[b, :] = both
        own = slice(j * SPAN + 8, j * SPAN + 8 + TR)
        s_ref[own, :] = s_ref[own, :] + in_ref[TR * j : TR * j + TR, :]
        bs_ref[EDGES.at(0, 1, j), :] = s_ref[BULK.at(0, 0, j), :]
        bs_ref[EDGES.at(1, 0, j), :] = s_ref[BULK.at(0, TR // 8 - 1, j), :]
    run_steps(STEPS - STEPS // 2, BULK, state, consts, east_ref, row0, col0, add_bulk_edges(edge_ref))
    pairs = []
    for src, dst in ((qe_ref, qe_hbm), (qs_ref, qs_hbm)):
        for j in range(4):
            pairs.append((src.at[j * SPAN + 8 : j * SPAN + 8 + TR, :], dst.at[:, 128 * j : 128 * j + 128]))
    stored = copies(sem_tiles, pairs)
    for j in range(4):
        cols = slice(128 * j, 128 * j + 128)
        bed_ref[:, cols] = s_ref[j * SPAN + 8 : j * SPAN + 8 + TR, :] - bed_ref[:, cols]
    for n in range(3):
        for j in range(4):
            for g, i in ((0, 0), (1, TR // 8 - 1)):
                rows = slice(8 * (8 * n + 2 * j + g), 8 * (8 * n + 2 * j + g) + 8)
                if n == 0:
                    own_ref[rows, :] = bed_ref[8 * i : 8 * i + 8, 128 * j : 128 * j + 128]
                else:
                    own_ref[rows, :] = state[n][BULK.at(0, i, j), :]
    stored += copies(sem_left, ((bed_ref, depth_hbm), (left_ref, left_hbm)))
    wait(land)
    stored += land_part(
        live_ref[0], soil, got_ref, north_ref, south_ref, mean_ref, note_ref, slot_ref, rain_ref, cap_ref, soil_ref,
        cond_ref, soil_out, cond_x, pond_ref, sem_out,
    )
    wait(stored)


def middle_call(live, north, south, up, down, inflow, state, bed, got, mean, prep, slot, rain, cap, soil, cond):
    tile = array(TR, TC)
    buffer, small, strip = pltpu.VMEM((EXT, 128), F32), pltpu.VMEM((BANDS, 128), F32), pltpu.VMEM((STRIP, 128), F32)
    blocks, layers = pltpu.VMEM((NB, 128), F32), pltpu.VMEM((NB * NL, 128), F32)
    counts = (4, 10, 6, 3 * CHUNKS, 8, 2, 2 * CHUNKS)
    return pl.pallas_call(
        middle_kernel,
        out_shape=(tile,) * 3 + (array(LEFT, 128), array(NB * NL, 128)),
        in_specs=[SMEM] + [HBM] * 22,
        out_specs=(HBM,) * 5,
        scratch_shapes=[strip] * 4
        + [pltpu.VMEM((PANELS * TR, 128), F32)]
        + [buffer] * 7
        + [pltpu.VMEM((TR, TC), F32), pltpu.VMEM((DEV * K, 128), F32), pltpu.VMEM((8, 128), F32)]
        + [pltpu.VMEM((16, 128), F32), pltpu.VMEM((1, NB), jnp.int32), blocks, blocks]
        + [layers, pltpu.VMEM((NL, LAND), BF16), layers, blocks]
        + [pltpu.VMEM((LEFT, 128), F32), small, small, buffer]
        + [pltpu.SemaphoreType.DMA((n,)) for n in counts],
        compiler_params=params(FULL),
        name="middle_steps",
    )(live, north, south, up, down, inflow, *state, bed, got, mean, prep, slot, rain, cap, soil, cond)


def last_kernel(
    depth_in, qe_in, qs_in, north_hbm, south_hbm, left_hbm,
    depth_out, qe_out, qs_out, we_ref, ns_ref,
    north_ref, south_ref, left_ref, beast, tile_ref, sem_in, sem,
):
    got = copies(sem_in, ((left_hbm, left_ref), (north_hbm, north_ref), (south_hbm, south_ref)))
    row0, col0 = place()
    bs_ref, bqe_ref, bqs_ref, bmbe, bcre, bmbs, bcrs, bbed = (
        left_ref.at[BANDS * n : BANDS * n + BANDS, :] for n in range(8)
    )
    top = 8 * BANDS + SUMS
    sum_ref = left_ref.at[8 * BANDS : top, :]
    edge_ref = left_ref.at[top : top + 2 * TR, :]
    own_in = left_ref.at[top + 2 * TR : LEFT, :]
    band = (bs_ref, bqe_ref, bqs_ref)
    wait(got)
    for j in range(PANELS):
        for g, i, ref in ((0, 0, north_ref), (1, 1, south_ref)):
            p = EDGES.at(g, i, j)
            bs_ref[p, :] = bs_ref[p, :] + ref[8 * j : 8 * j + 8, :]
    run_steps(
        STEPS - STEPS // 2, EDGES, band, (bmbe, bcre, bmbs, bcrs), beast, row0, col0, add_band_edges(sum_ref, bqs_ref)
    )
    half = iota((8, 128), 0) < 4
    pairs = []
    for n, out in enumerate((depth_out, qe_out, qs_out)):
        for g, i in ((0, 1), (1, 0)):
            to = slice(16 * n + 8 * g, 16 * n + 8 * g + 8)
            for j in range(4):
                p = EDGES.at(g, i, j)
                mine = bs_ref[p, :] - bbed[p, :] if n == 0 else band[n][p, :]
                rows = slice(8 * (8 * n + 2 * j + g), 8 * (8 * n + 2 * j + g) + 8)
                bulk = own_in[rows, :]
                both = jnp.where(half, mine, bulk) if g == 0 else jnp.where(half, bulk, mine)
                tile_ref[to, 128 * j : 128 * j + 128] = both
            rows = slice(0, 8) if g == 0 else slice(TR - 8, TR)
            pairs.append((tile_ref.at[to, :], out.at[rows, :]))
    stored = copies(sem, pairs)
    for n in range(2):
        first, last = slice(TR * n, TR * n + 8), slice(TR * n + TR - 8, TR * n + TR)
        edge_ref[first, :] = jnp.where(half, sum_ref[8 * n : 8 * n + 8, :], edge_ref[first, :])
        edge_ref[last, :] = jnp.where(half, edge_ref[last, :], sum_ref[16 + 8 * n : 24 + 8 * n, :])
    we_ref[0:1, :] = edge_ref[TR : 2 * TR, :].T[127:128, :]
    we_ref[1:2, :] = edge_ref[0:TR, :].T[127:128, :]
    for j in range(4):
        for g in range(2):
            row = 32 + 8 * (4 * g + j) + 7
            ns_ref[g : g + 1, 128 * j : 128 * j + 128] = sum_ref[row : row + 1, :]
    wait(stored)


def last_call(tiles, north, south, left):
    strip = pltpu.VMEM((PANELS * 8, 128), F32)
    return pl.pallas_call(
        last_kernel,
        out_shape=(array(TR, TC), array(TR, TC), array(TR, TC), array(2, TR), array(2, TC)),
        in_specs=[HBM] * 6,
        out_specs=(HBM, HBM, HBM, VMEM, VMEM),
        scratch_shapes=[strip, strip, pltpu.VMEM((LEFT, 128), F32), pltpu.VMEM((BANDS, 128), F32)]
        + [pltpu.VMEM((48, TC), F32), pltpu.SemaphoreType.DMA((3,)), pltpu.SemaphoreType.DMA((6,))],
        input_output_aliases={0: 0, 1: 1, 2: 2},
        compiler_params=pltpu.CompilerParams(vmem_limit_bytes=61 * 1024 * 1024),
        name="last_steps",
    )(*tiles, north, south, left)


def shift(first, second, axis):
    count = lax.axis_size(axis)
    ahead = [(i, i + 1) for i in range(count - 1)]
    back = [(j, i) for i, j in ahead]
    return lax.ppermute(first, axis, ahead), lax.ppermute(second, axis, back)


def local(
    soil_water, conduct, rainfall, infil_cap, live_counts, send_slot, recv_row,
    bed_height, manning, depth_in, east_in, south_in, wet_mask,
):
    rain = rainfall.reshape(NB, 128)
    cap = infil_cap.reshape(NB, 128)
    soil = soil_water.reshape(2, 8, NB, 128).transpose(0, 2, 1, 3).reshape(NB * NL, 128)
    fields = (depth_in, wet_mask, bed_height, manning, east_in, south_in)

    sent, pond, recv = send_call(live_counts, send_slot, recv_row, rain, cap, depth_in, wet_mask)
    got = lax.all_to_all(sent.reshape(DEV, 1, K * 128), ALL, split_axis=0, concat_axis=0, tiled=True)
    got = got.reshape(DEV * K, 128)

    to_west, to_east, mean = cols_call(live_counts, recv, soil, fields)
    west, east = shift(to_east, to_west, "gx")
    up, down, side, prep = rows_call(west, east, mean, recv, pond, fields)
    north, south = shift(down, up, ROWS)
    state = first_call(side, fields)

    inflow, in_up, in_down = inflow_call(state[-1], got, prep)
    in_north, in_south = shift(in_down, in_up, ROWS)
    *tiles, left, soil_out = middle_call(
        live_counts, north, south, up, down, inflow, state, bed_height,
        got, mean, prep, send_slot, rain, cap, soil, conduct,
    )
    depth, east_q, south_q, edge_we, edge_ns = last_call(tiles, in_north, in_south, left)
    soil_out = soil_out.reshape(2, NB, 8, 128).transpose(0, 2, 1, 3).reshape(NL, LAND)
    return soil_out, depth, east_q, south_q, edge_we, edge_ns


def solution(mesh):
    placed = (
        P(None, ALL),
        P(None, ALL),
        P(ALL),
        P(ALL),
        P(ALL),
        P(ALL, None),
        P(ALL, None),
    ) + (P(ROWS, "gx"),) * 6
    return jax.shard_map(
        local,
        mesh=mesh,
        in_specs=placed,
        out_specs=(
            P(None, ALL),
            P(ROWS, "gx"),
            P(ROWS, "gx"),
            P(ROWS, "gx"),
            P("gx", ROWS),
            P(ROWS, "gx"),
        ),
        check_vma=False,
    )
```

```python
import jax
import jax.numpy as jnp
from jax import lax
from jax.experimental import pallas as pl
from jax.experimental.pallas import tpu as pltpu
from jax.sharding import PartitionSpec as P

F32 = jnp.float32
BF16 = jnp.bfloat16

NL = 16
STEPS = 8
TR = 256
TC = 512
NB = 192
LAND = NB * 128
DEV = 256
HALO = 8
K = 7
PANELS = 5
SPAN = TR + 16
EXT = PANELS * SPAN
BAND = 48
BANDS = 2 * PANELS * BAND
STRIP = 5 * PANELS * 8
NEAR = 5 * PANELS * 2 * 24
PREP = 2 * DEV + TR + 16 + 8
SHELF = PREP + 2 * STRIP
FLOW = PANELS * TR + 2 * DEV + 8
MEAN_LANE = 40
FULL = 63

gravity = 9.81
cell_size = 30.0
time_step = 2.5
depth_floor = 0.25
half_rate = 0.5
lateral_rate = 0.2
drainage = 0.05
slope_coef = gravity * time_step / cell_size
fric_coef = gravity * time_step

ROWS = ("grp", "gy")
ALL = ("grp", "gy", "gx")
VMEM = pl.BlockSpec(memory_space=pltpu.VMEM)
SMEM = pl.BlockSpec(memory_space=pltpu.SMEM)
HBM = pl.BlockSpec(memory_space=pltpu.HBM)
ANY = pl.BlockSpec(memory_space=pl.ANY)


def params(mib):
    return pltpu.CompilerParams(vmem_limit_bytes=mib * 1024 * 1024)


def array(*shape):
    return jax.ShapeDtypeStruct(shape, F32)


def iota(shape, dim):
    return lax.broadcasted_iota(jnp.int32, shape, dim)


def copies(sem, pairs):
    made = [pltpu.make_async_copy(src, dst, sem.at[n]) for n, (src, dst) in enumerate(pairs)]
    for c in made:
        c.start()
    return made


def wait(made):
    for c in made:
        c.wait()


def parts(x):
    high = x.astype(BF16)
    low = (x - high.astype(F32)).astype(BF16)
    return high, low


def hot_dot(hot, x):
    both = jnp.dot(hot, jnp.concatenate(parts(x), axis=1), preferred_element_type=F32)
    return both[:, :128] + both[:, 128:]


def as_hot(mask):
    return mask.astype(F32).astype(BF16)


def twice(col):
    return jnp.concatenate([col, col], axis=1)


def turned(row):
    return jnp.broadcast_to(row, (128, row.shape[1])).T


def send_kernel(
    live_ref, slot_hbm, recv_hbm, rain_hbm, cap_hbm, depth_hbm, wet_hbm, soil_hbm,
    out_hbm, pond_hbm, recv_out,
    soil_ref, slot_ref, recv_ref, rain_ref, cap_ref, depth_ref, wet_ref, out_ref, pond_ref, tmp_ref, sem, sem_out,
):
    got = copies(
        sem,
        (
            (slot_hbm, slot_ref), (rain_hbm, rain_ref), (cap_hbm, cap_ref),
            (recv_hbm, recv_ref), (depth_hbm, depth_ref), (wet_hbm, wet_ref),
            (soil_hbm.at[NB * 8 : NB * 16, :], soil_ref),
        ),
    )
    live = live_ref[0]
    wait(got[:3])
    cell = iota((NB, 128), 0) * 128 + iota((NB, 128), 1)
    rain = jnp.where(cell < live, rain_ref[...], 0.0)
    rhs = jnp.concatenate(parts(rain) + parts(cap_ref[...]), axis=1)
    slot = slot_ref[...]
    tile = iota((DEV, NB), 0)
    lane = iota((DEV, 128), 1)
    for_west = jnp.zeros((DEV, 128), F32)
    for_east = jnp.zeros((DEV, 128), F32)
    for k in range(2):
        res = jnp.dot(as_hot(slot == 2 * tile + k), rhs, preferred_element_type=F32)
        for a in range(2):
            block = res[:, 256 * a : 256 * a + 128] + res[:, 256 * a + 128 : 256 * a + 256]
            out_ref[pl.ds(2 * a + k, DEV, stride=K), :] = block
            g = 2 * a + k
            low, high = 124 - 8 * g, 8 * g
            moved_w = pltpu.roll(block, (128 - 8 * g) % 128, 1) if g else block
            moved_e = pltpu.roll(block, 8 * g, 1) if g else block
            for_west = jnp.where((lane >= low) & (lane < low + 4), moved_w, for_west)
            for_east = jnp.where((lane >= high) & (lane < high + 4), moved_e, for_east)
    edge = jnp.where(lane < 64, pltpu.roll(for_east, DEV - 1, 0), pltpu.roll(for_west, 1, 0))
    wait(got[3:])
    half = NB * 8
    which = iota((half, 128), 0) // 8 * 128 + iota((half, 128), 1)
    kept = jnp.where(which < live, soil_ref[...], 0.0)
    mean = jnp.sum(jnp.sum(kept.reshape(half // 8, 8, 128), axis=0)) / (live.astype(F32) * 8.0)
    out_ref[pl.ds(6, DEV, stride=K), :] = jnp.where(lane == MEAN_LANE, mean, edge)
    tmp_ref[...] = turned(recv_ref[...].astype(F32))
    fields = []
    for c in range(4):
        cols = slice(128 * c, 128 * c + 128)
        fields.append(jnp.concatenate(parts(depth_ref[:, cols] * wet_ref[:, cols].astype(F32)), axis=1))
    place4 = iota((DEV, 256), 1).astype(F32) * 4.0
    recv_out[4:8, :] = jnp.zeros((4, 128), F32)
    for k in range(2):
        col = tmp_ref[pl.ds(k, DEV, stride=2), :]
        recv_out[2 * k : 2 * k + 1, :] = col[:128].T[0:1]
        recv_out[2 * k + 1 : 2 * k + 2, :] = col[128:].T[0:1]
        wide = twice(col)
        acc = jnp.zeros((DEV, 256), F32)
        for c in range(4):
            acc = acc + jnp.dot(as_hot(wide == place4 + float(c)), fields[c], preferred_element_type=F32)
        pond = acc[:, :128] + acc[:, 128:]
        out_ref[pl.ds(4 + k, DEV, stride=K), :] = pond
        pond_ref[DEV * k : DEV * k + DEV, :] = pond
    wait(copies(sem_out, ((out_ref, out_hbm), (pond_ref, pond_hbm))))


def send_call(live, slot, recv, rain, cap, depth, wet, soil):
    return pl.pallas_call(
        send_kernel,
        out_shape=(array(DEV * K, 128), array(2 * DEV, 128), array(8, 128)),
        in_specs=[SMEM] + [HBM] * 7,
        out_specs=(HBM, HBM, VMEM),
        scratch_shapes=[
            pltpu.VMEM((NB * 8, 128), F32),
            pltpu.VMEM((1, NB), jnp.int32),
            pltpu.VMEM((1, 2 * DEV), jnp.int32),
            pltpu.VMEM((NB, 128), F32),
            pltpu.VMEM((NB, 128), F32),
            pltpu.VMEM((TR, TC), F32),
            pltpu.VMEM((TR, TC), jnp.int32),
            pltpu.VMEM((DEV * K, 128), F32),
            pltpu.VMEM((2 * DEV, 128), F32),
            pltpu.VMEM((2 * DEV, 128), F32),
            pltpu.SemaphoreType.DMA((7,)),
            pltpu.SemaphoreType.DMA((2,)),
        ],
        compiler_params=params(FULL),
        name="message",
    )(live, slot, recv, rain, cap, depth, wet, soil)


def cols_kernel(
    recv_hbm, depth, wet, bed, man, qe, qs,
    to_west, to_east,
    west_ref, east_ref, wet_w, wet_e, sem,
):
    left, right = slice(0, 128), slice(TC - 128, TC)
    pairs = [(wet.at[:, left], wet_w), (wet.at[:, right], wet_e)]
    for n, f in enumerate((depth, bed, man, qe, qs)):
        rows = slice(TR * n, TR * n + TR)
        pairs.append((f.at[:, left], west_ref.at[rows, :]))
        pairs.append((f.at[:, right], east_ref.at[rows, :]))
    pairs.append((recv_hbm, to_west.at[TR : TR + 8, :]))
    pairs.append((recv_hbm, to_east.at[TR : TR + 8, :]))
    got = copies(sem, pairs)
    wait(got)
    lane = iota((TR, 128), 1)
    for src, mask, out, first in ((west_ref, wet_w, to_west, 0), (east_ref, wet_e, to_east, 120)):
        acc = jnp.zeros((TR, 128), F32)
        for n in range(5):
            own = src[TR * n : TR * n + TR, :]
            if n == 0:
                own = own * mask[...].astype(F32)
            shift = (8 * n - first) % 128
            moved = pltpu.roll(own, shift, 1) if shift else own
            acc = jnp.where((lane >= 8 * n) & (lane < 8 * n + 8), moved, acc)
        out[0:TR, :] = acc


def cols_call(recv, fields):
    return pl.pallas_call(
        cols_kernel,
        out_shape=(array(TR + 8, 128), array(TR + 8, 128)),
        in_specs=[HBM] * 7,
        scratch_shapes=[
            pltpu.VMEM((5 * TR, 128), F32),
            pltpu.VMEM((5 * TR, 128), F32),
            pltpu.VMEM((TR, 128), jnp.int32),
            pltpu.VMEM((TR, 128), jnp.int32),
            pltpu.SemaphoreType.DMA((14,)),
        ],
        compiler_params=params(FULL),
        name="column_strips",
    )(recv, *fields)


def inflow_kernel(got_ref, prep_ref, flow_hbm, up_ref, down_ref, flow_ref, sem):
    in_ref = flow_ref.at[0 : PANELS * TR, :]
    land_ref = flow_ref.at[PANELS * TR : FLOW, :]
    up_ref[0:STRIP, :] = prep_ref[PREP : PREP + STRIP, :]
    down_ref[0:STRIP, :] = prep_ref[PREP + STRIP : SHELF, :]
    for k in range(2):
        land_ref[DEV * k : DEV * k + DEV, :] = got_ref[pl.ds(4 + k, DEV, stride=K), :]
    n_rows, n_cols = lax.axis_size(ROWS), lax.axis_size("gx")
    my_row, my_col = lax.axis_index(ROWS), lax.axis_index("gx")
    here = my_row * n_cols + my_col

    def mean_of(device):
        at = jnp.clip(device, 0, DEV - 1) * K + 6
        return jnp.sum(jnp.where(iota((1, 128), 1) == MEAN_LANE, got_ref[pl.ds(at, 1), :], 0.0))

    mean = mean_of(here)
    lat = jnp.where(my_row > 0, mean_of(here - n_cols) - mean, 0.0)
    lat = lat + jnp.where(my_row < n_rows - 1, mean_of(here + n_cols) - mean, 0.0)
    lat = lat + jnp.where(my_col > 0, mean_of(here - 1) - mean, 0.0)
    lat = lat + jnp.where(my_col < n_cols - 1, mean_of(here + 1) - mean, 0.0)
    land_ref[2 * DEV : 2 * DEV + 8, :] = jnp.full((8, 128), lateral_rate * lat, F32)
    lane = iota((DEV, 128), 1)
    place4 = iota((TR, DEV), 0).astype(F32) * 4.0

    def runoff(rain, cap, pond):
        wetting = rain + jnp.maximum(pond, 0.0)
        return rain * (1.0 - cap / (wetting + half_rate))

    def line(k, base):
        at = base + 2 * k
        return jnp.concatenate([prep_ref[at : at + 1, :], prep_ref[at + 1 : at + 2, :]], axis=1)

    note, own = 2 * DEV + TR, PREP - 8
    flows = []
    for k in range(2):
        rain = got_ref[pl.ds(k, DEV, stride=K), :]
        cap = got_ref[pl.ds(2 + k, DEV, stride=K), :]
        flow = runoff(rain, cap, prep_ref[DEV * k : DEV * k + DEV, :])
        flows.append(jnp.concatenate(parts(flow), axis=1))
    for c in range(4):
        acc = jnp.zeros((TR, 256), F32)
        for k in range(2):
            hot = as_hot(line(k, own) == place4 + float(c))
            acc = acc + jnp.dot(hot, flows[k], preferred_element_type=F32)
        in_ref[TR * c : TR * c + TR, :] = acc[:, :128] + acc[:, 128:]
    parts_of = (slice(0, 4 * TR), slice(PANELS * TR, FLOW))
    stored = copies(sem, [(flow_ref.at[rows, :], flow_hbm.at[rows, :]) for rows in parts_of])

    edge = got_ref[pl.ds(6, DEV, stride=K), :]
    depth = prep_ref[2 * DEV : 2 * DEV + TR, :]
    lane_place = iota((DEV, TR), 1).astype(F32) * 4.0
    is_east, is_west = lane < 4, lane >= 124
    acc = jnp.zeros((TR, 128), F32)

    def pick(g):
        if g == 0:
            return edge
        return jnp.where(lane < 64, pltpu.roll(edge, 128 - 8 * g, 1), pltpu.roll(edge, 8 * g, 1))

    sides = ((note, 3, is_west), (note + 8, 0, is_east))
    for k in range(2):
        rain, cap = pick(k), pick(2 + k)
        pond = jnp.zeros((DEV, 128), F32)
        for base, c, mask in sides:
            col = twice(turned(line(k, base)))
            pond = jnp.where(mask, hot_dot(as_hot(col == lane_place + float(c)), depth), pond)
        flow = jnp.where(is_east | is_west, runoff(rain, cap, pond), 0.0)
        for base, c, mask in sides:
            hot = as_hot(line(k, base) == place4 + float(c))
            acc = acc + hot_dot(hot, jnp.where(mask, flow, 0.0))
    acc = jnp.where(is_west & (my_col > 0), acc, jnp.where(is_east & (my_col < n_cols - 1), acc, 0.0))
    side_rows = slice(4 * TR, 5 * TR)
    in_ref[side_rows, :] = acc
    stored.append(pltpu.make_async_copy(flow_ref.at[side_rows, :], flow_hbm.at[side_rows, :], sem.at[2]))
    stored[-1].start()
    for j in range(PANELS):
        to = slice(STRIP + 8 * j, STRIP + 8 * j + 8)
        up_ref[to, :] = in_ref[TR * j : TR * j + 8, :]
        down_ref[to, :] = in_ref[TR * j + TR - 8 : TR * j + TR, :]
    wait(stored)


def inflow_call(got, prep):
    strip = array(STRIP + PANELS * 8, 128)
    return pl.pallas_call(
        inflow_kernel,
        out_shape=(array(FLOW, 128), strip, strip),
        in_specs=[VMEM, VMEM],
        out_specs=(HBM, VMEM, VMEM),
        scratch_shapes=[pltpu.VMEM((FLOW, 128), F32), pltpu.SemaphoreType.DMA((3,))],
        compiler_params=params(52),
        name="inflow",
    )(got, prep)


class Grid:
    def __init__(self, bases, tiles, rows):
        self.bases, self.tiles, self.rows = bases, tiles, rows
        self.all = [(g, i) for g in range(len(bases)) for i in range(tiles)]

    def at(self, g, i, j, shift=0):
        start = self.bases[g][j] + 8 + 8 * i + shift
        return slice(start, start + 8)

    def south_open(self, g, i, row0):
        row = row0 + self.rows[g] + 8 * i + iota((8, 128), 0)
        return (row >= 0) & (row + 1 <= TR * lax.axis_size(ROWS) - 1)


BULK = Grid([[j * SPAN for j in range(PANELS)]], TR // 8, [0])
EDGES = Grid([[(PANELS * g + j) * BAND for j in range(PANELS)] for g in range(2)], 4, [-8, TR - 24])


def east_open(j, col0):
    lane = iota((8, 128), 1)
    if j < 4:
        col = col0 + 128 * j + lane
    else:
        col = col0 + jnp.where(lane < 64, TC + lane, lane - 128)
    return (col >= 0) & (col + 1 <= TC * lax.axis_size("gx") - 1)


def shifted(values, shift, lane, offset):
    moved = [pltpu.roll(v, shift, 1) for v in values]
    edge = iota((8, 128), 1) == lane
    return [jnp.where(edge, moved[(j + offset) % PANELS], moved[j]) for j in range(PANELS)]


def run_steps(count, grid, state, consts, east_ref, row0, col0, after):
    s_ref, qe_ref, qs_ref = state
    mbe_ref, cre_ref, mbs_ref, crs_ref = consts
    ge = [jnp.where(east_open(j, col0), slope_coef, 0.0).astype(F32) for j in range(PANELS)]

    def flux(q, a, b, mb, cr, g):
        h = jnp.maximum(jnp.maximum(a, b) - mb, depth_floor)
        numer = q - g * (h * (b - a))
        power = jnp.exp2(jnp.log(h) * F32(-7.0 / 3.0 / 0.6931471805599453))
        return numer * pltpu.reciprocal(1.0 + cr * jnp.abs(q) * power, approx=True)

    def one_step(_, c0):
        for g, i in grid.all:
            moved = shifted([s_ref[grid.at(g, i, j), :] for j in range(PANELS)], 127, 127, 1)
            for j in range(PANELS):
                east_ref[grid.at(g, i, j), :] = moved[j]
        for g, i in grid.all:
            gs = jnp.where(grid.south_open(g, i, row0), slope_coef, 0.0).astype(F32)
            for j in range(PANELS):
                p = grid.at(g, i, j)
                s = s_ref[p, :]
                qe_ref[p, :] = flux(qe_ref[p, :], s, east_ref[p, :], mbe_ref[p, :], cre_ref[p, :], ge[j])
                qs_ref[p, :] = flux(qs_ref[p, :], s, s_ref[grid.at(g, i, j, 1), :], mbs_ref[p, :], crs_ref[p, :], gs)
        for g, i in grid.all:
            qe = [qe_ref[grid.at(g, i, j), :] for j in range(PANELS)]
            west = shifted(qe, 1, 0, PANELS - 1)
            for j in range(PANELS):
                p = grid.at(g, i, j)
                change = (qe[j] - west[j]) + (qs_ref[p, :] - qs_ref[grid.at(g, i, j, -1), :])
                s_ref[p, :] = s_ref[p, :] - F32(time_step / cell_size) * change
            after(g, i, qe)
        return c0

    lax.fori_loop(0, count, one_step, 0)


def set_up(grid, state, consts, bed_ref, man_ref, row0, col0):
    s_ref, qe_ref, qs_ref = state
    mbe_ref, cre_ref, mbs_ref, crs_ref = consts
    open_e = east_open(3, col0)
    for g, i in grid.all:
        bed = [bed_ref[grid.at(g, i, j), :] for j in range(PANELS)]
        man = [man_ref[grid.at(g, i, j), :] for j in range(PANELS)]
        bed_e, man_e = shifted(bed, 127, 127, 1), shifted(man, 127, 127, 1)
        for j in range(PANELS):
            p = grid.at(g, i, j)
            mbe_ref[p, :] = jnp.maximum(bed[j], bed_e[j])
            mbs_ref[p, :] = jnp.maximum(bed[j], bed_ref[grid.at(g, i, j, 1), :])
            rough_e = 0.5 * (man[j] + man_e[j])
            rough_s = 0.5 * (man[j] + man_ref[grid.at(g, i, j, 1), :])
            cre_ref[p, :] = fric_coef * rough_e * rough_e
            crs_ref[p, :] = fric_coef * rough_s * rough_s
            s_ref[p, :] = s_ref[p, :] + bed[j]
        qe_ref[grid.at(g, i, 3), :] = jnp.where(open_e, qe_ref[grid.at(g, i, 3), :], 0.0)
        if grid.rows[g] + 8 * i == TR - 8:
            for j in range(PANELS):
                p = grid.at(g, i, j)
                qs_ref[p, :] = jnp.where(grid.south_open(g, i, row0), qs_ref[p, :], 0.0)


def clear_guards(grid, refs):
    zero = jnp.zeros((8, 128), F32)
    for ref in refs:
        for g in range(len(grid.bases)):
            for j in range(PANELS):
                ref[grid.at(g, -1, j), :] = zero
                ref[grid.at(g, grid.tiles, j), :] = zero


def place():
    return lax.axis_index(ROWS) * TR, lax.axis_index("gx") * TC


def add_bulk_edges(edge_ref):
    def after(g, i, qe):
        for n in range(2):
            rows = slice(TR * n + 8 * i, TR * n + 8 * i + 8)
            edge_ref[rows, :] = edge_ref[rows, :] + qe[3 + n]

    return after


def add_band_edges(sum_ref, qs_ref):
    def after(g, i, qe):
        if EDGES.rows[g] + 8 * i in (0, TR - 8):
            for n in range(2):
                rows = slice(16 * g + 8 * n, 16 * g + 8 * n + 8)
                sum_ref[rows, :] = sum_ref[rows, :] + qe[3 + n]
        if EDGES.rows[g] + 8 * i == (-8, TR - 8)[g]:
            for j in range(4):
                rows = slice(32 + 8 * (4 * g + j), 40 + 8 * (4 * g + j))
                sum_ref[rows, :] = sum_ref[rows, :] + qs_ref[EDGES.at(g, i, j), :]

    return after


SUMS = 32 + 64


def first_kernel(
    west_hbm, east_hbm, recv_hbm, pond_hbm, depth_hbm, wet_hbm, bed_hbm, man_hbm, qe_hbm, qs_hbm,
    s_out, qe_out, qs_out, mbe_out, cre_out, mbs_out, crs_out, edge_out, prep_out, near_out,
    s_ref, qe_ref, qs_ref, mbe_ref, cre_ref, mbs_ref, crs_ref, edge_ref, prep_ref, near_ref,
    bed_x, man_x, wet_ref, east_x, west_ref, east_ref, sem, sem_out,
):
    pairs = [
        (west_hbm, west_ref), (east_hbm, east_ref),
        (recv_hbm, prep_ref.at[PREP - 8 : PREP, :]), (pond_hbm, prep_ref.at[0 : 2 * DEV, :]), (wet_hbm, wet_ref),
    ]
    targets = (s_ref, bed_x, man_x, qe_ref, qs_ref)
    for n, src in enumerate((depth_hbm, bed_hbm, man_hbm, qe_hbm, qs_hbm)):
        for j in range(4):
            to = targets[n].at[j * SPAN + 8 : j * SPAN + 8 + TR, :]
            pairs.append((src.at[:, 128 * j : 128 * j + 128], to))
    got = copies(sem, pairs)
    row0, col0 = place()
    state, consts = (s_ref, qe_ref, qs_ref), (mbe_ref, cre_ref, mbs_ref, crs_ref)
    clear_guards(BULK, targets + consts)
    edge_ref[...] = jnp.zeros((2 * TR, 128), F32)
    wait(got[:2])
    lane = iota((TR, 128), 1)
    for n, ref in enumerate(targets):
        shift = (128 - 8 * n) % 128
        e, w = east_ref[0:TR, :], west_ref[0:TR, :]
        e = pltpu.roll(e, shift, 1) if shift else e
        w = pltpu.roll(w, 120 - 8 * n, 1)
        beside = jnp.where(lane < 8, e, jnp.where(lane >= 120, w, 0.0))
        ref[4 * SPAN + 8 : 4 * SPAN + 8 + TR, :] = beside
        if n == 0:
            prep_ref[2 * DEV : 2 * DEV + TR, :] = beside
    note = 2 * DEV + TR
    prep_ref[note : note + 8, :] = west_ref[TR : TR + 8, :]
    prep_ref[note + 8 : note + 16, :] = east_ref[TR : TR + 8, :]
    wait(got[2:])
    stored = []
    for j in range(4):
        own = slice(j * SPAN + 8, j * SPAN + 8 + TR)
        s_ref[own, :] = s_ref[own, :] * wet_ref[:, 128 * j : 128 * j + 128].astype(F32)
    for n, ref in enumerate(targets):
        for j in range(PANELS):
            at = PANELS * n + j
            base = j * SPAN + 8
            near_ref[48 * at : 48 * at + 24, :] = ref[base : base + 24, :]
            near_ref[48 * at + 24 : 48 * at + 48, :] = ref[base + TR - 24 : base + TR, :]
            up, down = PREP + 8 * at, PREP + STRIP + 8 * at
            prep_ref[up : up + 8, :] = ref[base : base + 8, :]
            prep_ref[down : down + 8, :] = ref[base + TR - 8 : base + TR, :]

    def store(pairs):
        for src, dst in pairs:
            stored.append(pltpu.make_async_copy(src, dst, sem_out.at[len(stored)]))
            stored[-1].start()

    store(((prep_ref, prep_out), (near_ref, near_out)))
    set_up(BULK, state, consts, bed_x, man_x, row0, col0)
    store(zip(consts, (mbe_out, cre_out, mbs_out, crs_out)))
    run_steps(STEPS // 2, BULK, state, consts, east_x, row0, col0, add_bulk_edges(edge_ref))
    store(zip(state + (edge_ref,), (s_out, qe_out, qs_out, edge_out)))
    wait(stored)


def first_call(west, east, recv, pond, fields):
    ext = array(EXT, 128)
    buffer, message = pltpu.VMEM((EXT, 128), F32), pltpu.VMEM((TR + 8, 128), F32)
    extra = (2 * TR, SHELF, NEAR)
    return pl.pallas_call(
        first_kernel,
        out_shape=(ext,) * 7 + tuple(array(n, 128) for n in extra),
        in_specs=[HBM] * 10,
        out_specs=(HBM,) * 10,
        scratch_shapes=[buffer] * 7
        + [pltpu.VMEM((n, 128), F32) for n in extra]
        + [buffer, buffer, pltpu.VMEM((TR, TC), jnp.int32), buffer, message, message]
        + [pltpu.SemaphoreType.DMA((25,)), pltpu.SemaphoreType.DMA((10,))],
        compiler_params=params(FULL),
        name="first_steps",
    )(west, east, recv, pond, *fields)


CHUNK = 32
CHUNKS = NB // CHUNK


def land_copies(soil_hbm, cond_hbm, soil_ref, cond_ref):
    pairs = []
    half = NB * 8
    for c in range(CHUNKS):
        cols = slice(c * CHUNK * 128, (c + 1) * CHUNK * 128)
        pairs.append((cond_hbm.at[:, cols], cond_ref.at[:, cols]))
        for h in range(2):
            rows = slice(h * half + c * CHUNK * 8, h * half + (c + 1) * CHUNK * 8)
            pairs.append((soil_hbm.at[rows, :], soil_ref.at[rows, :]))
    return pairs


def land_part(
    live, moved, land_ref, slot_ref, rain_ref, cap_ref, soil_ref, cond_ref, out_hbm, cond_x, pond_ref, sem_out
):
    half = NB * 8
    slot = jnp.broadcast_to(slot_ref[...].astype(F32), (128, NB))
    slot = jnp.concatenate([slot, jnp.full((128, 256 - NB), -1.0, F32)], axis=1).T
    slot = twice(slot[0:NB])
    tile2 = iota((NB, DEV), 1).astype(F32) * 2.0
    pond = jnp.zeros((NB, 128), F32)
    for k in range(2):
        pond = pond + hot_dot(as_hot(slot == tile2 + float(k)), land_ref[DEV * k : DEV * k + DEV, :])
    pond_ref[...] = pond
    lat = land_ref[2 * DEV : 2 * DEV + 8, :]
    sub, lane = iota((8, 128), 0), iota((8, 128), 1)
    group = range(CHUNK // 8)
    stored = []
    for c in range(CHUNKS):
        wait(moved[3 * c : 3 * c + 3])
        for b in range(c * CHUNK, (c + 1) * CHUNK):
            cond_x[16 * b : 16 * b + 16, :] = cond_ref[:, 128 * b : 128 * b + 128].astype(F32)

        def soil_at(g, layer):
            return pl.ds((layer // 8) * half + (c * CHUNK + 8 * g) * 8 + layer % 8, 8, stride=8)

        def cond_at(g, layer):
            return cond_x[pl.ds((c * CHUNK + 8 * g) * 16 + layer, 8, stride=16), :]

        uptake, kept = [], []
        for g in group:
            blocks = slice(c * CHUNK + 8 * g, c * CHUNK + 8 * g + 8)
            rain, cap = rain_ref[blocks, :], cap_ref[blocks, :]
            wetting = rain + jnp.maximum(pond_ref[blocks, :], 0.0)
            uptake.append(cap * wetting * pltpu.reciprocal(wetting + half_rate, approx=True))
            kept.append((blocks.start + sub) * 128 + lane < live)
        ratios = [[] for _ in group]
        values = [[] for _ in group]
        above = [None for _ in group]
        cond = [cond_at(g, 0) for g in group]
        for j in range(NL):
            for g in group:
                rhs = soil_ref[soil_at(g, j), :]
                if j == 0:
                    rhs = rhs + uptake[g]
                if j >= 8:
                    rhs = rhs + lat
                center = 1.0 if j < NL - 1 else 1.0 + drainage
                if j > 0:
                    rhs = rhs + above[g] * values[g][-1]
                    center = center + (above[g] + above[g] * ratios[g][-1])
                if j < NL - 1:
                    below = cond_at(g, j + 1)
                    face = 0.5 * (cond[g] + below)
                    cond[g] = below
                    center = center + face
                r = pltpu.reciprocal(center, approx=True)
                if j < NL - 1:
                    ratios[g].append(-face * r)
                    above[g] = face
                values[g].append(rhs * r)
        x = [values[g][-1] for g in group]
        for j in range(NL - 1, -1, -1):
            for g in group:
                if j < NL - 1:
                    x[g] = values[g][j] - ratios[g][j] * x[g]
                soil_ref[soil_at(g, j), :] = jnp.where(kept[g], x[g], soil_ref[soil_at(g, j), :])
        for h in range(2):
            rows = slice(h * half + c * CHUNK * 8, h * half + (c + 1) * CHUNK * 8)
            stored.append(pltpu.make_async_copy(soil_ref.at[rows, :], out_hbm.at[rows, :], sem_out.at[2 * c + h]))
            stored[-1].start()
    return stored


def middle_kernel(
    live_ref, flow_hbm, s_in, qe_in, qs_in, mbe_in, cre_in, mbs_in, crs_in, edge_in, bed_hbm,
    slot_hbm, rain_hbm, cap_hbm, soil_hbm, cond_hbm,
    depth_hbm, qe_hbm, qs_hbm, edge_hbm, soil_out,
    in_ref, s_ref, qe_ref, qs_ref, mbe_ref, cre_ref, mbs_ref, crs_ref, edge_ref, bed_ref,
    land_ref, slot_ref, rain_ref, cap_ref, soil_ref, cond_ref, cond_x, pond_ref,
    east_ref, sem_state, sem_land, sem_soil, sem_tiles, sem_out,
):
    state, consts = (s_ref, qe_ref, qs_ref), (mbe_ref, cre_ref, mbs_ref, crs_ref)
    in_hbm, land_hbm = flow_hbm.at[0 : PANELS * TR, :], flow_hbm.at[PANELS * TR : FLOW, :]
    sources = (s_in, in_hbm, qe_in, qs_in, mbe_in, cre_in, mbs_in, crs_in, edge_in, bed_hbm)
    loaded = copies(sem_state, list(zip(sources, (s_ref, in_ref, qe_ref, qs_ref) + consts + (edge_ref, bed_ref))))
    land = copies(
        sem_land, ((slot_hbm, slot_ref), (rain_hbm, rain_ref), (cap_hbm, cap_ref), (land_hbm, land_ref))
    )
    soil = copies(sem_soil, land_copies(soil_hbm, cond_hbm, soil_ref, cond_ref))
    row0, col0 = place()
    wait(loaded)
    for j in range(PANELS):
        own = slice(j * SPAN + 8, j * SPAN + 8 + TR)
        s_ref[own, :] = s_ref[own, :] + in_ref[TR * j : TR * j + TR, :]
    run_steps(STEPS - STEPS // 2, BULK, state, consts, east_ref, row0, col0, add_bulk_edges(edge_ref))
    pairs = [(edge_ref, edge_hbm)]
    for src, dst in ((qe_ref, qe_hbm), (qs_ref, qs_hbm)):
        for j in range(4):
            pairs.append((src.at[j * SPAN + 8 : j * SPAN + 8 + TR, :], dst.at[:, 128 * j : 128 * j + 128]))
    for j in range(4):
        cols = slice(128 * j, 128 * j + 128)
        bed_ref[:, cols] = s_ref[j * SPAN + 8 : j * SPAN + 8 + TR, :] - bed_ref[:, cols]
    pairs.append((bed_ref, depth_hbm))
    stored = copies(sem_tiles, pairs)
    wait(land)
    stored += land_part(
        live_ref[0], soil, land_ref, slot_ref, rain_ref, cap_ref, soil_ref, cond_ref, soil_out, cond_x, pond_ref, sem_out
    )
    wait(stored)


def middle_call(live, flow, state, edge, bed, slot, rain, cap, soil, cond):
    tile = array(TR, TC)
    buffer = pltpu.VMEM((EXT, 128), F32)
    blocks, layers = pltpu.VMEM((NB, 128), F32), pltpu.VMEM((NB * NL, 128), F32)
    counts = (10, 4, 3 * CHUNKS, 10, 2 * CHUNKS)
    return pl.pallas_call(
        middle_kernel,
        out_shape=(tile,) * 3 + (array(2 * TR, 128), array(NB * NL, 128)),
        in_specs=[SMEM] + [HBM] * 15,
        out_specs=(HBM,) * 5,
        scratch_shapes=[pltpu.VMEM((PANELS * TR, 128), F32)]
        + [buffer] * 7
        + [pltpu.VMEM((2 * TR, 128), F32), pltpu.VMEM((TR, TC), F32), pltpu.VMEM((2 * DEV + 8, 128), F32)]
        + [pltpu.VMEM((1, NB), jnp.int32), blocks, blocks]
        + [layers, pltpu.VMEM((NL, LAND), BF16), layers, blocks, buffer]
        + [pltpu.SemaphoreType.DMA((n,)) for n in counts],
        compiler_params=params(FULL),
        name="middle_steps",
    )(live, flow, *state, edge, bed, slot, rain, cap, soil, cond)


def last_kernel(
    depth_in, qe_in, qs_in, north_hbm, south_hbm, near_hbm, in_hbm, edge_hbm,
    depth_out, qe_out, qs_out, we_ref, ns_ref,
    north_ref, south_ref, near_ref, in_ref, edge_ref,
    bs_ref, bqe_ref, bqs_ref, bmbe, bcre, bmbs, bcrs, bbed, bman, beast, sum_ref, tile_ref, sem_in, sem,
):
    pairs = [(near_hbm, near_ref), (north_hbm, north_ref), (south_hbm, south_ref), (edge_hbm, edge_ref)]
    for j in range(PANELS):
        for g, start in ((0, 0), (1, TR - 24)):
            to = 24 * (2 * j + g)
            pairs.append((in_hbm.at[TR * j + start : TR * j + start + 24, :], in_ref.at[to : to + 24, :]))
    got = copies(sem_in, pairs)
    row0, col0 = place()
    band, consts = (bs_ref, bqe_ref, bqs_ref), (bmbe, bcre, bmbs, bcrs)
    targets = (bs_ref, bbed, bman, bqe_ref, bqs_ref)
    clear_guards(EDGES, targets + consts)
    sum_ref[...] = jnp.zeros((SUMS, 128), F32)
    wait(got)
    for n, out in enumerate(targets):
        for j in range(PANELS):
            at = PANELS * n + j
            strip = slice(8 * at, 8 * at + 8)
            out[EDGES.at(0, 0, j), :] = north_ref[strip, :]
            out[EDGES.at(1, 3, j), :] = south_ref[strip, :]
            for i in range(3):
                rows = 48 * at + 8 * i
                out[EDGES.at(0, i + 1, j), :] = near_ref[rows : rows + 8, :]
                out[EDGES.at(1, i, j), :] = near_ref[rows + 24 : rows + 32, :]
    set_up(EDGES, band, consts, bbed, bman, row0, col0)
    sums = add_band_edges(sum_ref, bqs_ref)
    run_steps(STEPS // 2, EDGES, band, consts, beast, row0, col0, sums)
    for j in range(PANELS):
        strip = slice(STRIP + 8 * j, STRIP + 8 * j + 8)
        for p, flow in ((EDGES.at(0, 0, j), north_ref[strip, :]), (EDGES.at(1, 3, j), south_ref[strip, :])):
            bs_ref[p, :] = bs_ref[p, :] + flow
        for i in range(3):
            for g, p in ((0, EDGES.at(0, i + 1, j)), (1, EDGES.at(1, i, j))):
                rows = 24 * (2 * j + g) + 8 * i
                bs_ref[p, :] = bs_ref[p, :] + in_ref[rows : rows + 8, :]
    run_steps(STEPS - STEPS // 2, EDGES, band, consts, beast, row0, col0, sums)
    pairs = []
    for n, out in enumerate((depth_out, qe_out, qs_out)):
        for g, i in ((0, 1), (1, 2)):
            to = slice(16 * n + 8 * g, 16 * n + 8 * g + 8)
            for j in range(4):
                p = EDGES.at(g, i, j)
                tile_ref[to, 128 * j : 128 * j + 128] = bs_ref[p, :] - bbed[p, :] if n == 0 else band[n][p, :]
            rows = slice(0, 8) if g == 0 else slice(TR - 8, TR)
            pairs.append((tile_ref.at[to, :], out.at[rows, :]))
    stored = copies(sem, pairs)
    for n in range(2):
        edge_ref[TR * n : TR * n + 8, :] = sum_ref[8 * n : 8 * n + 8, :]
        edge_ref[TR * n + TR - 8 : TR * n + TR, :] = sum_ref[16 + 8 * n : 24 + 8 * n, :]
    we_ref[0:1, :] = edge_ref[TR : 2 * TR, :].T[127:128, :]
    we_ref[1:2, :] = edge_ref[0:TR, :].T[127:128, :]
    for j in range(4):
        for g in range(2):
            row = 32 + 8 * (4 * g + j) + 7
            ns_ref[g : g + 1, 128 * j : 128 * j + 128] = sum_ref[row : row + 1, :]
    wait(stored)


def last_call(tiles, north, south, near, flow, edge):
    strip = pltpu.VMEM((STRIP + PANELS * 8, 128), F32)
    return pl.pallas_call(
        last_kernel,
        out_shape=(array(TR, TC), array(TR, TC), array(TR, TC), array(2, TR), array(2, TC)),
        in_specs=[HBM] * 8,
        out_specs=(HBM, HBM, HBM, VMEM, VMEM),
        scratch_shapes=[strip, strip]
        + [pltpu.VMEM((n, 128), F32) for n in (NEAR, 2 * PANELS * 24, 2 * TR)]
        + [pltpu.VMEM((BANDS, 128), F32)] * 10
        + [pltpu.VMEM((SUMS, 128), F32), pltpu.VMEM((48, TC), F32)]
        + [pltpu.SemaphoreType.DMA((4 + 2 * PANELS,)), pltpu.SemaphoreType.DMA((6,))],
        input_output_aliases={0: 0, 1: 1, 2: 2},
        compiler_params=params(FULL),
        name="last_steps",
    )(*tiles, north, south, near, flow, edge)


def shift(first, second, axis):
    count = lax.axis_size(axis)
    ahead = [(i, i + 1) for i in range(count - 1)]
    back = [(j, i) for i, j in ahead]
    return lax.ppermute(first, axis, ahead), lax.ppermute(second, axis, back)


def local(
    soil_water, conduct, rainfall, infil_cap, live_counts, send_slot, recv_row,
    bed_height, manning, depth_in, east_in, south_in, wet_mask,
):
    rain = rainfall.reshape(NB, 128)
    cap = infil_cap.reshape(NB, 128)
    soil = soil_water.reshape(2, 8, NB, 128).transpose(0, 2, 1, 3).reshape(NB * NL, 128)
    fields = (depth_in, wet_mask, bed_height, manning, east_in, south_in)

    sent, pond, recv = send_call(live_counts, send_slot, recv_row, rain, cap, depth_in, wet_mask, soil)
    got = lax.all_to_all(sent.reshape(DEV, 1, K * 128), ALL, split_axis=0, concat_axis=0, tiled=True)
    got = got.reshape(DEV * K, 128)

    to_west, to_east = cols_call(recv, fields)
    west, east = shift(to_east, to_west, "gx")
    *state, edge, prep, near = first_call(west, east, recv, pond, fields)

    flow, up, down = inflow_call(got, prep)
    north, south = shift(down, up, ROWS)
    *tiles, edge, soil_out = middle_call(
        live_counts, flow, state, edge, bed_height, send_slot, rain, cap, soil, conduct
    )
    depth, east_q, south_q, edge_we, edge_ns = last_call(tiles, north, south, near, flow, edge)
    soil_out = soil_out.reshape(2, NB, 8, 128).transpose(0, 2, 1, 3).reshape(NL, LAND)
    return soil_out, depth, east_q, south_q, edge_we, edge_ns


def solution(mesh):
    placed = (
        P(None, ALL),
        P(None, ALL),
        P(ALL),
        P(ALL),
        P(ALL),
        P(ALL, None),
        P(ALL, None),
    ) + (P(ROWS, "gx"),) * 6
    return jax.shard_map(
        local,
        mesh=mesh,
        in_specs=placed,
        out_specs=(
            P(None, ALL),
            P(ROWS, "gx"),
            P(ROWS, "gx"),
            P(ROWS, "gx"),
            P("gx", ROWS),
            P(ROWS, "gx"),
        ),
        check_vma=False,
    )
```

```python
import jax
import jax.numpy as jnp
from jax import lax
from jax.experimental import pallas as pl
from jax.experimental.pallas import tpu as pltpu
from jax.sharding import PartitionSpec as P

F32 = jnp.float32
BF16 = jnp.bfloat16

NL = 16
STEPS = 8
TR = 256
TC = 512
NB = 192
LAND = NB * 128
DEV = 256
HALO = 8
K = 7
PANELS = 5
SPAN = TR + 16
EXT = PANELS * SPAN
BAND = 48
BANDS = 2 * PANELS * BAND
STRIP = 5 * PANELS * 8
NEAR = 5 * PANELS * 2 * 24
PREP = 2 * DEV + TR + 16 + 8
SHELF = PREP + 2 * STRIP
FLOW = PANELS * TR + 2 * DEV + 8
MEAN_LANE = 40
FULL = 63

gravity = 9.81
cell_size = 30.0
time_step = 2.5
depth_floor = 0.25
half_rate = 0.5
lateral_rate = 0.2
drainage = 0.05
slope_coef = gravity * time_step / cell_size
fric_coef = gravity * time_step

ROWS = ("grp", "gy")
ALL = ("grp", "gy", "gx")
VMEM = pl.BlockSpec(memory_space=pltpu.VMEM)
SMEM = pl.BlockSpec(memory_space=pltpu.SMEM)
HBM = pl.BlockSpec(memory_space=pltpu.HBM)
ANY = pl.BlockSpec(memory_space=pl.ANY)


def params(mib):
    return pltpu.CompilerParams(vmem_limit_bytes=mib * 1024 * 1024)


def array(*shape):
    return jax.ShapeDtypeStruct(shape, F32)


def iota(shape, dim):
    return lax.broadcasted_iota(jnp.int32, shape, dim)


def copies(sem, pairs):
    made = [pltpu.make_async_copy(src, dst, sem.at[n]) for n, (src, dst) in enumerate(pairs)]
    for c in made:
        c.start()
    return made


def wait(made):
    for c in made:
        c.wait()


def parts(x):
    high = x.astype(BF16)
    low = (x - high.astype(F32)).astype(BF16)
    return high, low


def hot_dot(hot, x):
    both = jnp.dot(hot, jnp.concatenate(parts(x), axis=1), preferred_element_type=F32)
    return both[:, :128] + both[:, 128:]


def as_hot(mask):
    return mask.astype(F32).astype(BF16)


def twice(col):
    return jnp.concatenate([col, col], axis=1)


def turned(row):
    return jnp.broadcast_to(row, (128, row.shape[1])).T


def send_kernel(
    live_ref, slot_hbm, recv_hbm, rain_hbm, cap_hbm, depth_hbm, wet_hbm, soil_hbm,
    out_hbm, pond_hbm, recv_out,
    soil_ref, slot_ref, recv_ref, rain_ref, cap_ref, depth_ref, wet_ref, out_ref, pond_ref, tmp_ref, sem, sem_out,
):
    got = copies(
        sem,
        (
            (slot_hbm, slot_ref), (rain_hbm, rain_ref), (cap_hbm, cap_ref),
            (recv_hbm, recv_ref), (depth_hbm, depth_ref), (wet_hbm, wet_ref),
            (soil_hbm.at[NB * 8 : NB * 16, :], soil_ref),
        ),
    )
    live = live_ref[0]
    wait(got[:3])
    cell = iota((NB, 128), 0) * 128 + iota((NB, 128), 1)
    rain = jnp.where(cell < live, rain_ref[...], 0.0)
    rhs = jnp.concatenate(parts(rain) + parts(cap_ref[...]), axis=1)
    slot = slot_ref[...]
    tile = iota((DEV, NB), 0)
    lane = iota((DEV, 128), 1)
    for_west = jnp.zeros((DEV, 128), F32)
    for_east = jnp.zeros((DEV, 128), F32)
    for k in range(2):
        res = jnp.dot(as_hot(slot == 2 * tile + k), rhs, preferred_element_type=F32)
        for a in range(2):
            block = res[:, 256 * a : 256 * a + 128] + res[:, 256 * a + 128 : 256 * a + 256]
            out_ref[pl.ds(2 * a + k, DEV, stride=K), :] = block
            g = 2 * a + k
            low, high = 124 - 8 * g, 8 * g
            moved_w = pltpu.roll(block, (128 - 8 * g) % 128, 1) if g else block
            moved_e = pltpu.roll(block, 8 * g, 1) if g else block
            for_west = jnp.where((lane >= low) & (lane < low + 4), moved_w, for_west)
            for_east = jnp.where((lane >= high) & (lane < high + 4), moved_e, for_east)
    edge = jnp.where(lane < 64, pltpu.roll(for_east, DEV - 1, 0), pltpu.roll(for_west, 1, 0))
    wait(got[3:])
    half = NB * 8
    which = iota((half, 128), 0) // 8 * 128 + iota((half, 128), 1)
    kept = jnp.where(which < live, soil_ref[...], 0.0)
    mean = jnp.sum(jnp.sum(kept.reshape(half // 8, 8, 128), axis=0)) / (live.astype(F32) * 8.0)
    out_ref[pl.ds(6, DEV, stride=K), :] = jnp.where(lane == MEAN_LANE, mean, edge)
    tmp_ref[...] = turned(recv_ref[...].astype(F32))
    fields = []
    for c in range(4):
        cols = slice(128 * c, 128 * c + 128)
        fields.append(jnp.concatenate(parts(depth_ref[:, cols] * wet_ref[:, cols].astype(F32)), axis=1))
    place4 = iota((DEV, 256), 1).astype(F32) * 4.0
    recv_out[4:8, :] = jnp.zeros((4, 128), F32)
    for k in range(2):
        col = tmp_ref[pl.ds(k, DEV, stride=2), :]
        recv_out[2 * k : 2 * k + 1, :] = col[:128].T[0:1]
        recv_out[2 * k + 1 : 2 * k + 2, :] = col[128:].T[0:1]
        wide = twice(col)
        acc = jnp.zeros((DEV, 256), F32)
        for c in range(4):
            acc = acc + jnp.dot(as_hot(wide == place4 + float(c)), fields[c], preferred_element_type=F32)
        pond = acc[:, :128] + acc[:, 128:]
        out_ref[pl.ds(4 + k, DEV, stride=K), :] = pond
        pond_ref[DEV * k : DEV * k + DEV, :] = pond
    wait(copies(sem_out, ((out_ref, out_hbm), (pond_ref, pond_hbm))))


def send_call(live, slot, recv, rain, cap, depth, wet, soil):
    return pl.pallas_call(
        send_kernel,
        out_shape=(array(DEV * K, 128), array(2 * DEV, 128), array(8, 128)),
        in_specs=[SMEM] + [HBM] * 7,
        out_specs=(HBM, HBM, VMEM),
        scratch_shapes=[
            pltpu.VMEM((NB * 8, 128), F32),
            pltpu.VMEM((1, NB), jnp.int32),
            pltpu.VMEM((1, 2 * DEV), jnp.int32),
            pltpu.VMEM((NB, 128), F32),
            pltpu.VMEM((NB, 128), F32),
            pltpu.VMEM((TR, TC), F32),
            pltpu.VMEM((TR, TC), jnp.int32),
            pltpu.VMEM((DEV * K, 128), F32),
            pltpu.VMEM((2 * DEV, 128), F32),
            pltpu.VMEM((2 * DEV, 128), F32),
            pltpu.SemaphoreType.DMA((7,)),
            pltpu.SemaphoreType.DMA((2,)),
        ],
        compiler_params=params(FULL),
        name="message",
    )(live, slot, recv, rain, cap, depth, wet, soil)


def cols_kernel(
    recv_hbm, depth, wet, bed, man, qe, qs,
    to_west, to_east,
    west_ref, east_ref, wet_w, wet_e, sem,
):
    left, right = slice(0, 128), slice(TC - 128, TC)
    pairs = [(wet.at[:, left], wet_w), (wet.at[:, right], wet_e)]
    for n, f in enumerate((depth, bed, man, qe, qs)):
        rows = slice(TR * n, TR * n + TR)
        pairs.append((f.at[:, left], west_ref.at[rows, :]))
        pairs.append((f.at[:, right], east_ref.at[rows, :]))
    pairs.append((recv_hbm, to_west.at[TR : TR + 8, :]))
    pairs.append((recv_hbm, to_east.at[TR : TR + 8, :]))
    got = copies(sem, pairs)
    wait(got)
    lane = iota((TR, 128), 1)
    for src, mask, out, first in ((west_ref, wet_w, to_west, 0), (east_ref, wet_e, to_east, 120)):
        acc = jnp.zeros((TR, 128), F32)
        for n in range(5):
            own = src[TR * n : TR * n + TR, :]
            if n == 0:
                own = own * mask[...].astype(F32)
            shift = (8 * n - first) % 128
            moved = pltpu.roll(own, shift, 1) if shift else own
            acc = jnp.where((lane >= 8 * n) & (lane < 8 * n + 8), moved, acc)
        out[0:TR, :] = acc


def cols_call(recv, fields):
    return pl.pallas_call(
        cols_kernel,
        out_shape=(array(TR + 8, 128), array(TR + 8, 128)),
        in_specs=[HBM] * 7,
        scratch_shapes=[
            pltpu.VMEM((5 * TR, 128), F32),
            pltpu.VMEM((5 * TR, 128), F32),
            pltpu.VMEM((TR, 128), jnp.int32),
            pltpu.VMEM((TR, 128), jnp.int32),
            pltpu.SemaphoreType.DMA((14,)),
        ],
        compiler_params=params(FULL),
        name="column_strips",
    )(recv, *fields)


def inflow_kernel(after_any, got_ref, prep_ref, flow_hbm, up_ref, down_ref, flow_ref, sem):
    in_ref = flow_ref.at[0 : PANELS * TR, :]
    land_ref = flow_ref.at[PANELS * TR : FLOW, :]
    up_ref[0:STRIP, :] = prep_ref[PREP : PREP + STRIP, :]
    down_ref[0:STRIP, :] = prep_ref[PREP + STRIP : SHELF, :]
    for k in range(2):
        land_ref[DEV * k : DEV * k + DEV, :] = got_ref[pl.ds(4 + k, DEV, stride=K), :]
    n_rows, n_cols = lax.axis_size(ROWS), lax.axis_size("gx")
    my_row, my_col = lax.axis_index(ROWS), lax.axis_index("gx")
    here = my_row * n_cols + my_col

    def note_of(device):
        return got_ref[pl.ds(jnp.clip(device, 0, DEV - 1) * K + 6, 1), :]

    mean = note_of(here)
    lat = jnp.where(my_row > 0, note_of(here - n_cols) - mean, 0.0)
    lat = lat + jnp.where(my_row < n_rows - 1, note_of(here + n_cols) - mean, 0.0)
    lat = lat + jnp.where(my_col > 0, note_of(here - 1) - mean, 0.0)
    lat = lat + jnp.where(my_col < n_cols - 1, note_of(here + 1) - mean, 0.0)
    lat = jnp.sum(jnp.where(iota((1, 128), 1) == MEAN_LANE, lat, 0.0), axis=1, keepdims=True)
    land_ref[2 * DEV : 2 * DEV + 8, :] = jnp.broadcast_to(lateral_rate * lat, (8, 128))
    lane = iota((DEV, 128), 1)
    place4 = iota((TR, DEV), 0).astype(F32) * 4.0

    def runoff(rain, cap, pond):
        wetting = rain + jnp.maximum(pond, 0.0)
        return rain * (1.0 - cap / (wetting + half_rate))

    def line(k, base):
        at = base + 2 * k
        return jnp.concatenate([prep_ref[at : at + 1, :], prep_ref[at + 1 : at + 2, :]], axis=1)

    note, own = 2 * DEV + TR, PREP - 8
    flows = []
    for k in range(2):
        rain = got_ref[pl.ds(k, DEV, stride=K), :]
        cap = got_ref[pl.ds(2 + k, DEV, stride=K), :]
        flow = runoff(rain, cap, prep_ref[DEV * k : DEV * k + DEV, :])
        flows.append(jnp.concatenate(parts(flow), axis=1))
    for c in range(4):
        acc = jnp.zeros((TR, 256), F32)
        for k in range(2):
            hot = as_hot(line(k, own) == place4 + float(c))
            acc = acc + jnp.dot(hot, flows[k], preferred_element_type=F32)
        in_ref[TR * c : TR * c + TR, :] = acc[:, :128] + acc[:, 128:]
    parts_of = (slice(0, 4 * TR), slice(PANELS * TR, FLOW))
    stored = copies(sem, [(flow_ref.at[rows, :], flow_hbm.at[rows, :]) for rows in parts_of])

    edge = got_ref[pl.ds(6, DEV, stride=K), :]
    depth = prep_ref[2 * DEV : 2 * DEV + TR, :]
    lane_place = iota((DEV, TR), 1).astype(F32) * 4.0
    is_east, is_west = lane < 4, lane >= 124
    acc = jnp.zeros((TR, 128), F32)

    def pick(g):
        if g == 0:
            return edge
        return jnp.where(lane < 64, pltpu.roll(edge, 128 - 8 * g, 1), pltpu.roll(edge, 8 * g, 1))

    sides = ((note, 3, is_west), (note + 8, 0, is_east))
    for k in range(2):
        rain, cap = pick(k), pick(2 + k)
        pond = jnp.zeros((DEV, 128), F32)
        for base, c, mask in sides:
            col = twice(turned(line(k, base)))
            pond = jnp.where(mask, hot_dot(as_hot(col == lane_place + float(c)), depth), pond)
        flow = jnp.where(is_east | is_west, runoff(rain, cap, pond), 0.0)
        for base, c, mask in sides:
            hot = as_hot(line(k, base) == place4 + float(c))
            acc = acc + hot_dot(hot, jnp.where(mask, flow, 0.0))
    acc = jnp.where(is_west & (my_col > 0), acc, jnp.where(is_east & (my_col < n_cols - 1), acc, 0.0))
    side_rows = slice(4 * TR, 5 * TR)
    in_ref[side_rows, :] = acc
    stored.append(pltpu.make_async_copy(flow_ref.at[side_rows, :], flow_hbm.at[side_rows, :], sem.at[2]))
    stored[-1].start()
    for j in range(PANELS):
        to = slice(STRIP + 8 * j, STRIP + 8 * j + 8)
        up_ref[to, :] = in_ref[TR * j : TR * j + 8, :]
        down_ref[to, :] = in_ref[TR * j + TR - 8 : TR * j + TR, :]
    wait(stored)


def inflow_call(after, got, prep):
    strip = array(STRIP + PANELS * 8, 128)
    return pl.pallas_call(
        inflow_kernel,
        out_shape=(array(FLOW, 128), strip, strip),
        in_specs=[ANY, VMEM, VMEM],
        out_specs=(HBM, VMEM, VMEM),
        scratch_shapes=[pltpu.VMEM((FLOW, 128), F32), pltpu.SemaphoreType.DMA((3,))],
        compiler_params=params(52),
        name="inflow",
    )(after, got, prep)


class Grid:
    def __init__(self, bases, tiles, rows):
        self.bases, self.tiles, self.rows = bases, tiles, rows
        self.all = [(g, i) for g in range(len(bases)) for i in range(tiles)]

    def at(self, g, i, j, shift=0):
        start = self.bases[g][j] + 8 + 8 * i + shift
        return slice(start, start + 8)

    def south_open(self, g, i, row0):
        row = row0 + self.rows[g] + 8 * i + iota((8, 128), 0)
        return (row >= 0) & (row + 1 <= TR * lax.axis_size(ROWS) - 1)


BULK = Grid([[j * SPAN for j in range(PANELS)]], TR // 8, [0])
EDGES = Grid([[(PANELS * g + j) * BAND for j in range(PANELS)] for g in range(2)], 4, [-8, TR - 24])
EDGES_LATE = Grid([EDGES.bases[0], [b + 8 for b in EDGES.bases[1]]], 3, [-8, TR - 16])


def east_open(j, col0):
    lane = iota((8, 128), 1)
    if j < 4:
        col = col0 + 128 * j + lane
    else:
        col = col0 + jnp.where(lane < 64, TC + lane, lane - 128)
    return (col >= 0) & (col + 1 <= TC * lax.axis_size("gx") - 1)


def shifted(values, shift, lane, offset):
    moved = [pltpu.roll(v, shift, 1) for v in values]
    edge = iota((8, 128), 1) == lane
    return [jnp.where(edge, moved[(j + offset) % PANELS], moved[j]) for j in range(PANELS)]


def run_steps(count, grid, state, consts, east_ref, row0, col0, after):
    s_ref, qe_ref, qs_ref = state
    mbe_ref, cre_ref, mbs_ref, crs_ref = consts
    ge = [jnp.where(east_open(j, col0), slope_coef, 0.0).astype(F32) for j in range(PANELS)]

    def flux(q, a, b, mb, cr, g):
        h = jnp.maximum(jnp.maximum(a, b) - mb, depth_floor)
        numer = q - g * (h * (b - a))
        power = jnp.exp2(jnp.log(h) * F32(-7.0 / 3.0 / 0.6931471805599453))
        return numer * pltpu.reciprocal(1.0 + cr * jnp.abs(q) * power, approx=True)

    def one_step(_, c0):
        for g, i in grid.all:
            moved = shifted([s_ref[grid.at(g, i, j), :] for j in range(PANELS)], 127, 127, 1)
            for j in range(PANELS):
                east_ref[grid.at(g, i, j), :] = moved[j]
        for g, i in grid.all:
            gs = jnp.where(grid.south_open(g, i, row0), slope_coef, 0.0).astype(F32)
            for j in range(PANELS):
                p = grid.at(g, i, j)
                s = s_ref[p, :]
                qe_ref[p, :] = flux(qe_ref[p, :], s, east_ref[p, :], mbe_ref[p, :], cre_ref[p, :], ge[j])
                qs_ref[p, :] = flux(qs_ref[p, :], s, s_ref[grid.at(g, i, j, 1), :], mbs_ref[p, :], crs_ref[p, :], gs)
        for g, i in grid.all:
            qe = [qe_ref[grid.at(g, i, j), :] for j in range(PANELS)]
            west = shifted(qe, 1, 0, PANELS - 1)
            for j in range(PANELS):
                p = grid.at(g, i, j)
                change = (qe[j] - west[j]) + (qs_ref[p, :] - qs_ref[grid.at(g, i, j, -1), :])
                s_ref[p, :] = s_ref[p, :] - F32(time_step / cell_size) * change
            after(g, i, qe)
        return c0

    lax.fori_loop(0, count, one_step, 0)


def set_up(grid, state, consts, bed_ref, man_ref, row0, col0):
    s_ref, qe_ref, qs_ref = state
    mbe_ref, cre_ref, mbs_ref, crs_ref = consts
    open_e = east_open(3, col0)
    for g, i in grid.all:
        bed = [bed_ref[grid.at(g, i, j), :] for j in range(PANELS)]
        man = [man_ref[grid.at(g, i, j), :] for j in range(PANELS)]
        bed_e, man_e = shifted(bed, 127, 127, 1), shifted(man, 127, 127, 1)
        for j in range(PANELS):
            p = grid.at(g, i, j)
            mbe_ref[p, :] = jnp.maximum(bed[j], bed_e[j])
            mbs_ref[p, :] = jnp.maximum(bed[j], bed_ref[grid.at(g, i, j, 1), :])
            rough_e = 0.5 * (man[j] + man_e[j])
            rough_s = 0.5 * (man[j] + man_ref[grid.at(g, i, j, 1), :])
            cre_ref[p, :] = fric_coef * rough_e * rough_e
            crs_ref[p, :] = fric_coef * rough_s * rough_s
            s_ref[p, :] = s_ref[p, :] + bed[j]
        qe_ref[grid.at(g, i, 3), :] = jnp.where(open_e, qe_ref[grid.at(g, i, 3), :], 0.0)
        if grid.rows[g] + 8 * i == TR - 8:
            for j in range(PANELS):
                p = grid.at(g, i, j)
                qs_ref[p, :] = jnp.where(grid.south_open(g, i, row0), qs_ref[p, :], 0.0)


def clear_guards(grid, refs):
    zero = jnp.zeros((8, 128), F32)
    for ref in refs:
        for g in range(len(grid.bases)):
            for j in range(PANELS):
                ref[grid.at(g, -1, j), :] = zero
                ref[grid.at(g, grid.tiles, j), :] = zero


def place():
    return lax.axis_index(ROWS) * TR, lax.axis_index("gx") * TC


def add_bulk_edges(edge_ref):
    def after(g, i, qe):
        for n in range(2):
            rows = slice(TR * n + 8 * i, TR * n + 8 * i + 8)
            edge_ref[rows, :] = edge_ref[rows, :] + qe[3 + n]

    return after


def add_band_edges(grid, sum_ref, qs_ref):
    def after(g, i, qe):
        if grid.rows[g] + 8 * i in (0, TR - 8):
            for n in range(2):
                rows = slice(16 * g + 8 * n, 16 * g + 8 * n + 8)
                sum_ref[rows, :] = sum_ref[rows, :] + qe[3 + n]
        if grid.rows[g] + 8 * i == (-8, TR - 8)[g]:
            for j in range(4):
                rows = slice(32 + 8 * (4 * g + j), 40 + 8 * (4 * g + j))
                sum_ref[rows, :] = sum_ref[rows, :] + qs_ref[grid.at(g, i, j), :]

    return after


SUMS = 32 + 64


def first_kernel(
    west_hbm, east_hbm, recv_hbm, pond_hbm, depth_hbm, wet_hbm, bed_hbm, man_hbm, qe_hbm, qs_hbm,
    s_out, qe_out, qs_out, mbe_out, cre_out, mbs_out, crs_out, edge_out, prep_out, near_out,
    s_ref, qe_ref, qs_ref, mbe_ref, cre_ref, mbs_ref, crs_ref, edge_ref, prep_ref, near_ref,
    bed_x, man_x, wet_ref, east_x, west_ref, east_ref, sem, sem_out,
):
    pairs = [
        (west_hbm, west_ref), (east_hbm, east_ref),
        (recv_hbm, prep_ref.at[PREP - 8 : PREP, :]), (pond_hbm, prep_ref.at[0 : 2 * DEV, :]), (wet_hbm, wet_ref),
    ]
    targets = (s_ref, bed_x, man_x, qe_ref, qs_ref)
    for n, src in enumerate((depth_hbm, bed_hbm, man_hbm, qe_hbm, qs_hbm)):
        for j in range(4):
            to = targets[n].at[j * SPAN + 8 : j * SPAN + 8 + TR, :]
            pairs.append((src.at[:, 128 * j : 128 * j + 128], to))
    got = copies(sem, pairs)
    row0, col0 = place()
    state, consts = (s_ref, qe_ref, qs_ref), (mbe_ref, cre_ref, mbs_ref, crs_ref)
    clear_guards(BULK, targets + consts)
    edge_ref[...] = jnp.zeros((2 * TR, 128), F32)
    wait(got[:2])
    lane = iota((TR, 128), 1)
    for n, ref in enumerate(targets):
        shift = (128 - 8 * n) % 128
        e, w = east_ref[0:TR, :], west_ref[0:TR, :]
        e = pltpu.roll(e, shift, 1) if shift else e
        w = pltpu.roll(w, 120 - 8 * n, 1)
        beside = jnp.where(lane < 8, e, jnp.where(lane >= 120, w, 0.0))
        ref[4 * SPAN + 8 : 4 * SPAN + 8 + TR, :] = beside
        if n == 0:
            prep_ref[2 * DEV : 2 * DEV + TR, :] = beside
    note = 2 * DEV + TR
    prep_ref[note : note + 8, :] = west_ref[TR : TR + 8, :]
    prep_ref[note + 8 : note + 16, :] = east_ref[TR : TR + 8, :]
    wait(got[2:])
    stored = []
    for j in range(4):
        own = slice(j * SPAN + 8, j * SPAN + 8 + TR)
        s_ref[own, :] = s_ref[own, :] * wet_ref[:, 128 * j : 128 * j + 128].astype(F32)
    for n, ref in enumerate(targets):
        for j in range(PANELS):
            at = PANELS * n + j
            base = j * SPAN + 8
            near_ref[48 * at : 48 * at + 24, :] = ref[base : base + 24, :]
            near_ref[48 * at + 24 : 48 * at + 48, :] = ref[base + TR - 24 : base + TR, :]
            up, down = PREP + 8 * at, PREP + STRIP + 8 * at
            prep_ref[up : up + 8, :] = ref[base : base + 8, :]
            prep_ref[down : down + 8, :] = ref[base + TR - 8 : base + TR, :]

    def store(pairs):
        for src, dst in pairs:
            stored.append(pltpu.make_async_copy(src, dst, sem_out.at[len(stored)]))
            stored[-1].start()

    store(((prep_ref, prep_out), (near_ref, near_out)))
    set_up(BULK, state, consts, bed_x, man_x, row0, col0)
    store(zip(consts, (mbe_out, cre_out, mbs_out, crs_out)))
    run_steps(STEPS // 2, BULK, state, consts, east_x, row0, col0, add_bulk_edges(edge_ref))
    store(zip(state + (edge_ref,), (s_out, qe_out, qs_out, edge_out)))
    wait(stored)


def first_call(west, east, recv, pond, fields):
    ext = array(EXT, 128)
    buffer, message = pltpu.VMEM((EXT, 128), F32), pltpu.VMEM((TR + 8, 128), F32)
    extra = (2 * TR, SHELF, NEAR)
    return pl.pallas_call(
        first_kernel,
        out_shape=(ext,) * 7 + tuple(array(n, 128) for n in extra),
        in_specs=[HBM] * 10,
        out_specs=(HBM,) * 10,
        scratch_shapes=[buffer] * 7
        + [pltpu.VMEM((n, 128), F32) for n in extra]
        + [buffer, buffer, pltpu.VMEM((TR, TC), jnp.int32), buffer, message, message]
        + [pltpu.SemaphoreType.DMA((25,)), pltpu.SemaphoreType.DMA((10,))],
        compiler_params=params(FULL),
        name="first_steps",
    )(west, east, recv, pond, *fields)


CHUNK = 16
CHUNKS = NB // CHUNK


def soil_rows(layer, block):
    return pl.ds((layer // 8) * (NB * 8) + block * 8 + layer % 8, 8, stride=8)


def columns_kernel(
    after_any, live_ref, soil_hbm, cond_hbm,
    base_hbm, top_hbm, low_hbm,
    soil_ref, cond_ref, cond_x, base_ref, top_ref, low_ref, sem, sem_out,
):
    pairs = []
    half = NB * 8
    for c in range(CHUNKS):
        cols = slice(c * CHUNK * 128, (c + 1) * CHUNK * 128)
        pairs.append((cond_hbm.at[:, cols], cond_ref.at[:, cols]))
        for h in range(2):
            rows = slice(h * half + c * CHUNK * 8, h * half + (c + 1) * CHUNK * 8)
            pairs.append((soil_hbm.at[rows, :], soil_ref.at[rows, :]))
    moved = copies(sem, pairs)
    live = live_ref[0]
    sub, lane = iota((8, 128), 0), iota((8, 128), 1)
    group = range(CHUNK // 8)
    for c in range(CHUNKS):
        wait(moved[3 * c : 3 * c + 3])
        for b in range(c * CHUNK, (c + 1) * CHUNK):
            cond_x[16 * b : 16 * b + 16, :] = cond_ref[:, 128 * b : 128 * b + 128].astype(F32)
        blocks = [c * CHUNK + 8 * g for g in group]
        kept = [(b + sub) * 128 + lane < live for b in blocks]
        mark = [k.astype(F32) for k in kept]

        def cond_at(g, layer):
            return cond_x[pl.ds(blocks[g] * 16 + layer, 8, stride=16), :]

        def out_at(g, layer):
            return slice(layer * NB + blocks[g], layer * NB + blocks[g] + 8)

        ratios = [[] for _ in group]
        above = [None for _ in group]
        base = [[] for _ in group]
        top = [[] for _ in group]
        low = [[] for _ in group]
        cond = [cond_at(g, 0) for g in group]
        for j in range(NL):
            for g in group:
                center = 1.0 if j < NL - 1 else 1.0 + drainage
                if j > 0:
                    center = center + (above[g] + above[g] * ratios[g][-1])
                if j < NL - 1:
                    below = cond_at(g, j + 1)
                    face = 0.5 * (cond[g] + below)
                    cond[g] = below
                    center = center + face
                r = pltpu.reciprocal(center, approx=True)
                value = soil_ref[soil_rows(j, blocks[g]), :] * r
                if j == 0:
                    top[g].append(mark[g] * r)
                else:
                    carry = above[g] * r
                    value = value + carry * base[g][-1]
                    top[g].append(carry * top[g][-1])
                base[g].append(value)
                if j == 8:
                    low[g].append(mark[g] * r)
                if j > 8:
                    low[g].append(mark[g] * r + carry * low[g][-1])
                if j < NL - 1:
                    ratios[g].append(-face * r)
                    above[g] = face
        x = [base[g][-1] for g in group]
        u = [top[g][-1] for g in group]
        v = [low[g][-1] for g in group]
        for j in range(NL - 1, -1, -1):
            for g in group:
                if j < NL - 1:
                    ratio = ratios[g][j]
                    x[g] = base[g][j] - ratio * x[g]
                    u[g] = top[g][j] - ratio * u[g]
                    v[g] = (low[g][j - 8] - ratio * v[g]) if j >= 8 else -ratio * v[g]
                base_ref[out_at(g, j), :] = jnp.where(kept[g], x[g], soil_ref[soil_rows(j, blocks[g]), :])
                top_ref[out_at(g, j), :] = u[g]
                low_ref[out_at(g, j), :] = v[g]
    wait(copies(sem_out, ((base_ref, base_hbm), (top_ref, top_hbm), (low_ref, low_hbm))))


def columns_call(after, live, soil, cond):
    layers = array(NB * NL, 128)
    buffer = pltpu.VMEM((NB * NL, 128), F32)
    return pl.pallas_call(
        columns_kernel,
        out_shape=(layers,) * 3,
        in_specs=[ANY, SMEM, HBM, HBM],
        out_specs=(HBM,) * 3,
        scratch_shapes=[buffer, pltpu.VMEM((NL, LAND), BF16), buffer, buffer, buffer, buffer]
        + [pltpu.SemaphoreType.DMA((3 * CHUNKS,)), pltpu.SemaphoreType.DMA((3,))],
        compiler_params=params(FULL),
        name="soil_columns",
    )(after, live, soil, cond)


PARTS = 4


def land_part(land_ref, slot_ref, rain_ref, cap_ref, base_ref, top_ref, low_ref, out_hbm, soil_ref, sem_out):
    slot = jnp.broadcast_to(slot_ref[...].astype(F32), (128, NB))
    slot = jnp.concatenate([slot, jnp.full((128, 256 - NB), -1.0, F32)], axis=1).T
    slot = twice(slot[0:NB])
    tile2 = iota((NB, DEV), 1).astype(F32) * 2.0
    pond = jnp.zeros((NB, 128), F32)
    for k in range(2):
        pond = pond + hot_dot(as_hot(slot == tile2 + float(k)), land_ref[DEV * k : DEV * k + DEV, :])
    rain = rain_ref[...]
    wetting = rain + jnp.maximum(pond, 0.0)
    rain_ref[...] = cap_ref[...] * wetting * pltpu.reciprocal(wetting + half_rate, approx=True)
    lat = land_ref[2 * DEV : 2 * DEV + 8, :]
    stored = []
    share = NB // PARTS
    for c in range(PARTS):
        for b in range(c * share, (c + 1) * share, 8):
            uptake = rain_ref[b : b + 8, :]
            for j in range(NL):
                rows = slice(j * NB + b, j * NB + b + 8)
                x = base_ref[rows, :] + (uptake * top_ref[rows, :] + lat * low_ref[rows, :])
                soil_ref[soil_rows(j, b), :] = x
        for h in range(2):
            rows = slice(h * NB * 8 + c * share * 8, h * NB * 8 + (c + 1) * share * 8)
            stored.append(pltpu.make_async_copy(soil_ref.at[rows, :], out_hbm.at[rows, :], sem_out.at[2 * c + h]))
            stored[-1].start()
    return stored


def middle_kernel(
    flow_hbm, s_in, qe_in, qs_in, mbe_in, cre_in, mbs_in, crs_in, edge_in, bed_hbm,
    slot_hbm, rain_hbm, cap_hbm, base_hbm, top_hbm, low_hbm,
    depth_hbm, qe_hbm, qs_hbm, edge_hbm, soil_out,
    in_ref, s_ref, qe_ref, qs_ref, mbe_ref, cre_ref, mbs_ref, crs_ref, edge_ref, bed_ref,
    land_ref, slot_ref, rain_ref, cap_ref, base_ref, top_ref, low_ref, soil_ref,
    east_ref, sem_state, sem_land, sem_tiles, sem_out,
):
    state, consts = (s_ref, qe_ref, qs_ref), (mbe_ref, cre_ref, mbs_ref, crs_ref)
    in_hbm, land_hbm = flow_hbm.at[0 : PANELS * TR, :], flow_hbm.at[PANELS * TR : FLOW, :]
    sources = (s_in, in_hbm, qe_in, qs_in, mbe_in, cre_in, mbs_in, crs_in, edge_in, bed_hbm)
    loaded = copies(sem_state, list(zip(sources, (s_ref, in_ref, qe_ref, qs_ref) + consts + (edge_ref, bed_ref))))
    sources = (slot_hbm, rain_hbm, cap_hbm, land_hbm, base_hbm, top_hbm, low_hbm)
    land = copies(sem_land, list(zip(sources, (slot_ref, rain_ref, cap_ref, land_ref, base_ref, top_ref, low_ref))))
    row0, col0 = place()
    wait(loaded)
    for j in range(PANELS):
        own = slice(j * SPAN + 8, j * SPAN + 8 + TR)
        s_ref[own, :] = s_ref[own, :] + in_ref[TR * j : TR * j + TR, :]
    run_steps(STEPS - STEPS // 2, BULK, state, consts, east_ref, row0, col0, add_bulk_edges(edge_ref))
    pairs = [(edge_ref, edge_hbm)]
    for src, dst in ((qe_ref, qe_hbm), (qs_ref, qs_hbm)):
        for j in range(4):
            pairs.append((src.at[j * SPAN + 8 : j * SPAN + 8 + TR, :], dst.at[:, 128 * j : 128 * j + 128]))
    for j in range(4):
        cols = slice(128 * j, 128 * j + 128)
        bed_ref[:, cols] = s_ref[j * SPAN + 8 : j * SPAN + 8 + TR, :] - bed_ref[:, cols]
    pairs.append((bed_ref, depth_hbm))
    stored = copies(sem_tiles, pairs)
    wait(land)
    stored += land_part(land_ref, slot_ref, rain_ref, cap_ref, base_ref, top_ref, low_ref, soil_out, soil_ref, sem_out)
    wait(stored)


def middle_call(flow, state, edge, bed, slot, rain, cap, soil):
    tile = array(TR, TC)
    buffer = pltpu.VMEM((EXT, 128), F32)
    blocks, layers = pltpu.VMEM((NB, 128), F32), pltpu.VMEM((NB * NL, 128), F32)
    counts = (10, 7, 10, 2 * PARTS)
    return pl.pallas_call(
        middle_kernel,
        out_shape=(tile,) * 3 + (array(2 * TR, 128), array(NB * NL, 128)),
        in_specs=[HBM] * 16,
        out_specs=(HBM,) * 5,
        scratch_shapes=[pltpu.VMEM((PANELS * TR, 128), F32)]
        + [buffer] * 7
        + [pltpu.VMEM((2 * TR, 128), F32), pltpu.VMEM((TR, TC), F32), pltpu.VMEM((2 * DEV + 8, 128), F32)]
        + [pltpu.VMEM((1, NB), jnp.int32), blocks, blocks]
        + [layers] * 4
        + [buffer]
        + [pltpu.SemaphoreType.DMA((n,)) for n in counts],
        compiler_params=params(FULL),
        name="middle_steps",
    )(flow, *state, edge, bed, slot, rain, cap, *soil)


def last_kernel(
    depth_in, qe_in, qs_in, north_hbm, south_hbm, near_hbm, in_hbm, edge_hbm,
    depth_out, qe_out, qs_out, we_ref, ns_ref,
    north_ref, south_ref, near_ref, in_ref, edge_ref,
    bs_ref, bqe_ref, bqs_ref, bmbe, bcre, bmbs, bcrs, bbed, bman, beast, sum_ref, tile_ref, sem_in, sem,
):
    pairs = [(near_hbm, near_ref), (north_hbm, north_ref), (south_hbm, south_ref), (edge_hbm, edge_ref)]
    for j in range(PANELS):
        for g, start in ((0, 0), (1, TR - 24)):
            to = 24 * (2 * j + g)
            pairs.append((in_hbm.at[TR * j + start : TR * j + start + 24, :], in_ref.at[to : to + 24, :]))
    got = copies(sem_in, pairs)
    row0, col0 = place()
    band, consts = (bs_ref, bqe_ref, bqs_ref), (bmbe, bcre, bmbs, bcrs)
    targets = (bs_ref, bbed, bman, bqe_ref, bqs_ref)
    clear_guards(EDGES, targets + consts)
    sum_ref[...] = jnp.zeros((SUMS, 128), F32)
    wait(got)
    for n, out in enumerate(targets):
        for j in range(PANELS):
            at = PANELS * n + j
            strip = slice(8 * at, 8 * at + 8)
            out[EDGES.at(0, 0, j), :] = north_ref[strip, :]
            out[EDGES.at(1, 3, j), :] = south_ref[strip, :]
            for i in range(3):
                rows = 48 * at + 8 * i
                out[EDGES.at(0, i + 1, j), :] = near_ref[rows : rows + 8, :]
                out[EDGES.at(1, i, j), :] = near_ref[rows + 24 : rows + 32, :]
    set_up(EDGES, band, consts, bbed, bman, row0, col0)
    sums = add_band_edges(EDGES, sum_ref, bqs_ref)
    run_steps(STEPS // 2, EDGES, band, consts, beast, row0, col0, sums)
    for j in range(PANELS):
        strip = slice(STRIP + 8 * j, STRIP + 8 * j + 8)
        for p, flow in ((EDGES.at(0, 0, j), north_ref[strip, :]), (EDGES.at(1, 3, j), south_ref[strip, :])):
            bs_ref[p, :] = bs_ref[p, :] + flow
        for i in range(3):
            for g, p in ((0, EDGES.at(0, i + 1, j)), (1, EDGES.at(1, i, j))):
                rows = 24 * (2 * j + g) + 8 * i
                bs_ref[p, :] = bs_ref[p, :] + in_ref[rows : rows + 8, :]
    sums = add_band_edges(EDGES_LATE, sum_ref, bqs_ref)
    run_steps(STEPS - STEPS // 2, EDGES_LATE, band, consts, beast, row0, col0, sums)
    pairs = []
    for n, out in enumerate((depth_out, qe_out, qs_out)):
        for g, i in ((0, 1), (1, 2)):
            to = slice(16 * n + 8 * g, 16 * n + 8 * g + 8)
            for j in range(4):
                p = EDGES.at(g, i, j)
                tile_ref[to, 128 * j : 128 * j + 128] = bs_ref[p, :] - bbed[p, :] if n == 0 else band[n][p, :]
            rows = slice(0, 8) if g == 0 else slice(TR - 8, TR)
            pairs.append((tile_ref.at[to, :], out.at[rows, :]))
    stored = copies(sem, pairs)
    for n in range(2):
        edge_ref[TR * n : TR * n + 8, :] = sum_ref[8 * n : 8 * n + 8, :]
        edge_ref[TR * n + TR - 8 : TR * n + TR, :] = sum_ref[16 + 8 * n : 24 + 8 * n, :]
    we_ref[0:1, :] = edge_ref[TR : 2 * TR, :].T[127:128, :]
    we_ref[1:2, :] = edge_ref[0:TR, :].T[127:128, :]
    for j in range(4):
        for g in range(2):
            row = 32 + 8 * (4 * g + j) + 7
            ns_ref[g : g + 1, 128 * j : 128 * j + 128] = sum_ref[row : row + 1, :]
    wait(stored)


def last_call(tiles, north, south, near, flow, edge):
    strip = pltpu.VMEM((STRIP + PANELS * 8, 128), F32)
    return pl.pallas_call(
        last_kernel,
        out_shape=(array(TR, TC), array(TR, TC), array(TR, TC), array(2, TR), array(2, TC)),
        in_specs=[HBM] * 8,
        out_specs=(HBM, HBM, HBM, VMEM, VMEM),
        scratch_shapes=[strip, strip]
        + [pltpu.VMEM((n, 128), F32) for n in (NEAR, 2 * PANELS * 24, 2 * TR)]
        + [pltpu.VMEM((BANDS, 128), F32)] * 10
        + [pltpu.VMEM((SUMS, 128), F32), pltpu.VMEM((48, TC), F32)]
        + [pltpu.SemaphoreType.DMA((4 + 2 * PANELS,)), pltpu.SemaphoreType.DMA((6,))],
        input_output_aliases={0: 0, 1: 1, 2: 2},
        compiler_params=params(FULL),
        name="last_steps",
    )(*tiles, north, south, near, flow, edge)


def shift(first, second, axis):
    count = lax.axis_size(axis)
    ahead = [(i, i + 1) for i in range(count - 1)]
    back = [(j, i) for i, j in ahead]
    return lax.ppermute(first, axis, ahead), lax.ppermute(second, axis, back)


def local(
    soil_water, conduct, rainfall, infil_cap, live_counts, send_slot, recv_row,
    bed_height, manning, depth_in, east_in, south_in, wet_mask,
):
    rain = rainfall.reshape(NB, 128)
    cap = infil_cap.reshape(NB, 128)
    soil = soil_water.reshape(2, 8, NB, 128).transpose(0, 2, 1, 3).reshape(NB * NL, 128)
    fields = (depth_in, wet_mask, bed_height, manning, east_in, south_in)

    sent, pond, recv = send_call(live_counts, send_slot, recv_row, rain, cap, depth_in, wet_mask, soil)
    got = lax.all_to_all(sent.reshape(DEV, 1, K * 128), ALL, split_axis=0, concat_axis=0, tiled=True)
    got = got.reshape(DEV * K, 128)

    to_west, to_east = cols_call(recv, fields)
    west, east = shift(to_east, to_west, "gx")
    solved = columns_call(to_west, live_counts, soil, conduct)
    *state, edge, prep, near = first_call(west, east, recv, pond, fields)

    flow, up, down = inflow_call(solved[0], got, prep)
    north, south = shift(down, up, ROWS)
    *tiles, edge, soil_out = middle_call(
        flow, state, edge, bed_height, send_slot, rain, cap, solved
    )
    depth, east_q, south_q, edge_we, edge_ns = last_call(tiles, north, south, near, flow, edge)
    soil_out = soil_out.reshape(2, NB, 8, 128).transpose(0, 2, 1, 3).reshape(NL, LAND)
    return soil_out, depth, east_q, south_q, edge_we, edge_ns


def solution(mesh):
    placed = (
        P(None, ALL),
        P(None, ALL),
        P(ALL),
        P(ALL),
        P(ALL),
        P(ALL, None),
        P(ALL, None),
    ) + (P(ROWS, "gx"),) * 6
    return jax.shard_map(
        local,
        mesh=mesh,
        in_specs=placed,
        out_specs=(
            P(None, ALL),
            P(ROWS, "gx"),
            P(ROWS, "gx"),
            P(ROWS, "gx"),
            P("gx", ROWS),
            P(ROWS, "gx"),
        ),
        check_vma=False,
    )
```

```python
import jax
import jax.numpy as jnp
from jax import lax
from jax.experimental import pallas as pl
from jax.experimental.pallas import tpu as pltpu
from jax.sharding import PartitionSpec as P

F32 = jnp.float32
BF16 = jnp.bfloat16

NL = 16
STEPS = 8
TR = 256
TC = 512
NB = 192
LAND = NB * 128
DEV = 256
HALO = 8
K = 7
PANELS = 5
SPAN = TR + 16
EXT = PANELS * SPAN
BAND = 48
BANDS = 2 * PANELS * BAND
STRIP = 5 * PANELS * 8
NEAR = 5 * PANELS * 2 * 24
PREP = 2 * DEV + TR + 16 + 8
SHELF = PREP + 2 * STRIP
ROOM = 4096
FLOW = PANELS * TR + 2 * DEV + 8
MEAN_LANE = 40
FULL = 63

gravity = 9.81
cell_size = 30.0
time_step = 2.5
depth_floor = 0.25
half_rate = 0.5
lateral_rate = 0.2
drainage = 0.05
slope_coef = gravity * time_step / cell_size
fric_coef = gravity * time_step

ROWS = ("grp", "gy")
ALL = ("grp", "gy", "gx")
VMEM = pl.BlockSpec(memory_space=pltpu.VMEM)
SMEM = pl.BlockSpec(memory_space=pltpu.SMEM)
HBM = pl.BlockSpec(memory_space=pltpu.HBM)
ANY = pl.BlockSpec(memory_space=pl.ANY)


def params(mib):
    return pltpu.CompilerParams(vmem_limit_bytes=mib * 1024 * 1024)


def array(*shape):
    return jax.ShapeDtypeStruct(shape, F32)


def iota(shape, dim):
    return lax.broadcasted_iota(jnp.int32, shape, dim)


def copies(sem, pairs):
    made = [pltpu.make_async_copy(src, dst, sem.at[n]) for n, (src, dst) in enumerate(pairs)]
    for c in made:
        c.start()
    return made


def wait(made):
    for c in made:
        c.wait()


def parts(x):
    high = x.astype(BF16)
    low = (x - high.astype(F32)).astype(BF16)
    return high, low


def hot_dot(hot, x):
    both = jnp.dot(hot, jnp.concatenate(parts(x), axis=1), preferred_element_type=F32)
    return both[:, :128] + both[:, 128:]


def as_hot(mask):
    return mask.astype(F32).astype(BF16)


def twice(col):
    return jnp.concatenate([col, col], axis=1)


def turned(row):
    return jnp.broadcast_to(row, (128, row.shape[1])).T


def send_kernel(
    live_ref, slot_hbm, recv_hbm, rain_hbm, cap_hbm, depth_hbm, wet_hbm, soil_hbm,
    out_hbm, pond_hbm, recv_hbm_out,
    recv_out, soil_ref, slot_ref, recv_ref, rain_ref, cap_ref, depth_ref, wet_ref, out_ref, pond_ref, tmp_ref, sem, sem_out,
):
    got = copies(
        sem,
        (
            (slot_hbm, slot_ref), (rain_hbm, rain_ref), (cap_hbm, cap_ref),
            (recv_hbm, recv_ref), (depth_hbm, depth_ref), (wet_hbm, wet_ref),
            (soil_hbm.at[NB * 8 : NB * 16, :], soil_ref),
        ),
    )
    live = live_ref[0]
    wait(got[:3])
    cell = iota((NB, 128), 0) * 128 + iota((NB, 128), 1)
    rain = jnp.where(cell < live, rain_ref[...], 0.0)
    rhs = jnp.concatenate(parts(rain) + parts(cap_ref[...]), axis=1)
    slot = slot_ref[...]
    tile = iota((DEV, NB), 0)
    lane = iota((DEV, 128), 1)
    for_west = jnp.zeros((DEV, 128), F32)
    for_east = jnp.zeros((DEV, 128), F32)
    for k in range(2):
        res = jnp.dot(as_hot(slot == 2 * tile + k), rhs, preferred_element_type=F32)
        for a in range(2):
            block = res[:, 256 * a : 256 * a + 128] + res[:, 256 * a + 128 : 256 * a + 256]
            out_ref[pl.ds(2 * a + k, DEV, stride=K), :] = block
            g = 2 * a + k
            low, high = 124 - 8 * g, 8 * g
            moved_w = pltpu.roll(block, (128 - 8 * g) % 128, 1) if g else block
            moved_e = pltpu.roll(block, 8 * g, 1) if g else block
            for_west = jnp.where((lane >= low) & (lane < low + 4), moved_w, for_west)
            for_east = jnp.where((lane >= high) & (lane < high + 4), moved_e, for_east)
    edge = jnp.where(lane < 64, pltpu.roll(for_east, DEV - 1, 0), pltpu.roll(for_west, 1, 0))
    wait(got[3:])
    half = NB * 8
    which = iota((half, 128), 0) // 8 * 128 + iota((half, 128), 1)
    kept = jnp.where(which < live, soil_ref[...], 0.0)
    mean = jnp.sum(jnp.sum(kept.reshape(half // 8, 8, 128), axis=0)) / (live.astype(F32) * 8.0)
    out_ref[pl.ds(6, DEV, stride=K), :] = jnp.where(lane == MEAN_LANE, mean, edge)
    tmp_ref[...] = turned(recv_ref[...].astype(F32))
    fields = []
    for c in range(4):
        cols = slice(128 * c, 128 * c + 128)
        fields.append(jnp.concatenate(parts(depth_ref[:, cols] * wet_ref[:, cols].astype(F32)), axis=1))
    place4 = iota((DEV, 256), 1).astype(F32) * 4.0
    recv_out[4:8, :] = jnp.zeros((4, 128), F32)
    for k in range(2):
        col = tmp_ref[pl.ds(k, DEV, stride=2), :]
        recv_out[2 * k : 2 * k + 1, :] = col[:128].T[0:1]
        recv_out[2 * k + 1 : 2 * k + 2, :] = col[128:].T[0:1]
        wide = twice(col)
        acc = jnp.zeros((DEV, 256), F32)
        for c in range(4):
            acc = acc + jnp.dot(as_hot(wide == place4 + float(c)), fields[c], preferred_element_type=F32)
        pond = acc[:, :128] + acc[:, 128:]
        out_ref[pl.ds(4 + k, DEV, stride=K), :] = pond
        pond_ref[DEV * k : DEV * k + DEV, :] = pond
    wait(copies(sem_out, ((out_ref, out_hbm), (pond_ref, pond_hbm), (recv_out, recv_hbm_out))))


def send_call(live, slot, recv, rain, cap, depth, wet, soil):
    return pl.pallas_call(
        send_kernel,
        out_shape=(array(DEV * K, 128), array(2 * DEV, 128), array(8, 128)),
        in_specs=[SMEM] + [HBM] * 7,
        out_specs=(HBM,) * 3,
        scratch_shapes=[
            pltpu.VMEM((8, 128), F32),
            pltpu.VMEM((NB * 8, 128), F32),
            pltpu.VMEM((1, NB), jnp.int32),
            pltpu.VMEM((1, 2 * DEV), jnp.int32),
            pltpu.VMEM((NB, 128), F32),
            pltpu.VMEM((NB, 128), F32),
            pltpu.VMEM((TR, TC), F32),
            pltpu.VMEM((TR, TC), jnp.int32),
            pltpu.VMEM((DEV * K, 128), F32),
            pltpu.VMEM((2 * DEV, 128), F32),
            pltpu.VMEM((2 * DEV, 128), F32),
            pltpu.SemaphoreType.DMA((7,)),
            pltpu.SemaphoreType.DMA((3,)),
        ],
        compiler_params=params(FULL),
        name="message",
    )(live, slot, recv, rain, cap, depth, wet, soil)


def cols_kernel(
    recv_hbm, depth, wet, bed, man, qe, qs,
    to_west, to_east,
    west_ref, east_ref, wet_w, wet_e, sem,
):
    left, right = slice(0, 128), slice(TC - 128, TC)
    pairs = [(wet.at[:, left], wet_w), (wet.at[:, right], wet_e)]
    for n, f in enumerate((depth, bed, man, qe, qs)):
        rows = slice(TR * n, TR * n + TR)
        pairs.append((f.at[:, left], west_ref.at[rows, :]))
        pairs.append((f.at[:, right], east_ref.at[rows, :]))
    pairs.append((recv_hbm, to_west.at[TR : TR + 8, :]))
    pairs.append((recv_hbm, to_east.at[TR : TR + 8, :]))
    got = copies(sem, pairs)
    wait(got)
    lane = iota((TR, 128), 1)
    for src, mask, out, first in ((west_ref, wet_w, to_west, 0), (east_ref, wet_e, to_east, 120)):
        acc = jnp.zeros((TR, 128), F32)
        for n in range(5):
            own = src[TR * n : TR * n + TR, :]
            if n == 0:
                own = own * mask[...].astype(F32)
            shift = (8 * n - first) % 128
            moved = pltpu.roll(own, shift, 1) if shift else own
            acc = jnp.where((lane >= 8 * n) & (lane < 8 * n + 8), moved, acc)
        out[0:TR, :] = acc


def cols_call(recv, fields):
    return pl.pallas_call(
        cols_kernel,
        out_shape=(array(TR + 8, 128), array(TR + 8, 128)),
        in_specs=[HBM] * 7,
        scratch_shapes=[
            pltpu.VMEM((5 * TR, 128), F32),
            pltpu.VMEM((5 * TR, 128), F32),
            pltpu.VMEM((TR, 128), jnp.int32),
            pltpu.VMEM((TR, 128), jnp.int32),
            pltpu.SemaphoreType.DMA((14,)),
        ],
        compiler_params=params(FULL),
        name="column_strips",
    )(recv, *fields)


def inflow_kernel(
    after_any, got_ref, prep_hbm,
    flow_hbm, up_hbm, down_hbm,
    flow_ref, up_ref, down_ref, prep_ref, sem_in, sem,
):
    in_ref = flow_ref.at[0 : PANELS * TR, :]
    land_ref = flow_ref.at[PANELS * TR : FLOW, :]
    moved = copies(
        sem_in,
        (
            (prep_hbm.at[0:PREP, :], prep_ref),
            (prep_hbm.at[PREP : PREP + STRIP, :], up_ref.at[0:STRIP, :]),
            (prep_hbm.at[PREP + STRIP : SHELF, :], down_ref.at[0:STRIP, :]),
        ),
    )
    for k in range(2):
        land_ref[DEV * k : DEV * k + DEV, :] = got_ref[pl.ds(4 + k, DEV, stride=K), :]
    n_rows, n_cols = lax.axis_size(ROWS), lax.axis_size("gx")
    my_row, my_col = lax.axis_index(ROWS), lax.axis_index("gx")
    here = my_row * n_cols + my_col

    def note_of(device):
        return got_ref[pl.ds(jnp.clip(device, 0, DEV - 1) * K + 6, 1), :]

    mean = note_of(here)
    lat = jnp.where(my_row > 0, note_of(here - n_cols) - mean, 0.0)
    lat = lat + jnp.where(my_row < n_rows - 1, note_of(here + n_cols) - mean, 0.0)
    lat = lat + jnp.where(my_col > 0, note_of(here - 1) - mean, 0.0)
    lat = lat + jnp.where(my_col < n_cols - 1, note_of(here + 1) - mean, 0.0)
    lat = jnp.sum(jnp.where(iota((1, 128), 1) == MEAN_LANE, lat, 0.0), axis=1, keepdims=True)
    land_ref[2 * DEV : 2 * DEV + 8, :] = jnp.broadcast_to(lateral_rate * lat, (8, 128))
    lane = iota((DEV, 128), 1)
    place4 = iota((TR, DEV), 0).astype(F32) * 4.0

    def runoff(rain, cap, pond):
        wetting = rain + jnp.maximum(pond, 0.0)
        return rain * (1.0 - cap / (wetting + half_rate))

    def line(k, base):
        at = base + 2 * k
        return jnp.concatenate([prep_ref[at : at + 1, :], prep_ref[at + 1 : at + 2, :]], axis=1)

    note, own = 2 * DEV + TR, PREP - 8
    wait(moved)
    flows = []
    for k in range(2):
        rain = got_ref[pl.ds(k, DEV, stride=K), :]
        cap = got_ref[pl.ds(2 + k, DEV, stride=K), :]
        flow = runoff(rain, cap, prep_ref[DEV * k : DEV * k + DEV, :])
        flows.append(jnp.concatenate(parts(flow), axis=1))
    for c in range(4):
        acc = jnp.zeros((TR, 256), F32)
        for k in range(2):
            hot = as_hot(line(k, own) == place4 + float(c))
            acc = acc + jnp.dot(hot, flows[k], preferred_element_type=F32)
        in_ref[TR * c : TR * c + TR, :] = acc[:, :128] + acc[:, 128:]
    parts_of = (slice(0, 4 * TR), slice(PANELS * TR, FLOW))
    stored = copies(sem, [(flow_ref.at[rows, :], flow_hbm.at[rows, :]) for rows in parts_of])

    edge = got_ref[pl.ds(6, DEV, stride=K), :]
    depth = prep_ref[2 * DEV : 2 * DEV + TR, :]
    lane_place = iota((DEV, TR), 1).astype(F32) * 4.0
    is_east, is_west = lane < 4, lane >= 124
    acc = jnp.zeros((TR, 128), F32)

    def pick(g):
        if g == 0:
            return edge
        return jnp.where(lane < 64, pltpu.roll(edge, 128 - 8 * g, 1), pltpu.roll(edge, 8 * g, 1))

    sides = ((note, 3, is_west), (note + 8, 0, is_east))
    for k in range(2):
        rain, cap = pick(k), pick(2 + k)
        pond = jnp.zeros((DEV, 128), F32)
        for base, c, mask in sides:
            col = twice(turned(line(k, base)))
            pond = jnp.where(mask, hot_dot(as_hot(col == lane_place + float(c)), depth), pond)
        flow = jnp.where(is_east | is_west, runoff(rain, cap, pond), 0.0)
        for base, c, mask in sides:
            hot = as_hot(line(k, base) == place4 + float(c))
            acc = acc + hot_dot(hot, jnp.where(mask, flow, 0.0))
    acc = jnp.where(is_west & (my_col > 0), acc, jnp.where(is_east & (my_col < n_cols - 1), acc, 0.0))
    side_rows = slice(4 * TR, 5 * TR)
    in_ref[side_rows, :] = acc
    stored.append(pltpu.make_async_copy(flow_ref.at[side_rows, :], flow_hbm.at[side_rows, :], sem.at[2]))
    stored[-1].start()
    for j in range(PANELS):
        to = slice(STRIP + 8 * j, STRIP + 8 * j + 8)
        up_ref[to, :] = in_ref[TR * j : TR * j + 8, :]
        down_ref[to, :] = in_ref[TR * j + TR - 8 : TR * j + TR, :]
    for n, (src, dst) in enumerate(((up_ref, up_hbm), (down_ref, down_hbm))):
        stored.append(pltpu.make_async_copy(src, dst, sem.at[3 + n]))
        stored[-1].start()
    wait(stored)


def inflow_call(after, got, prep):
    strip = array(STRIP + PANELS * 8, 128)
    return pl.pallas_call(
        inflow_kernel,
        out_shape=(array(FLOW, 128), strip, strip),
        in_specs=[ANY, VMEM, HBM],
        out_specs=(HBM,) * 3,
        scratch_shapes=[pltpu.VMEM((n, 128), F32) for n in (FLOW, STRIP + PANELS * 8, STRIP + PANELS * 8, PREP)]
        + [pltpu.SemaphoreType.DMA((3,)), pltpu.SemaphoreType.DMA((5,))],
        compiler_params=params(52),
        name="inflow",
    )(after, got, prep)


class Grid:
    def __init__(self, bases, tiles, rows):
        self.bases, self.tiles, self.rows = bases, tiles, rows
        self.all = [(g, i) for g in range(len(bases)) for i in range(tiles)]

    def at(self, g, i, j, shift=0):
        start = self.bases[g][j] + 8 + 8 * i + shift
        return slice(start, start + 8)

    def south_open(self, g, i, row0):
        row = row0 + self.rows[g] + 8 * i + iota((8, 128), 0)
        return (row >= 0) & (row + 1 <= TR * lax.axis_size(ROWS) - 1)


BULK = Grid([[j * SPAN for j in range(PANELS)]], TR // 8, [0])
EDGES = Grid([[(PANELS * g + j) * BAND for j in range(PANELS)] for g in range(2)], 4, [-8, TR - 24])
EDGES_LATE = Grid([EDGES.bases[0], [b + 8 for b in EDGES.bases[1]]], 3, [-8, TR - 16])


def east_open(j, col0):
    lane = iota((8, 128), 1)
    if j < 4:
        col = col0 + 128 * j + lane
    else:
        col = col0 + jnp.where(lane < 64, TC + lane, lane - 128)
    return (col >= 0) & (col + 1 <= TC * lax.axis_size("gx") - 1)


def shifted(values, shift, lane, offset):
    moved = [pltpu.roll(v, shift, 1) for v in values]
    edge = iota((8, 128), 1) == lane
    return [jnp.where(edge, moved[(j + offset) % PANELS], moved[j]) for j in range(PANELS)]


def run_steps(count, grid, state, consts, east_ref, row0, col0, after):
    s_ref, qe_ref, qs_ref = state
    mbe_ref, cre_ref, mbs_ref, crs_ref = consts
    ge = [jnp.where(east_open(j, col0), slope_coef, 0.0).astype(F32) for j in range(PANELS)]

    def flux(q, a, b, mb, cr, g):
        h = jnp.maximum(jnp.maximum(a, b) - mb, depth_floor)
        numer = q - g * (h * (b - a))
        power = jnp.exp2(jnp.log(h) * F32(-7.0 / 3.0 / 0.6931471805599453))
        return numer * pltpu.reciprocal(1.0 + cr * jnp.abs(q) * power, approx=True)

    def one_step(_, c0):
        for g, i in grid.all:
            moved = shifted([s_ref[grid.at(g, i, j), :] for j in range(PANELS)], 127, 127, 1)
            for j in range(PANELS):
                east_ref[grid.at(g, i, j), :] = moved[j]
        for g, i in grid.all:
            gs = jnp.where(grid.south_open(g, i, row0), slope_coef, 0.0).astype(F32)
            for j in range(PANELS):
                p = grid.at(g, i, j)
                s = s_ref[p, :]
                qe_ref[p, :] = flux(qe_ref[p, :], s, east_ref[p, :], mbe_ref[p, :], cre_ref[p, :], ge[j])
                qs_ref[p, :] = flux(qs_ref[p, :], s, s_ref[grid.at(g, i, j, 1), :], mbs_ref[p, :], crs_ref[p, :], gs)
        for g, i in grid.all:
            qe = [qe_ref[grid.at(g, i, j), :] for j in range(PANELS)]
            west = shifted(qe, 1, 0, PANELS - 1)
            for j in range(PANELS):
                p = grid.at(g, i, j)
                change = (qe[j] - west[j]) + (qs_ref[p, :] - qs_ref[grid.at(g, i, j, -1), :])
                s_ref[p, :] = s_ref[p, :] - F32(time_step / cell_size) * change
            after(g, i, qe)
        return c0

    lax.fori_loop(0, count, one_step, 0)


def set_up(grid, state, consts, bed_ref, man_ref, row0, col0):
    s_ref, qe_ref, qs_ref = state
    mbe_ref, cre_ref, mbs_ref, crs_ref = consts
    open_e = east_open(3, col0)
    for g, i in grid.all:
        bed = [bed_ref[grid.at(g, i, j), :] for j in range(PANELS)]
        man = [man_ref[grid.at(g, i, j), :] for j in range(PANELS)]
        bed_e, man_e = shifted(bed, 127, 127, 1), shifted(man, 127, 127, 1)
        for j in range(PANELS):
            p = grid.at(g, i, j)
            mbe_ref[p, :] = jnp.maximum(bed[j], bed_e[j])
            mbs_ref[p, :] = jnp.maximum(bed[j], bed_ref[grid.at(g, i, j, 1), :])
            rough_e = 0.5 * (man[j] + man_e[j])
            rough_s = 0.5 * (man[j] + man_ref[grid.at(g, i, j, 1), :])
            cre_ref[p, :] = fric_coef * rough_e * rough_e
            crs_ref[p, :] = fric_coef * rough_s * rough_s
            s_ref[p, :] = s_ref[p, :] + bed[j]
        qe_ref[grid.at(g, i, 3), :] = jnp.where(open_e, qe_ref[grid.at(g, i, 3), :], 0.0)
        if grid.rows[g] + 8 * i == TR - 8:
            for j in range(PANELS):
                p = grid.at(g, i, j)
                qs_ref[p, :] = jnp.where(grid.south_open(g, i, row0), qs_ref[p, :], 0.0)


def clear_guards(grid, refs):
    zero = jnp.zeros((8, 128), F32)
    for ref in refs:
        for g in range(len(grid.bases)):
            for j in range(PANELS):
                ref[grid.at(g, -1, j), :] = zero
                ref[grid.at(g, grid.tiles, j), :] = zero


def place():
    return lax.axis_index(ROWS) * TR, lax.axis_index("gx") * TC


def add_bulk_edges(edge_ref):
    def after(g, i, qe):
        for n in range(2):
            rows = slice(TR * n + 8 * i, TR * n + 8 * i + 8)
            edge_ref[rows, :] = edge_ref[rows, :] + qe[3 + n]

    return after


def add_band_edges(grid, sum_ref, qs_ref):
    def after(g, i, qe):
        if grid.rows[g] + 8 * i in (0, TR - 8):
            for n in range(2):
                rows = slice(16 * g + 8 * n, 16 * g + 8 * n + 8)
                sum_ref[rows, :] = sum_ref[rows, :] + qe[3 + n]
        if grid.rows[g] + 8 * i == (-8, TR - 8)[g]:
            for j in range(4):
                rows = slice(32 + 8 * (4 * g + j), 40 + 8 * (4 * g + j))
                sum_ref[rows, :] = sum_ref[rows, :] + qs_ref[grid.at(g, i, j), :]

    return after


SUMS = 32 + 64


def first_kernel(
    west_hbm, east_hbm, recv_hbm, pond_hbm, depth_hbm, wet_hbm, bed_hbm, man_hbm, qe_hbm, qs_hbm,
    s_out, qe_out, qs_out, mbe_out, cre_out, mbs_out, crs_out, edge_out, prep_out, near_out,
    s_ref, qe_ref, qs_ref, mbe_ref, cre_ref, mbs_ref, crs_ref, edge_ref, prep_ref, near_ref,
    bed_x, man_x, wet_ref, east_x, west_ref, east_ref, sem, sem_out,
):
    pairs = [
        (west_hbm, west_ref), (east_hbm, east_ref),
        (recv_hbm, prep_ref.at[PREP - 8 : PREP, :]), (pond_hbm, prep_ref.at[0 : 2 * DEV, :]), (wet_hbm, wet_ref),
    ]
    targets = (s_ref, bed_x, man_x, qe_ref, qs_ref)
    for n, src in enumerate((depth_hbm, bed_hbm, man_hbm, qe_hbm, qs_hbm)):
        for j in range(4):
            to = targets[n].at[j * SPAN + 8 : j * SPAN + 8 + TR, :]
            pairs.append((src.at[:, 128 * j : 128 * j + 128], to))
    got = copies(sem, pairs)
    row0, col0 = place()
    state, consts = (s_ref, qe_ref, qs_ref), (mbe_ref, cre_ref, mbs_ref, crs_ref)
    clear_guards(BULK, targets + consts)
    edge_ref[...] = jnp.zeros((2 * TR, 128), F32)
    wait(got[:2])
    lane = iota((TR, 128), 1)
    for n, ref in enumerate(targets):
        shift = (128 - 8 * n) % 128
        e, w = east_ref[0:TR, :], west_ref[0:TR, :]
        e = pltpu.roll(e, shift, 1) if shift else e
        w = pltpu.roll(w, 120 - 8 * n, 1)
        beside = jnp.where(lane < 8, e, jnp.where(lane >= 120, w, 0.0))
        ref[4 * SPAN + 8 : 4 * SPAN + 8 + TR, :] = beside
        if n == 0:
            prep_ref[2 * DEV : 2 * DEV + TR, :] = beside
    note = 2 * DEV + TR
    prep_ref[note : note + 8, :] = west_ref[TR : TR + 8, :]
    prep_ref[note + 8 : note + 16, :] = east_ref[TR : TR + 8, :]
    wait(got[2:])
    stored = []
    for j in range(4):
        own = slice(j * SPAN + 8, j * SPAN + 8 + TR)
        s_ref[own, :] = s_ref[own, :] * wet_ref[:, 128 * j : 128 * j + 128].astype(F32)
    for n, ref in enumerate(targets):
        for j in range(PANELS):
            at = PANELS * n + j
            base = j * SPAN + 8
            near_ref[48 * at : 48 * at + 24, :] = ref[base : base + 24, :]
            near_ref[48 * at + 24 : 48 * at + 48, :] = ref[base + TR - 24 : base + TR, :]
            up, down = PREP + 8 * at, PREP + STRIP + 8 * at
            prep_ref[up : up + 8, :] = ref[base : base + 8, :]
            prep_ref[down : down + 8, :] = ref[base + TR - 8 : base + TR, :]

    def store(pairs):
        for src, dst in pairs:
            stored.append(pltpu.make_async_copy(src, dst, sem_out.at[len(stored)]))
            stored[-1].start()

    store(((prep_ref, prep_out.at[0:SHELF, :]), (near_ref, near_out)))
    set_up(BULK, state, consts, bed_x, man_x, row0, col0)
    store(zip(consts, (mbe_out, cre_out, mbs_out, crs_out)))
    run_steps(STEPS // 2, BULK, state, consts, east_x, row0, col0, add_bulk_edges(edge_ref))
    store(zip(state + (edge_ref,), (s_out, qe_out, qs_out, edge_out)))
    wait(stored)


def first_call(west, east, recv, pond, fields):
    ext = array(EXT, 128)
    buffer, message = pltpu.VMEM((EXT, 128), F32), pltpu.VMEM((TR + 8, 128), F32)
    extra = (2 * TR, SHELF, NEAR)
    return pl.pallas_call(
        first_kernel,
        out_shape=(ext,) * 7 + tuple(array(n, 128) for n in (2 * TR, ROOM, NEAR)),
        in_specs=[HBM] * 10,
        out_specs=(HBM,) * 10,
        scratch_shapes=[buffer] * 7
        + [pltpu.VMEM((n, 128), F32) for n in extra]
        + [buffer, buffer, pltpu.VMEM((TR, TC), jnp.int32), buffer, message, message]
        + [pltpu.SemaphoreType.DMA((25,)), pltpu.SemaphoreType.DMA((10,))],
        compiler_params=params(FULL),
        name="first_steps",
    )(west, east, recv, pond, *fields)


CHUNK = 16
CHUNKS = NB // CHUNK


def soil_rows(layer, block):
    return pl.ds((layer // 8) * (NB * 8) + block * 8 + layer % 8, 8, stride=8)


def columns_kernel(
    after_any, live_ref, soil_hbm, cond_hbm,
    base_hbm, top_hbm, low_hbm,
    soil_ref, cond_ref, cond_x, base_ref, top_ref, low_ref, sem, sem_out,
):
    pairs = []
    half = NB * 8
    for c in range(CHUNKS):
        cols = slice(c * CHUNK * 128, (c + 1) * CHUNK * 128)
        pairs.append((cond_hbm.at[:, cols], cond_ref.at[:, cols]))
        for h in range(2):
            rows = slice(h * half + c * CHUNK * 8, h * half + (c + 1) * CHUNK * 8)
            pairs.append((soil_hbm.at[rows, :], soil_ref.at[rows, :]))
    moved = copies(sem, pairs)
    live = live_ref[0]
    sub, lane = iota((8, 128), 0), iota((8, 128), 1)
    group = range(CHUNK // 8)
    for c in range(CHUNKS):
        wait(moved[3 * c : 3 * c + 3])
        for b in range(c * CHUNK, (c + 1) * CHUNK):
            cond_x[16 * b : 16 * b + 16, :] = cond_ref[:, 128 * b : 128 * b + 128].astype(F32)
        blocks = [c * CHUNK + 8 * g for g in group]
        kept = [(b + sub) * 128 + lane < live for b in blocks]
        mark = [k.astype(F32) for k in kept]

        def cond_at(g, layer):
            return cond_x[pl.ds(blocks[g] * 16 + layer, 8, stride=16), :]

        def out_at(g, layer):
            return slice(layer * NB + blocks[g], layer * NB + blocks[g] + 8)

        ratios = [[] for _ in group]
        above = [None for _ in group]
        base = [[] for _ in group]
        top = [[] for _ in group]
        low = [[] for _ in group]
        cond = [cond_at(g, 0) for g in group]
        for j in range(NL):
            for g in group:
                center = 1.0 if j < NL - 1 else 1.0 + drainage
                if j > 0:
                    center = center + (above[g] + above[g] * ratios[g][-1])
                if j < NL - 1:
                    below = cond_at(g, j + 1)
                    face = 0.5 * (cond[g] + below)
                    cond[g] = below
                    center = center + face
                r = pltpu.reciprocal(center, approx=True)
                value = soil_ref[soil_rows(j, blocks[g]), :] * r
                if j == 0:
                    top[g].append(mark[g] * r)
                else:
                    carry = above[g] * r
                    value = value + carry * base[g][-1]
                    top[g].append(carry * top[g][-1])
                base[g].append(value)
                if j == 8:
                    low[g].append(mark[g] * r)
                if j > 8:
                    low[g].append(mark[g] * r + carry * low[g][-1])
                if j < NL - 1:
                    ratios[g].append(-face * r)
                    above[g] = face
        x = [base[g][-1] for g in group]
        u = [top[g][-1] for g in group]
        v = [low[g][-1] for g in group]
        for j in range(NL - 1, -1, -1):
            for g in group:
                if j < NL - 1:
                    ratio = ratios[g][j]
                    x[g] = base[g][j] - ratio * x[g]
                    u[g] = top[g][j] - ratio * u[g]
                    v[g] = (low[g][j - 8] - ratio * v[g]) if j >= 8 else -ratio * v[g]
                base_ref[out_at(g, j), :] = jnp.where(kept[g], x[g], soil_ref[soil_rows(j, blocks[g]), :])
                top_ref[out_at(g, j), :] = u[g]
                low_ref[out_at(g, j), :] = v[g]
    wait(copies(sem_out, ((base_ref, base_hbm), (top_ref, top_hbm), (low_ref, low_hbm))))


def columns_call(after, live, soil, cond):
    layers = array(NB * NL, 128)
    buffer = pltpu.VMEM((NB * NL, 128), F32)
    return pl.pallas_call(
        columns_kernel,
        out_shape=(layers,) * 3,
        in_specs=[ANY, SMEM, HBM, HBM],
        out_specs=(HBM,) * 3,
        scratch_shapes=[buffer, pltpu.VMEM((NL, LAND), BF16), buffer, buffer, buffer, buffer]
        + [pltpu.SemaphoreType.DMA((3 * CHUNKS,)), pltpu.SemaphoreType.DMA((3,))],
        compiler_params=params(FULL),
        name="soil_columns",
    )(after, live, soil, cond)


PARTS = 4


def land_part(land_ref, slot_ref, rain_ref, cap_ref, base_ref, top_ref, low_ref, out_hbm, soil_ref, sem_out):
    slot = jnp.broadcast_to(slot_ref[...].astype(F32), (128, NB))
    slot = jnp.concatenate([slot, jnp.full((128, 256 - NB), -1.0, F32)], axis=1).T
    slot = twice(slot[0:NB])
    tile2 = iota((NB, DEV), 1).astype(F32) * 2.0
    pond = jnp.zeros((NB, 128), F32)
    for k in range(2):
        pond = pond + hot_dot(as_hot(slot == tile2 + float(k)), land_ref[DEV * k : DEV * k + DEV, :])
    rain = rain_ref[...]
    wetting = rain + jnp.maximum(pond, 0.0)
    rain_ref[...] = cap_ref[...] * wetting * pltpu.reciprocal(wetting + half_rate, approx=True)
    lat = land_ref[2 * DEV : 2 * DEV + 8, :]
    stored = []
    share = NB // PARTS
    for c in range(PARTS):
        for b in range(c * share, (c + 1) * share, 8):
            uptake = rain_ref[b : b + 8, :]
            for j in range(NL):
                rows = slice(j * NB + b, j * NB + b + 8)
                x = base_ref[rows, :] + (uptake * top_ref[rows, :] + lat * low_ref[rows, :])
                soil_ref[soil_rows(j, b), :] = x
        for h in range(2):
            rows = slice(h * NB * 8 + c * share * 8, h * NB * 8 + (c + 1) * share * 8)
            stored.append(pltpu.make_async_copy(soil_ref.at[rows, :], out_hbm.at[rows, :], sem_out.at[2 * c + h]))
            stored[-1].start()
    return stored


def middle_kernel(
    flow_hbm, s_in, qe_in, qs_in, mbe_in, cre_in, mbs_in, crs_in, edge_in, bed_hbm,
    slot_hbm, rain_hbm, cap_hbm, base_hbm, top_hbm, low_hbm,
    depth_hbm, qe_hbm, qs_hbm, edge_hbm, soil_out,
    in_ref, s_ref, qe_ref, qs_ref, mbe_ref, cre_ref, mbs_ref, crs_ref, edge_ref, bed_ref,
    land_ref, slot_ref, rain_ref, cap_ref, base_ref, top_ref, low_ref, soil_ref,
    east_ref, sem_state, sem_land, sem_tiles, sem_out,
):
    state, consts = (s_ref, qe_ref, qs_ref), (mbe_ref, cre_ref, mbs_ref, crs_ref)
    in_hbm, land_hbm = flow_hbm.at[0 : PANELS * TR, :], flow_hbm.at[PANELS * TR : FLOW, :]
    sources = (s_in, in_hbm, qe_in, qs_in, mbe_in, cre_in, mbs_in, crs_in, edge_in, bed_hbm)
    loaded = copies(sem_state, list(zip(sources, (s_ref, in_ref, qe_ref, qs_ref) + consts + (edge_ref, bed_ref))))
    sources = (slot_hbm, rain_hbm, cap_hbm, land_hbm, base_hbm, top_hbm, low_hbm)
    land = copies(sem_land, list(zip(sources, (slot_ref, rain_ref, cap_ref, land_ref, base_ref, top_ref, low_ref))))
    row0, col0 = place()
    wait(loaded)
    for j in range(PANELS):
        own = slice(j * SPAN + 8, j * SPAN + 8 + TR)
        s_ref[own, :] = s_ref[own, :] + in_ref[TR * j : TR * j + TR, :]
    run_steps(STEPS - STEPS // 2, BULK, state, consts, east_ref, row0, col0, add_bulk_edges(edge_ref))
    pairs = [(edge_ref, edge_hbm.at[0 : 2 * TR, :])]
    for src, dst in ((qe_ref, qe_hbm), (qs_ref, qs_hbm)):
        for j in range(4):
            pairs.append((src.at[j * SPAN + 8 : j * SPAN + 8 + TR, :], dst.at[:, 128 * j : 128 * j + 128]))
    for j in range(4):
        cols = slice(128 * j, 128 * j + 128)
        bed_ref[:, cols] = s_ref[j * SPAN + 8 : j * SPAN + 8 + TR, :] - bed_ref[:, cols]
    pairs.append((bed_ref, depth_hbm))
    stored = copies(sem_tiles, pairs)
    wait(land)
    stored += land_part(land_ref, slot_ref, rain_ref, cap_ref, base_ref, top_ref, low_ref, soil_out, soil_ref, sem_out)
    wait(stored)


def middle_call(flow, state, edge, bed, slot, rain, cap, soil):
    tile = array(TR, TC)
    buffer = pltpu.VMEM((EXT, 128), F32)
    blocks, layers = pltpu.VMEM((NB, 128), F32), pltpu.VMEM((NB * NL, 128), F32)
    counts = (10, 7, 10, 2 * PARTS)
    return pl.pallas_call(
        middle_kernel,
        out_shape=(tile,) * 3 + (array(ROOM, 128), array(NB * NL, 128)),
        in_specs=[HBM] * 16,
        out_specs=(HBM,) * 5,
        scratch_shapes=[pltpu.VMEM((PANELS * TR, 128), F32)]
        + [buffer] * 7
        + [pltpu.VMEM((2 * TR, 128), F32), pltpu.VMEM((TR, TC), F32), pltpu.VMEM((2 * DEV + 8, 128), F32)]
        + [pltpu.VMEM((1, NB), jnp.int32), blocks, blocks]
        + [layers] * 4
        + [buffer]
        + [pltpu.SemaphoreType.DMA((n,)) for n in counts],
        compiler_params=params(FULL),
        name="middle_steps",
    )(flow, *state, edge, bed, slot, rain, cap, *soil)


def last_kernel(
    depth_in, qe_in, qs_in, north_hbm, south_hbm, near_hbm, in_hbm, edge_hbm,
    depth_out, qe_out, qs_out, we_hbm, ns_hbm,
    we_ref, ns_ref, north_ref, south_ref, near_ref, in_ref, edge_ref,
    bs_ref, bqe_ref, bqs_ref, bmbe, bcre, bmbs, bcrs, bbed, bman, beast, sum_ref, tile_ref, sem_in, sem,
):
    pairs = [(near_hbm, near_ref), (north_hbm, north_ref), (south_hbm, south_ref)]
    pairs.append((edge_hbm.at[0 : 2 * TR, :], edge_ref))
    for j in range(PANELS):
        for g, start in ((0, 0), (1, TR - 24)):
            to = 24 * (2 * j + g)
            pairs.append((in_hbm.at[TR * j + start : TR * j + start + 24, :], in_ref.at[to : to + 24, :]))
    got = copies(sem_in, pairs)
    row0, col0 = place()
    band, consts = (bs_ref, bqe_ref, bqs_ref), (bmbe, bcre, bmbs, bcrs)
    targets = (bs_ref, bbed, bman, bqe_ref, bqs_ref)
    clear_guards(EDGES, targets + consts)
    sum_ref[...] = jnp.zeros((SUMS, 128), F32)
    wait(got)
    for n, out in enumerate(targets):
        for j in range(PANELS):
            at = PANELS * n + j
            strip = slice(8 * at, 8 * at + 8)
            out[EDGES.at(0, 0, j), :] = north_ref[strip, :]
            out[EDGES.at(1, 3, j), :] = south_ref[strip, :]
            for i in range(3):
                rows = 48 * at + 8 * i
                out[EDGES.at(0, i + 1, j), :] = near_ref[rows : rows + 8, :]
                out[EDGES.at(1, i, j), :] = near_ref[rows + 24 : rows + 32, :]
    set_up(EDGES, band, consts, bbed, bman, row0, col0)
    sums = add_band_edges(EDGES, sum_ref, bqs_ref)
    run_steps(STEPS // 2, EDGES, band, consts, beast, row0, col0, sums)
    for j in range(PANELS):
        strip = slice(STRIP + 8 * j, STRIP + 8 * j + 8)
        for p, flow in ((EDGES.at(0, 0, j), north_ref[strip, :]), (EDGES.at(1, 3, j), south_ref[strip, :])):
            bs_ref[p, :] = bs_ref[p, :] + flow
        for i in range(3):
            for g, p in ((0, EDGES.at(0, i + 1, j)), (1, EDGES.at(1, i, j))):
                rows = 24 * (2 * j + g) + 8 * i
                bs_ref[p, :] = bs_ref[p, :] + in_ref[rows : rows + 8, :]
    sums = add_band_edges(EDGES_LATE, sum_ref, bqs_ref)
    run_steps(STEPS - STEPS // 2, EDGES_LATE, band, consts, beast, row0, col0, sums)
    pairs = []
    for n, out in enumerate((depth_out, qe_out, qs_out)):
        for g, i in ((0, 1), (1, 2)):
            to = slice(16 * n + 8 * g, 16 * n + 8 * g + 8)
            for j in range(4):
                p = EDGES.at(g, i, j)
                tile_ref[to, 128 * j : 128 * j + 128] = bs_ref[p, :] - bbed[p, :] if n == 0 else band[n][p, :]
            rows = slice(0, 8) if g == 0 else slice(TR - 8, TR)
            pairs.append((tile_ref.at[to, :], out.at[rows, :]))
    stored = copies(sem, pairs)
    for n in range(2):
        edge_ref[TR * n : TR * n + 8, :] = sum_ref[8 * n : 8 * n + 8, :]
        edge_ref[TR * n + TR - 8 : TR * n + TR, :] = sum_ref[16 + 8 * n : 24 + 8 * n, :]
    we_ref[0:1, :] = edge_ref[TR : 2 * TR, :].T[127:128, :]
    we_ref[1:2, :] = edge_ref[0:TR, :].T[127:128, :]
    for j in range(4):
        for g in range(2):
            row = 32 + 8 * (4 * g + j) + 7
            ns_ref[g : g + 1, 128 * j : 128 * j + 128] = sum_ref[row : row + 1, :]
    for n, (src, dst) in enumerate(((we_ref, we_hbm), (ns_ref, ns_hbm))):
        stored.append(pltpu.make_async_copy(src, dst, sem.at[6 + n]))
        stored[-1].start()
    wait(stored)


def last_call(tiles, north, south, near, flow, edge):
    strip = pltpu.VMEM((STRIP + PANELS * 8, 128), F32)
    return pl.pallas_call(
        last_kernel,
        out_shape=(array(TR, TC), array(TR, TC), array(TR, TC), array(2, TR), array(2, TC)),
        in_specs=[HBM] * 8,
        out_specs=(HBM,) * 5,
        scratch_shapes=[pltpu.VMEM((2, TR), F32), pltpu.VMEM((2, TC), F32), strip, strip]
        + [pltpu.VMEM((n, 128), F32) for n in (NEAR, 2 * PANELS * 24, 2 * TR)]
        + [pltpu.VMEM((BANDS, 128), F32)] * 10
        + [pltpu.VMEM((SUMS, 128), F32), pltpu.VMEM((48, TC), F32)]
        + [pltpu.SemaphoreType.DMA((4 + 2 * PANELS,)), pltpu.SemaphoreType.DMA((8,))],
        input_output_aliases={0: 0, 1: 1, 2: 2},
        compiler_params=params(53),
        name="last_steps",
    )(*tiles, north, south, near, flow, edge)


def shift(first, second, axis):
    count = lax.axis_size(axis)
    ahead = [(i, i + 1) for i in range(count - 1)]
    back = [(j, i) for i, j in ahead]
    return lax.ppermute(first, axis, ahead), lax.ppermute(second, axis, back)


def local(
    soil_water, conduct, rainfall, infil_cap, live_counts, send_slot, recv_row,
    bed_height, manning, depth_in, east_in, south_in, wet_mask,
):
    rain = rainfall.reshape(NB, 128)
    cap = infil_cap.reshape(NB, 128)
    soil = soil_water.reshape(2, 8, NB, 128).transpose(0, 2, 1, 3).reshape(NB * NL, 128)
    fields = (depth_in, wet_mask, bed_height, manning, east_in, south_in)

    sent, pond, recv = send_call(live_counts, send_slot, recv_row, rain, cap, depth_in, wet_mask, soil)
    got = lax.all_to_all(sent.reshape(DEV, 1, K * 128), ALL, split_axis=0, concat_axis=0, tiled=True)
    got = got.reshape(DEV * K, 128)

    to_west, to_east = cols_call(recv, fields)
    west, east = shift(to_east, to_west, "gx")
    solved = columns_call(to_west, live_counts, soil, conduct)
    *state, edge, prep, near = first_call(west, east, recv, pond, fields)

    flow, up, down = inflow_call(solved[0], got, prep)
    north, south = shift(down, up, ROWS)
    *tiles, edge, soil_out = middle_call(
        flow, state, edge, bed_height, send_slot, rain, cap, solved
    )
    depth, east_q, south_q, edge_we, edge_ns = last_call(tiles, north, south, near, flow, edge)
    soil_out = soil_out.reshape(2, NB, 8, 128).transpose(0, 2, 1, 3).reshape(NL, LAND)
    return soil_out, depth, east_q, south_q, edge_we, edge_ns


def solution(mesh):
    placed = (
        P(None, ALL),
        P(None, ALL),
        P(ALL),
        P(ALL),
        P(ALL),
        P(ALL, None),
        P(ALL, None),
    ) + (P(ROWS, "gx"),) * 6
    return jax.shard_map(
        local,
        mesh=mesh,
        in_specs=placed,
        out_specs=(
            P(None, ALL),
            P(ROWS, "gx"),
            P(ROWS, "gx"),
            P(ROWS, "gx"),
            P("gx", ROWS),
            P(ROWS, "gx"),
        ),
        check_vma=False,
    )
```

```python
import jax
import jax.numpy as jnp
from jax import lax
from jax.experimental import pallas as pl
from jax.experimental.pallas import tpu as pltpu
from jax.sharding import PartitionSpec as P

F32 = jnp.float32
BF16 = jnp.bfloat16

NL = 16
STEPS = 8
TR = 256
TC = 512
NB = 192
LAND = NB * 128
DEV = 256
HALO = 8
K = 7
PANELS = 5
SPAN = TR + 16
EXT = PANELS * SPAN
BAND = 48
BANDS = 2 * PANELS * BAND
STRIP = 5 * PANELS * 8
NEAR = 5 * PANELS * 2 * 24
PREP = 2 * DEV + TR + 16 + 8
SHELF = PREP + 2 * STRIP
ROOM = 4096
FLOW = PANELS * TR + 2 * DEV + 8
MEAN_LANE = 40
FULL = 63

gravity = 9.81
cell_size = 30.0
time_step = 2.5
depth_floor = 0.25
half_rate = 0.5
lateral_rate = 0.2
drainage = 0.05
slope_coef = gravity * time_step / cell_size
fric_coef = gravity * time_step

ROWS = ("grp", "gy")
ALL = ("grp", "gy", "gx")
VMEM = pl.BlockSpec(memory_space=pltpu.VMEM)
SMEM = pl.BlockSpec(memory_space=pltpu.SMEM)
HBM = pl.BlockSpec(memory_space=pltpu.HBM)
ANY = pl.BlockSpec(memory_space=pl.ANY)


def params(mib):
    return pltpu.CompilerParams(vmem_limit_bytes=mib * 1024 * 1024)


def array(*shape):
    return jax.ShapeDtypeStruct(shape, F32)


def iota(shape, dim):
    return lax.broadcasted_iota(jnp.int32, shape, dim)


def copies(sem, pairs):
    made = [pltpu.make_async_copy(src, dst, sem.at[n]) for n, (src, dst) in enumerate(pairs)]
    for c in made:
        c.start()
    return made


def wait(made):
    for c in made:
        c.wait()


def parts(x):
    high = x.astype(BF16)
    low = (x - high.astype(F32)).astype(BF16)
    return high, low


def hot_dot(hot, x):
    both = jnp.dot(hot, jnp.concatenate(parts(x), axis=1), preferred_element_type=F32)
    return both[:, :128] + both[:, 128:]


def as_hot(mask):
    return mask.astype(F32).astype(BF16)


def twice(col):
    return jnp.concatenate([col, col], axis=1)


def turned(row):
    return jnp.broadcast_to(row, (128, row.shape[1])).T


def send_kernel(
    live_ref, slot_hbm, recv_hbm, rain_hbm, cap_hbm, depth_hbm, wet_hbm, soil_hbm,
    out_hbm, pond_hbm, recv_hbm_out,
    recv_out, soil_ref, slot_ref, recv_ref, rain_ref, cap_ref, depth_ref, wet_ref, out_ref, pond_ref, tmp_ref, sem, sem_out,
):
    got = copies(
        sem,
        (
            (slot_hbm, slot_ref), (rain_hbm, rain_ref), (cap_hbm, cap_ref),
            (recv_hbm, recv_ref), (depth_hbm, depth_ref), (wet_hbm, wet_ref),
            (soil_hbm.at[NB * 8 : NB * 16, :], soil_ref),
        ),
    )
    live = live_ref[0]
    wait(got[:3])
    cell = iota((NB, 128), 0) * 128 + iota((NB, 128), 1)
    rain = jnp.where(cell < live, rain_ref[...], 0.0)
    rhs = jnp.concatenate(parts(rain) + parts(cap_ref[...]), axis=1)
    slot = slot_ref[...]
    tile = iota((DEV, NB), 0)
    lane = iota((DEV, 128), 1)
    for_west = jnp.zeros((DEV, 128), F32)
    for_east = jnp.zeros((DEV, 128), F32)
    for k in range(2):
        res = jnp.dot(as_hot(slot == 2 * tile + k), rhs, preferred_element_type=F32)
        for a in range(2):
            block = res[:, 256 * a : 256 * a + 128] + res[:, 256 * a + 128 : 256 * a + 256]
            out_ref[pl.ds(2 * a + k, DEV, stride=K), :] = block
            g = 2 * a + k
            low, high = 124 - 8 * g, 8 * g
            moved_w = pltpu.roll(block, (128 - 8 * g) % 128, 1) if g else block
            moved_e = pltpu.roll(block, 8 * g, 1) if g else block
            for_west = jnp.where((lane >= low) & (lane < low + 4), moved_w, for_west)
            for_east = jnp.where((lane >= high) & (lane < high + 4), moved_e, for_east)
    edge = jnp.where(lane < 64, pltpu.roll(for_east, DEV - 1, 0), pltpu.roll(for_west, 1, 0))
    wait(got[3:])
    half = NB * 8
    which = iota((half, 128), 0) // 8 * 128 + iota((half, 128), 1)
    kept = jnp.where(which < live, soil_ref[...], 0.0)
    mean = jnp.sum(jnp.sum(kept.reshape(half // 8, 8, 128), axis=0)) / (live.astype(F32) * 8.0)
    out_ref[pl.ds(6, DEV, stride=K), :] = jnp.where(lane == MEAN_LANE, mean, edge)
    tmp_ref[...] = turned(recv_ref[...].astype(F32))
    fields = []
    for c in range(4):
        cols = slice(128 * c, 128 * c + 128)
        fields.append(jnp.concatenate(parts(depth_ref[:, cols] * wet_ref[:, cols].astype(F32)), axis=1))
    place4 = iota((DEV, 256), 1).astype(F32) * 4.0
    recv_out[4:8, :] = jnp.zeros((4, 128), F32)
    for k in range(2):
        col = tmp_ref[pl.ds(k, DEV, stride=2), :]
        recv_out[2 * k : 2 * k + 1, :] = col[:128].T[0:1]
        recv_out[2 * k + 1 : 2 * k + 2, :] = col[128:].T[0:1]
        wide = twice(col)
        acc = jnp.zeros((DEV, 256), F32)
        for c in range(4):
            acc = acc + jnp.dot(as_hot(wide == place4 + float(c)), fields[c], preferred_element_type=F32)
        pond = acc[:, :128] + acc[:, 128:]
        out_ref[pl.ds(4 + k, DEV, stride=K), :] = pond
        pond_ref[DEV * k : DEV * k + DEV, :] = pond
    wait(copies(sem_out, ((out_ref, out_hbm), (pond_ref, pond_hbm), (recv_out, recv_hbm_out))))


def send_call(live, slot, recv, rain, cap, depth, wet, soil):
    return pl.pallas_call(
        send_kernel,
        out_shape=(array(DEV * K, 128), array(2 * DEV, 128), array(8, 128)),
        in_specs=[SMEM] + [HBM] * 7,
        out_specs=(HBM,) * 3,
        scratch_shapes=[
            pltpu.VMEM((8, 128), F32),
            pltpu.VMEM((NB * 8, 128), F32),
            pltpu.VMEM((1, NB), jnp.int32),
            pltpu.VMEM((1, 2 * DEV), jnp.int32),
            pltpu.VMEM((NB, 128), F32),
            pltpu.VMEM((NB, 128), F32),
            pltpu.VMEM((TR, TC), F32),
            pltpu.VMEM((TR, TC), jnp.int32),
            pltpu.VMEM((DEV * K, 128), F32),
            pltpu.VMEM((2 * DEV, 128), F32),
            pltpu.VMEM((2 * DEV, 128), F32),
            pltpu.SemaphoreType.DMA((7,)),
            pltpu.SemaphoreType.DMA((3,)),
        ],
        compiler_params=params(FULL),
        name="message",
    )(live, slot, recv, rain, cap, depth, wet, soil)


def cols_kernel(
    recv_hbm, depth, wet, bed, man, qe, qs,
    to_west, to_east,
    west_ref, east_ref, wet_w, wet_e, sem,
):
    left, right = slice(0, 128), slice(TC - 128, TC)
    pairs = [(wet.at[:, left], wet_w), (wet.at[:, right], wet_e)]
    for n, f in enumerate((depth, bed, man, qe, qs)):
        rows = slice(TR * n, TR * n + TR)
        pairs.append((f.at[:, left], west_ref.at[rows, :]))
        pairs.append((f.at[:, right], east_ref.at[rows, :]))
    pairs.append((recv_hbm, to_west.at[TR : TR + 8, :]))
    pairs.append((recv_hbm, to_east.at[TR : TR + 8, :]))
    got = copies(sem, pairs)
    wait(got)
    lane = iota((TR, 128), 1)
    for src, mask, out, first in ((west_ref, wet_w, to_west, 0), (east_ref, wet_e, to_east, 120)):
        acc = jnp.zeros((TR, 128), F32)
        for n in range(5):
            own = src[TR * n : TR * n + TR, :]
            if n == 0:
                own = own * mask[...].astype(F32)
            shift = (8 * n - first) % 128
            moved = pltpu.roll(own, shift, 1) if shift else own
            acc = jnp.where((lane >= 8 * n) & (lane < 8 * n + 8), moved, acc)
        out[0:TR, :] = acc


def cols_call(recv, fields):
    return pl.pallas_call(
        cols_kernel,
        out_shape=(array(TR + 8, 128), array(TR + 8, 128)),
        in_specs=[HBM] * 7,
        scratch_shapes=[
            pltpu.VMEM((5 * TR, 128), F32),
            pltpu.VMEM((5 * TR, 128), F32),
            pltpu.VMEM((TR, 128), jnp.int32),
            pltpu.VMEM((TR, 128), jnp.int32),
            pltpu.SemaphoreType.DMA((14,)),
        ],
        compiler_params=params(FULL),
        name="column_strips",
    )(recv, *fields)


def inflow_kernel(
    after_any, got_ref, prep_hbm,
    flow_hbm, up_hbm, down_hbm,
    flow_ref, up_ref, down_ref, prep_ref, sem_in, sem,
):
    in_ref = flow_ref.at[0 : PANELS * TR, :]
    land_ref = flow_ref.at[PANELS * TR : FLOW, :]
    moved = copies(
        sem_in,
        (
            (prep_hbm.at[0:PREP, :], prep_ref),
            (prep_hbm.at[PREP : PREP + STRIP, :], up_ref.at[0:STRIP, :]),
            (prep_hbm.at[PREP + STRIP : SHELF, :], down_ref.at[0:STRIP, :]),
        ),
    )
    for k in range(2):
        land_ref[DEV * k : DEV * k + DEV, :] = got_ref[pl.ds(4 + k, DEV, stride=K), :]
    n_rows, n_cols = lax.axis_size(ROWS), lax.axis_size("gx")
    my_row, my_col = lax.axis_index(ROWS), lax.axis_index("gx")
    here = my_row * n_cols + my_col

    def note_of(device):
        return got_ref[pl.ds(jnp.clip(device, 0, DEV - 1) * K + 6, 1), :]

    mean = note_of(here)
    lat = jnp.where(my_row > 0, note_of(here - n_cols) - mean, 0.0)
    lat = lat + jnp.where(my_row < n_rows - 1, note_of(here + n_cols) - mean, 0.0)
    lat = lat + jnp.where(my_col > 0, note_of(here - 1) - mean, 0.0)
    lat = lat + jnp.where(my_col < n_cols - 1, note_of(here + 1) - mean, 0.0)
    lat = jnp.sum(jnp.where(iota((1, 128), 1) == MEAN_LANE, lat, 0.0), axis=1, keepdims=True)
    land_ref[2 * DEV : 2 * DEV + 8, :] = jnp.broadcast_to(lateral_rate * lat, (8, 128))
    lane = iota((DEV, 128), 1)
    place4 = iota((TR, DEV), 0).astype(F32) * 4.0

    def runoff(rain, cap, pond):
        wetting = rain + jnp.maximum(pond, 0.0)
        return rain * (1.0 - cap / (wetting + half_rate))

    def line(k, base):
        at = base + 2 * k
        return jnp.concatenate([prep_ref[at : at + 1, :], prep_ref[at + 1 : at + 2, :]], axis=1)

    note, own = 2 * DEV + TR, PREP - 8
    wait(moved)
    flows = []
    for k in range(2):
        rain = got_ref[pl.ds(k, DEV, stride=K), :]
        cap = got_ref[pl.ds(2 + k, DEV, stride=K), :]
        flow = runoff(rain, cap, prep_ref[DEV * k : DEV * k + DEV, :])
        flows.append(jnp.concatenate(parts(flow), axis=1))
    for c in range(4):
        acc = jnp.zeros((TR, 256), F32)
        for k in range(2):
            hot = as_hot(line(k, own) == place4 + float(c))
            acc = acc + jnp.dot(hot, flows[k], preferred_element_type=F32)
        in_ref[TR * c : TR * c + TR, :] = acc[:, :128] + acc[:, 128:]
    parts_of = (slice(0, 4 * TR), slice(PANELS * TR, FLOW))
    stored = copies(sem, [(flow_ref.at[rows, :], flow_hbm.at[rows, :]) for rows in parts_of])

    edge = got_ref[pl.ds(6, DEV, stride=K), :]
    depth = prep_ref[2 * DEV : 2 * DEV + TR, :]
    lane_place = iota((DEV, TR), 1).astype(F32) * 4.0
    is_east, is_west = lane < 4, lane >= 124
    acc = jnp.zeros((TR, 128), F32)

    def pick(g):
        if g == 0:
            return edge
        return jnp.where(lane < 64, pltpu.roll(edge, 128 - 8 * g, 1), pltpu.roll(edge, 8 * g, 1))

    sides = ((note, 3, is_west), (note + 8, 0, is_east))
    for k in range(2):
        rain, cap = pick(k), pick(2 + k)
        pond = jnp.zeros((DEV, 128), F32)
        for base, c, mask in sides:
            col = twice(turned(line(k, base)))
            pond = jnp.where(mask, hot_dot(as_hot(col == lane_place + float(c)), depth), pond)
        flow = jnp.where(is_east | is_west, runoff(rain, cap, pond), 0.0)
        for base, c, mask in sides:
            hot = as_hot(line(k, base) == place4 + float(c))
            acc = acc + hot_dot(hot, jnp.where(mask, flow, 0.0))
    acc = jnp.where(is_west & (my_col > 0), acc, jnp.where(is_east & (my_col < n_cols - 1), acc, 0.0))
    side_rows = slice(4 * TR, 5 * TR)
    in_ref[side_rows, :] = acc
    stored.append(pltpu.make_async_copy(flow_ref.at[side_rows, :], flow_hbm.at[side_rows, :], sem.at[2]))
    stored[-1].start()
    for j in range(PANELS):
        to = slice(STRIP + 8 * j, STRIP + 8 * j + 8)
        up_ref[to, :] = in_ref[TR * j : TR * j + 8, :]
        down_ref[to, :] = in_ref[TR * j + TR - 8 : TR * j + TR, :]
    for n, (src, dst) in enumerate(((up_ref, up_hbm), (down_ref, down_hbm))):
        stored.append(pltpu.make_async_copy(src, dst, sem.at[3 + n]))
        stored[-1].start()
    wait(stored)


def inflow_call(after, got, prep):
    strip = array(STRIP + PANELS * 8, 128)
    return pl.pallas_call(
        inflow_kernel,
        out_shape=(array(FLOW, 128), strip, strip),
        in_specs=[ANY, VMEM, HBM],
        out_specs=(HBM,) * 3,
        scratch_shapes=[pltpu.VMEM((n, 128), F32) for n in (FLOW, STRIP + PANELS * 8, STRIP + PANELS * 8, PREP)]
        + [pltpu.SemaphoreType.DMA((3,)), pltpu.SemaphoreType.DMA((5,))],
        compiler_params=params(52),
        name="inflow",
    )(after, got, prep)


class Grid:
    def __init__(self, bases, tiles, rows):
        self.bases, self.tiles, self.rows = bases, tiles, rows
        self.all = [(g, i) for g in range(len(bases)) for i in range(tiles)]

    def at(self, g, i, j, shift=0):
        start = self.bases[g][j] + 8 + 8 * i + shift
        return slice(start, start + 8)

    def south_open(self, g, i, row0):
        row = row0 + self.rows[g] + 8 * i + iota((8, 128), 0)
        return (row >= 0) & (row + 1 <= TR * lax.axis_size(ROWS) - 1)


BULK = Grid([[j * SPAN for j in range(PANELS)]], TR // 8, [0])
EDGES = Grid([[(PANELS * g + j) * BAND for j in range(PANELS)] for g in range(2)], 4, [-8, TR - 24])
EDGES_LATE = Grid([EDGES.bases[0], [b + 8 for b in EDGES.bases[1]]], 3, [-8, TR - 16])


def east_open(j, col0):
    lane = iota((8, 128), 1)
    if j < 4:
        col = col0 + 128 * j + lane
    else:
        col = col0 + jnp.where(lane < 64, TC + lane, lane - 128)
    return (col >= 0) & (col + 1 <= TC * lax.axis_size("gx") - 1)


def shifted(values, shift, lane, offset):
    moved = [pltpu.roll(v, shift, 1) for v in values]
    edge = iota((8, 128), 1) == lane
    return [jnp.where(edge, moved[(j + offset) % PANELS], moved[j]) for j in range(PANELS)]


def run_steps(count, grid, state, consts, east_ref, row0, col0, after):
    s_ref, qe_ref, qs_ref = state
    mbe_ref, cre_ref, mbs_ref, crs_ref = consts
    ge = [jnp.where(east_open(j, col0), slope_coef, 0.0).astype(F32) for j in range(PANELS)]

    def flux(q, a, b, mb, cr, g):
        h = jnp.maximum(jnp.maximum(a, b) - mb, depth_floor)
        numer = q - g * (h * (b - a))
        power = jnp.exp2(jnp.log(h) * F32(-7.0 / 3.0 / 0.6931471805599453))
        return numer * pltpu.reciprocal(1.0 + cr * jnp.abs(q) * power, approx=True)

    def one_step(_, c0):
        for g, i in grid.all:
            moved = shifted([s_ref[grid.at(g, i, j), :] for j in range(PANELS)], 127, 127, 1)
            for j in range(PANELS):
                east_ref[grid.at(g, i, j), :] = moved[j]
        for g, i in grid.all:
            gs = jnp.where(grid.south_open(g, i, row0), slope_coef, 0.0).astype(F32)
            for j in range(PANELS):
                p = grid.at(g, i, j)
                s = s_ref[p, :]
                qe_ref[p, :] = flux(qe_ref[p, :], s, east_ref[p, :], mbe_ref[p, :], cre_ref[p, :], ge[j])
                qs_ref[p, :] = flux(qs_ref[p, :], s, s_ref[grid.at(g, i, j, 1), :], mbs_ref[p, :], crs_ref[p, :], gs)
        for g, i in grid.all:
            qe = [qe_ref[grid.at(g, i, j), :] for j in range(PANELS)]
            west = shifted(qe, 1, 0, PANELS - 1)
            for j in range(PANELS):
                p = grid.at(g, i, j)
                change = (qe[j] - west[j]) + (qs_ref[p, :] - qs_ref[grid.at(g, i, j, -1), :])
                s_ref[p, :] = s_ref[p, :] - F32(time_step / cell_size) * change
            after(g, i, qe)
        return c0

    lax.fori_loop(0, count, one_step, 0)


def set_up(grid, state, consts, bed_ref, man_ref, row0, col0):
    s_ref, qe_ref, qs_ref = state
    mbe_ref, cre_ref, mbs_ref, crs_ref = consts
    open_e = east_open(3, col0)
    for g, i in grid.all:
        bed = [bed_ref[grid.at(g, i, j), :] for j in range(PANELS)]
        man = [man_ref[grid.at(g, i, j), :] for j in range(PANELS)]
        bed_e, man_e = shifted(bed, 127, 127, 1), shifted(man, 127, 127, 1)
        for j in range(PANELS):
            p = grid.at(g, i, j)
            mbe_ref[p, :] = jnp.maximum(bed[j], bed_e[j])
            mbs_ref[p, :] = jnp.maximum(bed[j], bed_ref[grid.at(g, i, j, 1), :])
            rough_e = 0.5 * (man[j] + man_e[j])
            rough_s = 0.5 * (man[j] + man_ref[grid.at(g, i, j, 1), :])
            cre_ref[p, :] = fric_coef * rough_e * rough_e
            crs_ref[p, :] = fric_coef * rough_s * rough_s
            s_ref[p, :] = s_ref[p, :] + bed[j]
        qe_ref[grid.at(g, i, 3), :] = jnp.where(open_e, qe_ref[grid.at(g, i, 3), :], 0.0)
        if grid.rows[g] + 8 * i == TR - 8:
            for j in range(PANELS):
                p = grid.at(g, i, j)
                qs_ref[p, :] = jnp.where(grid.south_open(g, i, row0), qs_ref[p, :], 0.0)


def clear_guards(grid, refs):
    zero = jnp.zeros((8, 128), F32)
    for ref in refs:
        for g in range(len(grid.bases)):
            for j in range(PANELS):
                ref[grid.at(g, -1, j), :] = zero
                ref[grid.at(g, grid.tiles, j), :] = zero


def place():
    return lax.axis_index(ROWS) * TR, lax.axis_index("gx") * TC


def add_bulk_edges(edge_ref):
    def after(g, i, qe):
        for n in range(2):
            rows = slice(TR * n + 8 * i, TR * n + 8 * i + 8)
            edge_ref[rows, :] = edge_ref[rows, :] + qe[3 + n]

    return after


def add_band_edges(grid, sum_ref, qs_ref):
    def after(g, i, qe):
        if grid.rows[g] + 8 * i in (0, TR - 8):
            for n in range(2):
                rows = slice(16 * g + 8 * n, 16 * g + 8 * n + 8)
                sum_ref[rows, :] = sum_ref[rows, :] + qe[3 + n]
        if grid.rows[g] + 8 * i == (-8, TR - 8)[g]:
            for j in range(4):
                rows = slice(32 + 8 * (4 * g + j), 40 + 8 * (4 * g + j))
                sum_ref[rows, :] = sum_ref[rows, :] + qs_ref[grid.at(g, i, j), :]

    return after


SUMS = 32 + 64


def first_kernel(
    west_hbm, east_hbm, recv_hbm, pond_hbm, depth_hbm, wet_hbm, bed_hbm, man_hbm, qe_hbm, qs_hbm,
    s_out, qe_out, qs_out, mbe_out, cre_out, mbs_out, crs_out, edge_out, prep_out, near_out,
    s_ref, qe_ref, qs_ref, mbe_ref, cre_ref, mbs_ref, crs_ref, edge_ref, prep_ref, near_ref,
    bed_x, man_x, wet_ref, east_x, west_ref, east_ref, sem, sem_out,
):
    pairs = [
        (west_hbm, west_ref), (east_hbm, east_ref),
        (recv_hbm, prep_ref.at[PREP - 8 : PREP, :]), (pond_hbm, prep_ref.at[0 : 2 * DEV, :]), (wet_hbm, wet_ref),
    ]
    targets = (s_ref, bed_x, man_x, qe_ref, qs_ref)
    for n, src in enumerate((depth_hbm, bed_hbm, man_hbm, qe_hbm, qs_hbm)):
        for j in range(4):
            to = targets[n].at[j * SPAN + 8 : j * SPAN + 8 + TR, :]
            pairs.append((src.at[:, 128 * j : 128 * j + 128], to))
    got = copies(sem, pairs)
    row0, col0 = place()
    state, consts = (s_ref, qe_ref, qs_ref), (mbe_ref, cre_ref, mbs_ref, crs_ref)
    clear_guards(BULK, targets + consts)
    edge_ref[...] = jnp.zeros((2 * TR, 128), F32)
    wait(got[:2])
    lane = iota((TR, 128), 1)
    for n, ref in enumerate(targets):
        shift = (128 - 8 * n) % 128
        e, w = east_ref[0:TR, :], west_ref[0:TR, :]
        e = pltpu.roll(e, shift, 1) if shift else e
        w = pltpu.roll(w, 120 - 8 * n, 1)
        beside = jnp.where(lane < 8, e, jnp.where(lane >= 120, w, 0.0))
        ref[4 * SPAN + 8 : 4 * SPAN + 8 + TR, :] = beside
        if n == 0:
            prep_ref[2 * DEV : 2 * DEV + TR, :] = beside
    note = 2 * DEV + TR
    prep_ref[note : note + 8, :] = west_ref[TR : TR + 8, :]
    prep_ref[note + 8 : note + 16, :] = east_ref[TR : TR + 8, :]
    wait(got[2:])
    stored = []
    for j in range(4):
        own = slice(j * SPAN + 8, j * SPAN + 8 + TR)
        s_ref[own, :] = s_ref[own, :] * wet_ref[:, 128 * j : 128 * j + 128].astype(F32)
    for n, ref in enumerate(targets):
        for j in range(PANELS):
            at = PANELS * n + j
            base = j * SPAN + 8
            near_ref[48 * at : 48 * at + 24, :] = ref[base : base + 24, :]
            near_ref[48 * at + 24 : 48 * at + 48, :] = ref[base + TR - 24 : base + TR, :]
            up, down = PREP + 8 * at, PREP + STRIP + 8 * at
            prep_ref[up : up + 8, :] = ref[base : base + 8, :]
            prep_ref[down : down + 8, :] = ref[base + TR - 8 : base + TR, :]

    def store(pairs):
        for src, dst in pairs:
            stored.append(pltpu.make_async_copy(src, dst, sem_out.at[len(stored)]))
            stored[-1].start()

    store(((prep_ref, prep_out.at[0:SHELF, :]), (near_ref, near_out)))
    set_up(BULK, state, consts, bed_x, man_x, row0, col0)
    store(zip(consts, (mbe_out, cre_out, mbs_out, crs_out)))
    run_steps(STEPS // 2, BULK, state, consts, east_x, row0, col0, add_bulk_edges(edge_ref))
    store(zip(state + (edge_ref,), (s_out, qe_out, qs_out, edge_out)))
    wait(stored)


def first_call(west, east, recv, pond, fields):
    ext = array(EXT, 128)
    buffer, message = pltpu.VMEM((EXT, 128), F32), pltpu.VMEM((TR + 8, 128), F32)
    extra = (2 * TR, SHELF, NEAR)
    return pl.pallas_call(
        first_kernel,
        out_shape=(ext,) * 7 + tuple(array(n, 128) for n in (2 * TR, ROOM, NEAR)),
        in_specs=[HBM] * 10,
        out_specs=(HBM,) * 10,
        scratch_shapes=[buffer] * 7
        + [pltpu.VMEM((n, 128), F32) for n in extra]
        + [buffer, buffer, pltpu.VMEM((TR, TC), jnp.int32), buffer, message, message]
        + [pltpu.SemaphoreType.DMA((25,)), pltpu.SemaphoreType.DMA((10,))],
        compiler_params=params(FULL),
        name="first_steps",
    )(west, east, recv, pond, *fields)


CHUNK = 16
CHUNKS = NB // CHUNK


def soil_rows(layer, block):
    return pl.ds((layer // 8) * (NB * 8) + block * 8 + layer % 8, 8, stride=8)


def columns_kernel(
    after_any, live_ref, soil_hbm, cond_hbm,
    base_hbm, top_hbm, low_hbm,
    soil_ref, cond_ref, cond_x, base_ref, top_ref, low_ref, sem, sem_out,
):
    pairs = []
    half = NB * 8
    for c in range(CHUNKS):
        cols = slice(c * CHUNK * 128, (c + 1) * CHUNK * 128)
        pairs.append((cond_hbm.at[:, cols], cond_ref.at[:, cols]))
        for h in range(2):
            rows = slice(h * half + c * CHUNK * 8, h * half + (c + 1) * CHUNK * 8)
            pairs.append((soil_hbm.at[rows, :], soil_ref.at[rows, :]))
    moved = copies(sem, pairs)
    live = live_ref[0]
    sub, lane = iota((8, 128), 0), iota((8, 128), 1)
    group = range(CHUNK // 8)
    for c in range(CHUNKS):
        wait(moved[3 * c : 3 * c + 3])
        for b in range(c * CHUNK, (c + 1) * CHUNK):
            cond_x[16 * b : 16 * b + 16, :] = cond_ref[:, 128 * b : 128 * b + 128].astype(F32)
        blocks = [c * CHUNK + 8 * g for g in group]
        kept = [(b + sub) * 128 + lane < live for b in blocks]
        mark = [k.astype(F32) for k in kept]

        def cond_at(g, layer):
            return cond_x[pl.ds(blocks[g] * 16 + layer, 8, stride=16), :]

        def out_at(g, layer):
            return slice(layer * NB + blocks[g], layer * NB + blocks[g] + 8)

        ratios = [[] for _ in group]
        above = [None for _ in group]
        base = [[] for _ in group]
        top = [[] for _ in group]
        low = [[] for _ in group]
        cond = [cond_at(g, 0) for g in group]
        for j in range(NL):
            for g in group:
                center = 1.0 if j < NL - 1 else 1.0 + drainage
                if j > 0:
                    center = center + (above[g] + above[g] * ratios[g][-1])
                if j < NL - 1:
                    below = cond_at(g, j + 1)
                    face = 0.5 * (cond[g] + below)
                    cond[g] = below
                    center = center + face
                r = pltpu.reciprocal(center, approx=True)
                value = soil_ref[soil_rows(j, blocks[g]), :] * r
                if j == 0:
                    top[g].append(mark[g] * r)
                else:
                    carry = above[g] * r
                    value = value + carry * base[g][-1]
                    top[g].append(carry * top[g][-1])
                base[g].append(value)
                if j == 8:
                    low[g].append(mark[g] * r)
                if j > 8:
                    low[g].append(mark[g] * r + carry * low[g][-1])
                if j < NL - 1:
                    ratios[g].append(-face * r)
                    above[g] = face
        x = [base[g][-1] for g in group]
        u = [top[g][-1] for g in group]
        v = [low[g][-1] for g in group]
        for j in range(NL - 1, -1, -1):
            for g in group:
                if j < NL - 1:
                    ratio = ratios[g][j]
                    x[g] = base[g][j] - ratio * x[g]
                    u[g] = top[g][j] - ratio * u[g]
                    v[g] = (low[g][j - 8] - ratio * v[g]) if j >= 8 else -ratio * v[g]
                base_ref[out_at(g, j), :] = jnp.where(kept[g], x[g], soil_ref[soil_rows(j, blocks[g]), :])
                top_ref[out_at(g, j), :] = u[g]
                low_ref[out_at(g, j), :] = v[g]
    wait(copies(sem_out, ((base_ref, base_hbm), (top_ref, top_hbm), (low_ref, low_hbm))))


def columns_call(after, live, soil, cond):
    layers = array(NB * NL, 128)
    buffer = pltpu.VMEM((NB * NL, 128), F32)
    return pl.pallas_call(
        columns_kernel,
        out_shape=(layers,) * 3,
        in_specs=[ANY, SMEM, HBM, HBM],
        out_specs=(HBM,) * 3,
        scratch_shapes=[buffer, pltpu.VMEM((NL, LAND), BF16), buffer, buffer, buffer, buffer]
        + [pltpu.SemaphoreType.DMA((3 * CHUNKS,)), pltpu.SemaphoreType.DMA((3,))],
        compiler_params=params(FULL),
        name="soil_columns",
    )(after, live, soil, cond)


PARTS = 4


def land_part(land_ref, slot_ref, rain_ref, cap_ref, base_ref, top_ref, low_ref, out_hbm, soil_ref, sem_out):
    slot = jnp.broadcast_to(slot_ref[...].astype(F32), (128, NB))
    slot = jnp.concatenate([slot, jnp.full((128, 256 - NB), -1.0, F32)], axis=1).T
    slot = twice(slot[0:NB])
    tile2 = iota((NB, DEV), 1).astype(F32) * 2.0
    pond = jnp.zeros((NB, 128), F32)
    for k in range(2):
        pond = pond + hot_dot(as_hot(slot == tile2 + float(k)), land_ref[DEV * k : DEV * k + DEV, :])
    rain = rain_ref[...]
    wetting = rain + jnp.maximum(pond, 0.0)
    rain_ref[...] = cap_ref[...] * wetting * pltpu.reciprocal(wetting + half_rate, approx=True)
    lat = land_ref[2 * DEV : 2 * DEV + 8, :]
    stored = []
    share = NB // PARTS
    for c in range(PARTS):
        for b in range(c * share, (c + 1) * share, 8):
            uptake = rain_ref[b : b + 8, :]
            for j in range(NL):
                rows = slice(j * NB + b, j * NB + b + 8)
                x = base_ref[rows, :] + (uptake * top_ref[rows, :] + lat * low_ref[rows, :])
                soil_ref[soil_rows(j, b), :] = x
        for h in range(2):
            rows = slice(h * NB * 8 + c * share * 8, h * NB * 8 + (c + 1) * share * 8)
            stored.append(pltpu.make_async_copy(soil_ref.at[rows, :], out_hbm.at[rows, :], sem_out.at[2 * c + h]))
            stored[-1].start()
    return stored


def middle_kernel(
    flow_hbm, s_in, qe_in, qs_in, mbe_in, cre_in, mbs_in, crs_in, edge_in, bed_hbm,
    slot_hbm, rain_hbm, cap_hbm, base_hbm, top_hbm, low_hbm,
    depth_hbm, qe_hbm, qs_hbm, edge_hbm, soil_out,
    in_ref, s_ref, qe_ref, qs_ref, mbe_ref, cre_ref, mbs_ref, crs_ref, edge_ref, bed_ref,
    land_ref, slot_ref, rain_ref, cap_ref, base_ref, top_ref, low_ref, soil_ref,
    east_ref, sem_state, sem_land, sem_tiles, sem_out,
):
    state, consts = (s_ref, qe_ref, qs_ref), (mbe_ref, cre_ref, mbs_ref, crs_ref)
    in_hbm, land_hbm = flow_hbm.at[0 : PANELS * TR, :], flow_hbm.at[PANELS * TR : FLOW, :]
    sources = (s_in, in_hbm, qe_in, qs_in, mbe_in, cre_in, mbs_in, crs_in, edge_in)
    loaded = copies(sem_state, list(zip(sources, (s_ref, in_ref, qe_ref, qs_ref) + consts + (edge_ref,))))
    row0, col0 = place()
    wait(loaded[:2])
    for j in range(PANELS):
        own = slice(j * SPAN + 8, j * SPAN + 8 + TR)
        s_ref[own, :] = s_ref[own, :] + in_ref[TR * j : TR * j + TR, :]
    wait(loaded[2:])
    sources = (bed_hbm, slot_hbm, rain_hbm, cap_hbm, land_hbm, base_hbm, top_hbm, low_hbm)
    targets = (bed_ref, slot_ref, rain_ref, cap_ref, land_ref, base_ref, top_ref, low_ref)
    land = copies(sem_land, list(zip(sources, targets)))
    run_steps(STEPS - STEPS // 2, BULK, state, consts, east_ref, row0, col0, add_bulk_edges(edge_ref))
    pairs = [(edge_ref, edge_hbm.at[0 : 2 * TR, :])]
    for src, dst in ((qe_ref, qe_hbm), (qs_ref, qs_hbm)):
        for j in range(4):
            pairs.append((src.at[j * SPAN + 8 : j * SPAN + 8 + TR, :], dst.at[:, 128 * j : 128 * j + 128]))
    wait(land)
    for j in range(4):
        cols = slice(128 * j, 128 * j + 128)
        bed_ref[:, cols] = s_ref[j * SPAN + 8 : j * SPAN + 8 + TR, :] - bed_ref[:, cols]
    pairs.append((bed_ref, depth_hbm))
    stored = copies(sem_tiles, pairs)
    stored += land_part(land_ref, slot_ref, rain_ref, cap_ref, base_ref, top_ref, low_ref, soil_out, soil_ref, sem_out)
    wait(stored)


def middle_call(flow, state, edge, bed, slot, rain, cap, soil):
    tile = array(TR, TC)
    buffer = pltpu.VMEM((EXT, 128), F32)
    blocks, layers = pltpu.VMEM((NB, 128), F32), pltpu.VMEM((NB * NL, 128), F32)
    counts = (9, 8, 10, 2 * PARTS)
    return pl.pallas_call(
        middle_kernel,
        out_shape=(tile,) * 3 + (array(ROOM, 128), array(NB * NL, 128)),
        in_specs=[HBM] * 16,
        out_specs=(HBM,) * 5,
        scratch_shapes=[pltpu.VMEM((PANELS * TR, 128), F32)]
        + [buffer] * 7
        + [pltpu.VMEM((2 * TR, 128), F32), pltpu.VMEM((TR, TC), F32), pltpu.VMEM((2 * DEV + 8, 128), F32)]
        + [pltpu.VMEM((1, NB), jnp.int32), blocks, blocks]
        + [layers] * 4
        + [buffer]
        + [pltpu.SemaphoreType.DMA((n,)) for n in counts],
        compiler_params=params(FULL),
        name="middle_steps",
    )(flow, *state, edge, bed, slot, rain, cap, *soil)


def last_kernel(
    depth_in, qe_in, qs_in, north_hbm, south_hbm, near_hbm, in_hbm, edge_hbm,
    depth_out, qe_out, qs_out, we_hbm, ns_hbm,
    we_ref, ns_ref, north_ref, south_ref, near_ref, in_ref, edge_ref,
    bs_ref, bqe_ref, bqs_ref, bmbe, bcre, bmbs, bcrs, bbed, bman, beast, sum_ref, tile_ref, sem_in, sem,
):
    pairs = [(near_hbm, near_ref), (north_hbm, north_ref), (south_hbm, south_ref)]
    pairs.append((edge_hbm.at[0 : 2 * TR, :], edge_ref))
    for j in range(PANELS):
        for g, start in ((0, 0), (1, TR - 24)):
            to = 24 * (2 * j + g)
            pairs.append((in_hbm.at[TR * j + start : TR * j + start + 24, :], in_ref.at[to : to + 24, :]))
    got = copies(sem_in, pairs)
    row0, col0 = place()
    band, consts = (bs_ref, bqe_ref, bqs_ref), (bmbe, bcre, bmbs, bcrs)
    targets = (bs_ref, bbed, bman, bqe_ref, bqs_ref)
    clear_guards(EDGES, targets + consts)
    sum_ref[...] = jnp.zeros((SUMS, 128), F32)
    wait(got)
    for n, out in enumerate(targets):
        for j in range(PANELS):
            at = PANELS * n + j
            strip = slice(8 * at, 8 * at + 8)
            out[EDGES.at(0, 0, j), :] = north_ref[strip, :]
            out[EDGES.at(1, 3, j), :] = south_ref[strip, :]
            for i in range(3):
                rows = 48 * at + 8 * i
                out[EDGES.at(0, i + 1, j), :] = near_ref[rows : rows + 8, :]
                out[EDGES.at(1, i, j), :] = near_ref[rows + 24 : rows + 32, :]
    set_up(EDGES, band, consts, bbed, bman, row0, col0)
    sums = add_band_edges(EDGES, sum_ref, bqs_ref)
    run_steps(STEPS // 2, EDGES, band, consts, beast, row0, col0, sums)
    for j in range(PANELS):
        strip = slice(STRIP + 8 * j, STRIP + 8 * j + 8)
        for p, flow in ((EDGES.at(0, 0, j), north_ref[strip, :]), (EDGES.at(1, 3, j), south_ref[strip, :])):
            bs_ref[p, :] = bs_ref[p, :] + flow
        for i in range(3):
            for g, p in ((0, EDGES.at(0, i + 1, j)), (1, EDGES.at(1, i, j))):
                rows = 24 * (2 * j + g) + 8 * i
                bs_ref[p, :] = bs_ref[p, :] + in_ref[rows : rows + 8, :]
    sums = add_band_edges(EDGES_LATE, sum_ref, bqs_ref)
    run_steps(STEPS - STEPS // 2, EDGES_LATE, band, consts, beast, row0, col0, sums)
    pairs = []
    for n, out in enumerate((depth_out, qe_out, qs_out)):
        for g, i in ((0, 1), (1, 2)):
            to = slice(16 * n + 8 * g, 16 * n + 8 * g + 8)
            for j in range(4):
                p = EDGES.at(g, i, j)
                tile_ref[to, 128 * j : 128 * j + 128] = bs_ref[p, :] - bbed[p, :] if n == 0 else band[n][p, :]
            rows = slice(0, 8) if g == 0 else slice(TR - 8, TR)
            pairs.append((tile_ref.at[to, :], out.at[rows, :]))
    stored = copies(sem, pairs)
    for n in range(2):
        edge_ref[TR * n : TR * n + 8, :] = sum_ref[8 * n : 8 * n + 8, :]
        edge_ref[TR * n + TR - 8 : TR * n + TR, :] = sum_ref[16 + 8 * n : 24 + 8 * n, :]
    we_ref[0:1, :] = edge_ref[TR : 2 * TR, :].T[127:128, :]
    we_ref[1:2, :] = edge_ref[0:TR, :].T[127:128, :]
    for j in range(4):
        for g in range(2):
            row = 32 + 8 * (4 * g + j) + 7
            ns_ref[g : g + 1, 128 * j : 128 * j + 128] = sum_ref[row : row + 1, :]
    for n, (src, dst) in enumerate(((we_ref, we_hbm), (ns_ref, ns_hbm))):
        stored.append(pltpu.make_async_copy(src, dst, sem.at[6 + n]))
        stored[-1].start()
    wait(stored)


def last_call(tiles, north, south, near, flow, edge):
    strip = pltpu.VMEM((STRIP + PANELS * 8, 128), F32)
    return pl.pallas_call(
        last_kernel,
        out_shape=(array(TR, TC), array(TR, TC), array(TR, TC), array(2, TR), array(2, TC)),
        in_specs=[HBM] * 8,
        out_specs=(HBM,) * 5,
        scratch_shapes=[pltpu.VMEM((2, TR), F32), pltpu.VMEM((2, TC), F32), strip, strip]
        + [pltpu.VMEM((n, 128), F32) for n in (NEAR, 2 * PANELS * 24, 2 * TR)]
        + [pltpu.VMEM((BANDS, 128), F32)] * 10
        + [pltpu.VMEM((SUMS, 128), F32), pltpu.VMEM((48, TC), F32)]
        + [pltpu.SemaphoreType.DMA((4 + 2 * PANELS,)), pltpu.SemaphoreType.DMA((8,))],
        input_output_aliases={0: 0, 1: 1, 2: 2},
        compiler_params=params(53),
        name="last_steps",
    )(*tiles, north, south, near, flow, edge)


def shift(first, second, axis):
    count = lax.axis_size(axis)
    ahead = [(i, i + 1) for i in range(count - 1)]
    back = [(j, i) for i, j in ahead]
    return lax.ppermute(first, axis, ahead), lax.ppermute(second, axis, back)


def local(
    soil_water, conduct, rainfall, infil_cap, live_counts, send_slot, recv_row,
    bed_height, manning, depth_in, east_in, south_in, wet_mask,
):
    rain = rainfall.reshape(NB, 128)
    cap = infil_cap.reshape(NB, 128)
    soil = soil_water.reshape(2, 8, NB, 128).transpose(0, 2, 1, 3).reshape(NB * NL, 128)
    fields = (depth_in, wet_mask, bed_height, manning, east_in, south_in)

    sent, pond, recv = send_call(live_counts, send_slot, recv_row, rain, cap, depth_in, wet_mask, soil)
    got = lax.all_to_all(sent.reshape(DEV, 1, K * 128), ALL, split_axis=0, concat_axis=0, tiled=True)
    got = got.reshape(DEV * K, 128)

    to_west, to_east = cols_call(recv, fields)
    west, east = shift(to_east, to_west, "gx")
    solved = columns_call(to_west, live_counts, soil, conduct)
    *state, edge, prep, near = first_call(west, east, recv, pond, fields)

    flow, up, down = inflow_call(solved[0], got, prep)
    north, south = shift(down, up, ROWS)
    *tiles, edge, soil_out = middle_call(
        flow, state, edge, bed_height, send_slot, rain, cap, solved
    )
    depth, east_q, south_q, edge_we, edge_ns = last_call(tiles, north, south, near, flow, edge)
    soil_out = soil_out.reshape(2, NB, 8, 128).transpose(0, 2, 1, 3).reshape(NL, LAND)
    return soil_out, depth, east_q, south_q, edge_we, edge_ns


def solution(mesh):
    placed = (
        P(None, ALL),
        P(None, ALL),
        P(ALL),
        P(ALL),
        P(ALL),
        P(ALL, None),
        P(ALL, None),
    ) + (P(ROWS, "gx"),) * 6
    return jax.shard_map(
        local,
        mesh=mesh,
        in_specs=placed,
        out_specs=(
            P(None, ALL),
            P(ROWS, "gx"),
            P(ROWS, "gx"),
            P(ROWS, "gx"),
            P("gx", ROWS),
            P(ROWS, "gx"),
        ),
        check_vma=False,
    )
```
